128 devices in a mesh: sec: 4 (over z), dev: 32 (over y, x, core).
Axes of the slice: x: 4, y: 4, z: 4, core: 2. Of those that a mesh axis runs over, the one named last changes fastest.
Arguments:
- fluid_distribution_functions: float32 [19, 512, 64, 128], P(None, 'sec', 'dev'), may hold values from 0 to 0.5, as said below
- voxel_phase_markers: int32 [512, 64, 128], P('sec', 'dev'), may hold values 0 or 1
- starting_thermal_profile: float32 [512, 64, 128], P(('sec', 'dev')), may hold values from -6 to 6
Outputs:
- populations_out: float32 [19, 512, 64, 128], P(None, 'sec', 'dev')
- temperature: float32 [512, 64, 128], P(('sec', 'dev'))
The draws below stay inside these ranges and needn't reach their ends.
Inputs may be any that keep to these rules, and one draw needn't show every extreme that they name: `fluid_distribution_functions`: each population lies near its weight times a density near one, positive.
All inputs are finite; a program needn't handle non-finite values. No bound on the sum of `voxel_phase_markers` on one device may be relied on, other than what follows from the above.
Results may differ from the reference program's by a relative error of at most 0.0001.
Values sent between devices are 32-bit elements; how exact they have to be, the bound alone decides.
A program may use at most 128 MiB of HBM per device.

```python
import jax
import jax.numpy as jnp
from jax import lax

GRID_WIDTH_EAST = 128
FSTEPS = 4
HSTEPS = 4
GRID_WIDTH_NORTH = 64
GRID_WIDTH_UPWARD = 512


lattice_dirs = [(0, 0, 0), (1, 0, 0), (-1, 0, 0), (0, 1, 0), (0, -1, 0), (0, 0, 1), (0, 0, -1), (1, 1, 0), (-1, -1, 0), (1, -1, 0), (-1, 1, 0), (1, 0, 1), (-1, 0, -1), (1, 0, -1), (-1, 0, 1), (0, 1, 1), (0, -1, -1), (0, 1, -1), (0, -1, 1)]


lattice_weights = [1.0 / 3.0] + [1.0 / 18.0] * 6 + [1.0 / 36.0] * 12


def draw_fluid_distribution_functions(key, part):
    key = jax.random.fold_in(key, 11)
    key_dens, key_vel, key_noise = jax.random.split(key, 3)
    dens = 1.0 + 0.1 * jax.random.uniform(key_dens, (GRID_WIDTH_UPWARD, GRID_WIDTH_NORTH, GRID_WIDTH_EAST), jnp.float32, -1.0, 1.0)
    fluid_speed_vectors = 0.05 * jax.random.uniform(key_vel, (3, GRID_WIDTH_UPWARD, GRID_WIDTH_NORTH, GRID_WIDTH_EAST), jnp.float32, -1.0, 1.0)
    noise = 1.0 + 0.1 * jax.random.uniform(key_noise, (19, GRID_WIDTH_UPWARD, GRID_WIDTH_NORTH, GRID_WIDTH_EAST), jnp.float32, -1.0, 1.0)
    dirs = jnp.array(lattice_dirs, jnp.float32)
    weights = jnp.array(lattice_weights, jnp.float32)
    along = dirs[:, 0, None, None, None] * fluid_speed_vectors[0] + dirs[:, 1, None, None, None] * fluid_speed_vectors[1] + dirs[:, 2, None, None, None] * fluid_speed_vectors[2]
    return (weights[:, None, None, None] * dens * (1.0 + 3.0 * along) * noise).astype(jnp.float32)


def place_ends(values, rng, least, high):
    dims = values.shape
    spot = [jax.random.randint(jax.random.fold_in(rng, axis), (), 0, dims[axis]) for axis in range(len(dims))]
    values = values.at[tuple(spot)].set(least)
    longest = dims.index(max(dims))
    spot[longest] = (spot[longest] + 1) % dims[longest]
    return values.at[tuple(spot)].set(high)


def shard_levels(own_key, dims, shards, low, high):
    factor_of = 1.0
    for dim, parts in shards:
        heights = jax.random.uniform(jax.random.fold_in(jax.random.fold_in(own_key, 6), dim), (parts,), jnp.float32, low / len(shards), high / len(shards))
        factor_of = factor_of * jnp.repeat(jnp.exp(heights), dims[dim] // parts).reshape((-1,) + (1,) * (len(dims) - 1 - dim))
    return factor_of


def scatter_about(stream_key, extent, deviation, bound, shards=(), held_as=jnp.bfloat16):
    entries = jax.random.normal(stream_key, extent, jnp.float32) * deviation
    if len(shards) > 0:
        entries = shard_levels(stream_key, extent, shards, -0.22, 0.18) * entries
    return jnp.clip(entries, min=-bound, max=bound).astype(held_as)


def setup_inputs(seed: int = 0) -> dict:
    keys = jax.random.split(jax.random.key(seed), 4)
    return {
        "fluid_distribution_functions": draw_fluid_distribution_functions(jax.random.fold_in(keys[3], 71), 0),
        "voxel_phase_markers": place_ends((jax.random.randint(keys[1], (GRID_WIDTH_UPWARD, GRID_WIDTH_NORTH, GRID_WIDTH_EAST), 0, 5) < 3).astype(jnp.int32), jax.random.fold_in(keys[1], 1), 0, 1),
        "starting_thermal_profile": scatter_about(keys[2], (GRID_WIDTH_UPWARD, GRID_WIDTH_NORTH, GRID_WIDTH_EAST), 1.0, 6.0, ((0, 128),), jnp.float32),
    }


lattice_dirs = [(0, 0, 0), (1, 0, 0), (-1, 0, 0), (0, 1, 0), (0, -1, 0), (0, 0, 1), (0, 0, -1),
                (1, 1, 0), (-1, -1, 0), (1, -1, 0), (-1, 1, 0), (1, 0, 1), (-1, 0, -1), (1, 0, -1), (-1, 0, 1),
                (0, 1, 1), (0, -1, -1), (0, 1, -1), (0, -1, 1)]
lattice_weights = [1.0 / 3.0] + [1.0 / 18.0] * 6 + [1.0 / 36.0] * 12
opposite_index = [0, 2, 1, 4, 3, 6, 5, 8, 7, 10, 9, 12, 11, 14, 13, 16, 15, 18, 17]
heat_dirs = [(0, 0, 0), (1, 0, 0), (-1, 0, 0), (0, 1, 0), (0, -1, 0), (0, 0, 1), (0, 0, -1)]
heat_weights = [0.25] + [0.125] * 6
omega = 0.8
rate_pore = 1.0 / 0.7
rate_grain = 1.0 / 1.4


def moments(pops):
    dirs = jnp.array(lattice_dirs, jnp.float32)
    dens = jnp.sum(pops, axis=0)
    mom = jnp.einsum("ia,izyx->azyx", dirs, pops, precision=lax.Precision.HIGHEST)
    return dens, mom / dens


def collide(pops):
    dirs = jnp.array(lattice_dirs, jnp.float32)
    weights = jnp.array(lattice_weights, jnp.float32)
    dens, fluid_speed_vectors = moments(pops)
    along = jnp.einsum("ia,azyx->izyx", dirs, fluid_speed_vectors, precision=lax.Precision.HIGHEST)
    usq = jnp.sum(fluid_speed_vectors * fluid_speed_vectors, axis=0)
    feq = weights[:, None, None, None] * dens * (1.0 + 3.0 * along + 4.5 * along * along - 1.5 * usq)
    return pops + omega * (feq - pops)


def thermal_balance_distribution(temp, fluid_speed_vectors):
    dirs = jnp.array(heat_dirs, jnp.float32)
    weights = jnp.array(heat_weights, jnp.float32)
    along = jnp.einsum("ia,azyx->izyx", dirs, fluid_speed_vectors, precision=lax.Precision.HIGHEST)
    return weights[:, None, None, None] * temp * (1.0 + 4.0 * along)


def heat_collide(thermal_scalar_grid, fluid_speed_vectors, rate):
    temp = jnp.sum(thermal_scalar_grid, axis=0)
    return thermal_scalar_grid + rate * (thermal_balance_distribution(temp, fluid_speed_vectors) - thermal_scalar_grid)


def reference(fluid_distribution_functions, voxel_phase_markers, starting_thermal_profile):
    pore = voxel_phase_markers.astype(jnp.float32)
    pops = fluid_distribution_functions
    for step in range(FSTEPS):
        post = collide(pops)
        moved = []
        for i, (cx, cy, cz) in enumerate(lattice_dirs):
            shifted = jnp.roll(post[i], (cz, cy, cx), axis=(0, 1, 2))
            source_pore = jnp.roll(pore, (cz, cy, cx), axis=(0, 1, 2))
            moved.append(jnp.where(source_pore > 0.5, shifted, post[opposite_index[i]]))
        pops = jnp.stack(moved)
    dens, fluid_speed_vectors = moments(pops)
    fluid_speed_vectors = fluid_speed_vectors * pore
    rate = pore * rate_pore + (1.0 - pore) * rate_grain
    thermal_scalar_grid = thermal_balance_distribution(starting_thermal_profile, fluid_speed_vectors)
    for step in range(HSTEPS):
        post = heat_collide(thermal_scalar_grid, fluid_speed_vectors, rate)
        thermal_scalar_grid = jnp.stack([jnp.roll(post[i], (cz, cy, cx), axis=(0, 1, 2)) for i, (cx, cy, cz) in enumerate(heat_dirs)])
    return pops, jnp.sum(thermal_scalar_grid, axis=0)
```

```python
import functools

import jax
import jax.numpy as jnp
from jax import lax
from jax.experimental import pallas as pl
from jax.experimental.pallas import tpu as pltpu
from jax.sharding import PartitionSpec as P

FSTEPS = 4
HSTEPS = 4

DIRS = [
    (0, 0, 0), (1, 0, 0), (-1, 0, 0), (0, 1, 0), (0, -1, 0), (0, 0, 1), (0, 0, -1),
    (1, 1, 0), (-1, -1, 0), (1, -1, 0), (-1, 1, 0), (1, 0, 1), (-1, 0, -1), (1, 0, -1), (-1, 0, 1),
    (0, 1, 1), (0, -1, -1), (0, 1, -1), (0, -1, 1),
]
OPP = [0, 2, 1, 4, 3, 6, 5, 8, 7, 10, 9, 12, 11, 14, 13, 16, 15, 18, 17]
OMEGA = 0.8
RATE_PORE = 1.0 / 0.7
RATE_GRAIN = 1.0 / 1.4

ORDER = [16, 4, 8, 9, 18, 5, 11, 14, 15, 3, 7, 10, 17, 6, 12, 13, 16, 0, 1, 2]
PLANE = {i: p for p, i in reversed(list(enumerate(ORDER)))}
CYM, CZP, CYP, CZM = (0, 5), (4, 9), (8, 13), (12, 17)
PLANES = len(ORDER)

MESH = pl.DeviceIdType.MESH
PAD = 8


def collide(f):
    rho = f[0]
    d = {}
    for i in range(1, 19, 2):
        rho = rho + (f[i] + f[i + 1])
        d[i] = f[i] - f[i + 1]
    mx = (d[1] + d[7]) + (d[9] + d[11]) + d[13]
    my = (d[3] + d[7]) + (d[15] - d[9]) + d[17]
    mz = (d[5] + d[11]) + (d[15] - d[13]) - d[17]
    inv = 1.0 / rho
    ux, uy, uz = mx * inv, my * inv, mz * inv
    even = rho - 1.5 * (mx * ux + my * uy + mz * uz)
    keep = 1.0 - OMEGA
    post = {0: keep * f[0] + (OMEGA / 3.0) * even}
    for i in range(1, 19, 2):
        w = OMEGA / (18.0 if i < 7 else 36.0)
        cx, cy, cz = DIRS[i]
        m = u = None
        for c, mm, uu in ((cx, mx, ux), (cy, my, uy), (cz, mz, uz)):
            if c == 0:
                continue
            if m is None:
                m, u = mm, uu
            elif c > 0:
                m, u = m + mm, u + uu
            else:
                m, u = m - mm, u - uu
        e = w * even + (4.5 * w) * (m * u)
        o = (3.0 * w) * m
        post[i] = keep * f[i] + (e + o)
        post[i + 1] = keep * f[i + 1] + (e - o)
    return post


def velocity(f):
    rho = f[0]
    d = {}
    for i in range(1, 19, 2):
        rho = rho + (f[i] + f[i + 1])
        d[i] = f[i] - f[i + 1]
    mx = (d[1] + d[7]) + (d[9] + d[11]) + d[13]
    my = (d[3] + d[7]) + (d[15] - d[9]) + d[17]
    mz = (d[5] + d[11]) + (d[15] - d[13]) - d[17]
    inv = 1.0 / rho
    return mx * inv, my * inv, mz * inv


def lane_shift(x, c):
    return pltpu.roll(x, c % x.shape[-1], 1) if c else x


def kernel(
    S, D, Z, ZC, X, ZH,
    f_hbm, lab_hbm, t0_ref, out_hbm, tout_ref,
    fbuf, lraw, obuf, post, hdn, hup, lab, hlab, mask, vel, heat, gdn, gup, stage, tin, tout, tback,
    lsem, fsem, osem, bsem, lrsem, y_send, z_send, y_recv, z_recv,
    a_send, a_recv, hy_send, hz_send, hy_recv, hz_recv,
):
    N = Z // ZC
    NH = Z // ZH
    R = 2
    TILE = (Z // D) * R
    me_s, me_d = lax.axis_index("sec"), lax.axis_index("dev")

    def at(ds, dd):
        return (lax.rem(me_s + ds + S, S), lax.rem(me_d + dd + D, D))

    def other(k):
        return (me_s, lax.rem(me_d + k, D))

    def chunk_of(j):
        half = j // 2
        return jnp.where(j % 2 == 0, half, N - 1 - half)

    lab_copy = pltpu.make_async_copy(lab_hbm, lraw, lsem)
    lab_copy.start()

    def f_copy(j):
        rows = pl.ds(pl.multiple_of(chunk_of(j) * (ZC * R), ZC * R), ZC * R)
        return pltpu.make_async_copy(f_hbm.at[:, rows, :], fbuf.at[:, rows, :], fsem.at[j])

    @pl.loop(0, N)
    def _(j):
        f_copy(j).start()

    barrier = pltpu.get_barrier_semaphore()

    @pl.loop(1, D)
    def _(k):
        pl.semaphore_signal(barrier, inc=1, device_id=other(k), device_id_type=MESH)

    for ds in (-1, 1):
        for dd in (-1, 0, 1):
            pl.semaphore_signal(barrier, inc=1, device_id=at(ds, dd), device_id_type=MESH)

    G = min(8, D)
    for z in range(Z // D):
        for y in range(R):
            for m in range(D // G):
                stage[pl.ds(TILE * G * m + R * z + y, G, stride=TILE), :] = t0_ref[
                    z, pl.ds(R * G * m + y, G, stride=R), :
                ]

    lab_copy.wait()
    for y in range(R):
        for b in range(Z // 8):
            lab[y, pl.ds(PAD + 8 * b, 8), :] = lraw[pl.ds(16 * b + y, 8, stride=R), :]

    pl.semaphore_wait(barrier, D - 1 + 6)

    def remote(src, dst, send, recv, to):
        return pltpu.make_async_remote_copy(
            src_ref=src, dst_ref=dst, send_sem=send, recv_sem=recv, device_id=to, device_id_type=MESH
        )

    low, high = pl.ds(PAD, 8), pl.ds(Z, 8)
    under, over = pl.ds(0, 8), pl.ds(PAD + Z, 8)
    inner = pl.ds(PAD, Z)
    lab_copies = [
        remote(lab.at[1, inner], hlab.at[0, inner], bsem.at[0], lrsem.at[0], at(0, 1)),
        remote(lab.at[0, inner], hlab.at[1, inner], bsem.at[1], lrsem.at[1], at(0, -1)),
        remote(lab.at[:, high], lab.at[:, under], bsem.at[2], lrsem.at[2], at(1, 0)),
        remote(lab.at[:, low], lab.at[:, over], bsem.at[3], lrsem.at[3], at(-1, 0)),
        remote(lab.at[1, high], hlab.at[0, under], bsem.at[4], lrsem.at[4], at(1, 1)),
        remote(lab.at[1, low], hlab.at[0, over], bsem.at[5], lrsem.at[5], at(-1, 1)),
        remote(lab.at[0, low], hlab.at[1, over], bsem.at[6], lrsem.at[6], at(-1, -1)),
        remote(lab.at[0, high], hlab.at[1, under], bsem.at[7], lrsem.at[7], at(1, -1)),
    ]
    for c in lab_copies:
        c.start()

    mine = pl.ds(pl.multiple_of(me_d * TILE, TILE), TILE)

    @pl.loop(1, D)
    def _(k):
        to = other(k)
        rows = pl.ds(pl.multiple_of(to[1] * TILE, TILE), TILE)
        remote(stage.at[rows], tin.at[mine], a_send.at[0], a_recv.at[0], to).start()

    tin[mine, :] = stage[mine, :]

    def y_copies(s, j):
        rows = pl.ds(pl.multiple_of(PAD + chunk_of(j) * ZC, 8), ZC)
        return (
            remote(post.at[s, 1, pl.ds(CYP[0], 5), rows], hdn.at[s, :, rows], y_send.at[s, 0, j], y_recv.at[s, 0, j], at(0, 1)),
            remote(post.at[s, 0, pl.ds(CYM[0], 5), rows], hup.at[s, :, rows], y_send.at[s, 1, j], y_recv.at[s, 1, j], at(0, -1)),
        )

    def z_copies(s):
        czp, czm = pl.ds(CZP[0], 5), pl.ds(CZM[0], 5)
        return (
            remote(post.at[s, :, czp, high], post.at[s, :, czp, under], z_send.at[s, 0], z_recv.at[s, 0], at(1, 0)),
            remote(post.at[s, :, czm, low], post.at[s, :, czm, over], z_send.at[s, 1], z_recv.at[s, 1], at(-1, 0)),
            remote(post.at[s, 1, PLANE[15], high], hdn.at[s, PLANE[15] - CYP[0], under], z_send.at[s, 2], z_recv.at[s, 2], at(1, 1)),
            remote(post.at[s, 1, PLANE[17], low], hdn.at[s, PLANE[17] - CYP[0], over], z_send.at[s, 3], z_recv.at[s, 3], at(-1, 1)),
            remote(post.at[s, 0, PLANE[16], low], hup.at[s, PLANE[16] - CYM[0], over], z_send.at[s, 4], z_recv.at[s, 4], at(-1, -1)),
            remote(post.at[s, 0, PLANE[18], high], hup.at[s, PLANE[18] - CYM[0], under], z_send.at[s, 5], z_recv.at[s, 5], at(1, -1)),
        )

    def store_post(s, y, rows, p):
        for plane, i in enumerate(ORDER):
            post[s, y, plane, rows, :] = p[i]

    def send_chunk(s, j):
        for c in y_copies(s, j):
            c.start()

        @pl.when(j == 1)
        def _():
            for c in z_copies(s):
                c.start()

    def source(s, y, i, z):
        cx, cy, cz = DIRS[i]
        rows = pl.ds(z - cz, 8)
        if y - cy < 0:
            v = hdn[s, PLANE[i] - CYP[0], rows, :]
        elif y - cy >= R:
            v = hup[s, PLANE[i] - CYM[0], rows, :]
        else:
            plane = 16 if i == 16 else PLANE[i]
            v = post[s, y - cy, plane, rows, :]
        return lane_shift(v, cx)

    def stream(s, y, z):
        here = pl.ds(z, 8)
        f = [post[s, y, PLANE[0], here, :]]
        for i in range(1, 19):
            open_ = mask[i - 1, y, pl.ds(z - PAD, 8), :] != 0
            f.append(jnp.where(open_, source(s, y, i, z), post[s, y, PLANE[OPP[i]], here, :]))
        return f

    def wait_sources(s, j):
        @pl.when(j == 0)
        def _():
            for q in (0, 1):
                for c in y_copies(s, q):
                    c.wait_recv()
            for c in z_copies(s):
                c.wait_recv()

        @pl.when(j + 2 < N)
        def _():
            for c in y_copies(s, j + 2):
                c.wait_recv()

    @pl.loop(0, N)
    def _(j):
        f_copy(j).wait()
        z0 = chunk_of(j) * ZC
        for y in range(R):
            @pl.loop(0, ZC // 8)
            def _(b):
                z = pl.multiple_of(z0 + 8 * b, 8)
                f = [fbuf[i, pl.ds(2 * z + y, 8, stride=R), :] for i in range(19)]
                store_post(0, y, pl.ds(pl.multiple_of(z + PAD, 8), 8), collide(f))
        send_chunk(0, j)

    for c in lab_copies:
        c.wait_recv()
    for y in range(R):
        @pl.loop(0, Z // 8)
        def _(b):
            z = pl.multiple_of(8 * b + PAD, 8)
            for cy in (-1, 0, 1):
                for cz in (-1, 0, 1):
                    use = [i for i in range(1, 19) if DIRS[i][1:] == (cy, cz)]
                    rows = pl.ds(z - cz, 8)
                    if y - cy < 0:
                        v = hlab[0, rows, :]
                    elif y - cy >= R:
                        v = hlab[1, rows, :]
                    else:
                        v = lab[y - cy, rows, :]
                    for i in use:
                        mask[i - 1, y, pl.ds(pl.multiple_of(8 * b, 8), 8), :] = lane_shift(v, DIRS[i][0])

    @pl.loop(1, FSTEPS)
    def _(s):
        @pl.loop(0, N)
        def _(j):
            wait_sources(s - 1, j)
            z0 = chunk_of(j) * ZC
            for y in range(R):
                @pl.loop(0, ZC // 8)
                def _(b):
                    z = pl.multiple_of(z0 + 8 * b + PAD, 8)
                    store_post(s, y, pl.ds(z, 8), collide(stream(s - 1, y, z)))
            send_chunk(s, j)

    def hy_copies(t, j):
        rows = pl.ds(pl.multiple_of(PAD + j * ZH, 8), ZH)
        return (
            remote(heat.at[t, 3, 1, rows], gdn.at[t, rows], hy_send.at[t, 0, j], hy_recv.at[t, 0, j], at(0, 1)),
            remote(heat.at[t, 4, 0, rows], gup.at[t, rows], hy_send.at[t, 1, j], hy_recv.at[t, 1, j], at(0, -1)),
        )

    def hz_copies(t):
        return (
            remote(heat.at[t, 5, :, high], heat.at[t, 5, :, under], hz_send.at[t, 0], hz_recv.at[t, 0], at(1, 0)),
            remote(heat.at[t, 6, :, low], heat.at[t, 6, :, over], hz_send.at[t, 1], hz_recv.at[t, 1], at(-1, 0)),
        )

    def balance(temp, ux, uy, uz):
        a, b = 0.25 * temp, 0.125 * temp
        h = 0.5 * temp
        hx, hy, hz = h * ux, h * uy, h * uz
        return [a, b + hx, b - hx, b + hy, b - hy, b + hz, b - hz]

    def gather(t, y, z):
        here = pl.ds(z, 8)
        g = [heat[t, 0, y, here, :]]
        g.append(lane_shift(heat[t, 1, y, here, :], 1))
        g.append(lane_shift(heat[t, 2, y, here, :], -1))
        g.append(gdn[t, here, :] if y == 0 else heat[t, 3, 0, here, :])
        g.append(gup[t, here, :] if y == 1 else heat[t, 4, 1, here, :])
        g.append(heat[t, 5, y, pl.ds(z - 1, 8), :])
        g.append(heat[t, 6, y, pl.ds(z + 1, 8), :])
        return g

    def total(g):
        return ((g[0] + g[1]) + (g[2] + g[3])) + ((g[4] + g[5]) + g[6])

    def out_copy(j):
        rows = pl.ds(pl.multiple_of(chunk_of(j) * (ZC * R), ZC * R), ZC * R)
        return pltpu.make_async_copy(obuf.at[:, rows, :], out_hbm.at[:, rows, :], osem.at[j])

    whole = pl.ds(0, Z * R - TILE)
    pltpu.make_async_copy(stage.at[whole], tin.at[whole], a_recv.at[0]).wait()

    @pl.loop(0, N)
    def _(j):
        wait_sources(FSTEPS - 1, j)
        z0 = chunk_of(j) * ZC
        for y in range(R):
            @pl.loop(0, ZC // 8)
            def _(b):
                zr = pl.multiple_of(z0 + 8 * b, 8)
                z = pl.multiple_of(zr + PAD, 8)
                f = stream(FSTEPS - 1, y, z)
                inter = pl.ds(2 * zr + y, 8, stride=R)
                for i in range(19):
                    obuf[i, inter, :] = f[i]
                pore = lab[y, pl.ds(z, 8), :].astype(jnp.float32)
                u = [pore * v for v in velocity(f)]
                flat = pl.ds(zr, 8)
                for k in range(3):
                    vel[k, y, flat, :] = u[k]
                vel[3, y, flat, :] = pore * RATE_PORE + (1.0 - pore) * RATE_GRAIN
                g = balance(tin[inter, :], *u)
                for k in range(7):
                    heat[0, k, y, pl.ds(z, 8), :] = g[k]
        out_copy(j).start()

    @pl.loop(0, NH)
    def _(j):
        for c in hy_copies(0, j):
            c.start()
    for c in hz_copies(0):
        c.start()

    def heat_wait(t, j):
        @pl.when(j == 0)
        def _():
            for c in hz_copies(t):
                c.wait_recv()
        for c in hy_copies(t, j):
            c.wait_recv()

    @pl.loop(1, HSTEPS)
    def _(t):
        @pl.loop(0, NH)
        def _(j):
            heat_wait(t - 1, j)
            for y in range(R):
                @pl.loop(0, ZH // 8)
                def _(b):
                    zr = pl.multiple_of(j * ZH + 8 * b, 8)
                    z = pl.multiple_of(zr + PAD, 8)
                    g = gather(t - 1, y, z)
                    flat = pl.ds(zr, 8)
                    u = [vel[k, y, flat, :] for k in range(3)]
                    rate = vel[3, y, flat, :]
                    q = balance(total(g), *u)
                    for k in range(7):
                        heat[t, k, y, pl.ds(z, 8), :] = g[k] + rate * (q[k] - g[k])
            for c in hy_copies(t, j):
                c.start()
        for c in hz_copies(t):
            c.start()

    @pl.loop(0, NH)
    def _(j):
        heat_wait(HSTEPS - 1, j)
        for y in range(R):
            @pl.loop(0, ZH // 8)
            def _(b):
                zr = pl.multiple_of(j * ZH + 8 * b, 8)
                z = pl.multiple_of(zr + PAD, 8)
                tout[pl.ds(2 * zr + y, 8, stride=R), :] = total(gather(HSTEPS - 1, y, z))

    @pl.loop(1, D)
    def _(k):
        to = other(k)
        rows = pl.ds(pl.multiple_of(to[1] * TILE, TILE), TILE)
        remote(tout.at[rows], tback.at[mine], a_send.at[1], a_recv.at[1], to).start()

    tback[mine, :] = tout[mine, :]

    for c in lab_copies:
        c.wait_send()

    @pl.loop(0, FSTEPS)
    def _(s):
        @pl.loop(0, N)
        def _(j):
            for c in y_copies(s, j):
                c.wait_send()
        for c in z_copies(s):
            c.wait_send()

    @pl.loop(0, HSTEPS)
    def _(t):
        @pl.loop(0, NH)
        def _(j):
            for c in hy_copies(t, j):
                c.wait_send()
        for c in hz_copies(t):
            c.wait_send()

    @pl.loop(0, N)
    def _(j):
        out_copy(j).wait()

    pltpu.make_async_copy(stage.at[whole], tin.at[whole], a_send.at[0]).wait()
    pltpu.make_async_copy(tout.at[whole], tback.at[whole], a_send.at[1]).wait()
    pltpu.make_async_copy(tout.at[whole], tback.at[whole], a_recv.at[1]).wait()
    for z in range(Z // D):
        for y in range(R):
            for m in range(D // G):
                tout_ref[z, pl.ds(R * G * m + y, G, stride=R), :] = tback[
                    pl.ds(TILE * G * m + R * z + y, G, stride=TILE), :
                ]


def local(S, D, f, labels, t0, zc=16, zh=32):
    _, Z, R, X = f.shape
    zc, zh = min(zc, Z), min(zh, Z)
    N, NH = Z // zc, Z // zh
    Zp = Z + 2 * PAD
    f32, i32 = jnp.float32, jnp.int32
    V, DMA = pltpu.VMEM, pltpu.SemaphoreType.DMA
    any_ = pl.BlockSpec(memory_space=pl.ANY)
    vmem = pl.BlockSpec(memory_space=pltpu.VMEM)
    pops, temp = pl.pallas_call(
        functools.partial(kernel, S, D, Z, zc, X, zh),
        out_shape=(
            jax.ShapeDtypeStruct((19, Z * R, X), f32),
            jax.ShapeDtypeStruct(t0.shape, f32),
        ),
        in_specs=[any_, any_, vmem],
        out_specs=(any_, vmem),
        scratch_shapes=[
            V((19, Z * R, X), f32),
            V((Z * R, X), i32),
            V((19, Z * R, X), f32),
            V((FSTEPS, R, PLANES, Zp, X), f32),
            V((FSTEPS, 5, Zp, X), f32),
            V((FSTEPS, 5, Zp, X), f32),
            V((R, Zp, X), i32),
            V((2, Zp, X), i32),
            V((18, R, Z, X), i32),
            V((4, R, Z, X), f32),
            V((HSTEPS, 7, R, Zp, X), f32),
            V((HSTEPS, Zp, X), f32),
            V((HSTEPS, Zp, X), f32),
            V((Z * R, X), f32),
            V((Z * R, X), f32),
            V((Z * R, X), f32),
            V((Z * R, X), f32),
            DMA(()),
            DMA((N,)),
            DMA((N,)),
            DMA((8,)),
            DMA((8,)),
            DMA((FSTEPS, 2, N)),
            DMA((FSTEPS, 6)),
            DMA((FSTEPS, 2, N)),
            DMA((FSTEPS, 6)),
            DMA((2,)),
            DMA((2,)),
            DMA((HSTEPS, 2, NH)),
            DMA((HSTEPS, 2)),
            DMA((HSTEPS, 2, NH)),
            DMA((HSTEPS, 2)),
        ],
        compiler_params=pltpu.CompilerParams(
            collective_id=0, has_side_effects=True, vmem_limit_bytes=56 * 1024 * 1024
        ),
    )(f.reshape(19, Z * R, X), labels.reshape(Z * R, X), t0)
    return pops.reshape(19, Z, R, X), temp


def solution(mesh):
    S, D = mesh.shape["sec"], mesh.shape["dev"]
    return jax.shard_map(
        functools.partial(local, S, D),
        mesh=mesh,
        in_specs=(
            P(None, "sec", "dev", None),
            P("sec", "dev", None),
            P(("sec", "dev"), None, None),
        ),
        out_specs=(P(None, "sec", "dev", None), P(("sec", "dev"), None, None)),
        check_vma=False,
    )
```

```python
import functools

import jax
import jax.numpy as jnp
from jax import lax
from jax.experimental import pallas as pl
from jax.experimental.pallas import tpu as pltpu
from jax.sharding import PartitionSpec as P

FSTEPS = 4
HSTEPS = 4

DIRS = [
    (0, 0, 0), (1, 0, 0), (-1, 0, 0), (0, 1, 0), (0, -1, 0), (0, 0, 1), (0, 0, -1),
    (1, 1, 0), (-1, -1, 0), (1, -1, 0), (-1, 1, 0), (1, 0, 1), (-1, 0, -1), (1, 0, -1), (-1, 0, 1),
    (0, 1, 1), (0, -1, -1), (0, 1, -1), (0, -1, 1),
]
OPP = [0, 2, 1, 4, 3, 6, 5, 8, 7, 10, 9, 12, 11, 14, 13, 16, 15, 18, 17]
OMEGA = 0.8
RATE_PORE = 1.0 / 0.7
RATE_GRAIN = 1.0 / 1.4

ORDER = [16, 4, 8, 9, 18, 5, 11, 14, 15, 3, 7, 10, 17, 6, 12, 13, 16, 0, 1, 2]
PLANE = {i: p for p, i in reversed(list(enumerate(ORDER)))}
CYM, CZP, CYP, CZM = (0, 5), (4, 9), (8, 13), (12, 17)
PLANES = len(ORDER)

MESH = pl.DeviceIdType.MESH
PAD = 8
BF = 16
BH = 32


def collide(f):
    rho = f[0]
    d = {}
    for i in range(1, 19, 2):
        rho = rho + (f[i] + f[i + 1])
        d[i] = f[i] - f[i + 1]
    mx = (d[1] + d[7]) + (d[9] + d[11]) + d[13]
    my = (d[3] + d[7]) + (d[15] - d[9]) + d[17]
    mz = (d[5] + d[11]) + (d[15] - d[13]) - d[17]
    inv = 1.0 / rho
    ux, uy, uz = mx * inv, my * inv, mz * inv
    even = rho - 1.5 * (mx * ux + my * uy + mz * uz)
    keep = 1.0 - OMEGA
    post = {0: keep * f[0] + (OMEGA / 3.0) * even}
    for i in range(1, 19, 2):
        w = OMEGA / (18.0 if i < 7 else 36.0)
        cx, cy, cz = DIRS[i]
        m = u = None
        for c, mm, uu in ((cx, mx, ux), (cy, my, uy), (cz, mz, uz)):
            if c == 0:
                continue
            if m is None:
                m, u = mm, uu
            elif c > 0:
                m, u = m + mm, u + uu
            else:
                m, u = m - mm, u - uu
        e = w * even + (4.5 * w) * (m * u)
        o = (3.0 * w) * m
        post[i] = keep * f[i] + (e + o)
        post[i + 1] = keep * f[i + 1] + (e - o)
    return post


def velocity(f):
    rho = f[0]
    d = {}
    for i in range(1, 19, 2):
        rho = rho + (f[i] + f[i + 1])
        d[i] = f[i] - f[i + 1]
    mx = (d[1] + d[7]) + (d[9] + d[11]) + d[13]
    my = (d[3] + d[7]) + (d[15] - d[9]) + d[17]
    mz = (d[5] + d[11]) + (d[15] - d[13]) - d[17]
    inv = 1.0 / rho
    return mx * inv, my * inv, mz * inv


def lane_shift(x, c):
    return pltpu.roll(x, c % x.shape[-1], 1) if c else x


def kernel(
    S, D, Z, ZC, X, ZH,
    f_hbm, lab_hbm, t0_ref, out_hbm, tout_ref,
    fbuf, lraw, obuf, post, hdn, hup, lab, hlab, mask, vel, heat, gdn, gup, stage, tin, tout, tback,
    lsem, fsem, osem, bsem, lrsem, y_send, z_send, y_recv, z_recv,
    a_send, a_recv, hy_send, hz_send, hy_recv, hz_recv,
):
    N = Z // ZC
    NH = Z // ZH
    R = 2
    TILE = (Z // D) * R
    me_s, me_d = lax.axis_index("sec"), lax.axis_index("dev")

    def at(ds, dd):
        return (lax.rem(me_s + ds + S, S), lax.rem(me_d + dd + D, D))

    def other(k):
        return (me_s, lax.rem(me_d + k, D))

    def chunk_of(j):
        half = j // 2
        return jnp.where(j % 2 == 0, half, N - 1 - half)

    lab_copy = pltpu.make_async_copy(lab_hbm, lraw, lsem)
    lab_copy.start()

    def f_copy(j):
        rows = pl.ds(pl.multiple_of(chunk_of(j) * (ZC * R), ZC * R), ZC * R)
        return pltpu.make_async_copy(f_hbm.at[:, rows, :], fbuf.at[:, rows, :], fsem.at[j])

    @pl.loop(0, N)
    def _(j):
        f_copy(j).start()

    barrier = pltpu.get_barrier_semaphore()

    @pl.loop(1, D)
    def _(k):
        pl.semaphore_signal(barrier, inc=1, device_id=other(k), device_id_type=MESH)

    for ds in (-1, 1):
        for dd in (-1, 0, 1):
            pl.semaphore_signal(barrier, inc=1, device_id=at(ds, dd), device_id_type=MESH)

    G = min(8, D)
    for z in range(Z // D):
        for y in range(R):
            for m in range(D // G):
                stage[pl.ds(TILE * G * m + R * z + y, G, stride=TILE), :] = t0_ref[
                    z, pl.ds(R * G * m + y, G, stride=R), :
                ]

    lab_copy.wait()
    for y in range(R):
        for b in range(Z // 8):
            lab[y, pl.ds(PAD + 8 * b, 8), :] = lraw[pl.ds(16 * b + y, 8, stride=R), :]

    pl.semaphore_wait(barrier, D - 1 + 6)

    def remote(src, dst, send, recv, to):
        return pltpu.make_async_remote_copy(
            src_ref=src, dst_ref=dst, send_sem=send, recv_sem=recv, device_id=to, device_id_type=MESH
        )

    low, high = pl.ds(PAD, 8), pl.ds(Z, 8)
    under, over = pl.ds(0, 8), pl.ds(PAD + Z, 8)
    inner = pl.ds(PAD, Z)
    lab_copies = [
        remote(lab.at[1, inner], hlab.at[0, inner], bsem.at[0], lrsem.at[0], at(0, 1)),
        remote(lab.at[0, inner], hlab.at[1, inner], bsem.at[1], lrsem.at[1], at(0, -1)),
        remote(lab.at[:, high], lab.at[:, under], bsem.at[2], lrsem.at[2], at(1, 0)),
        remote(lab.at[:, low], lab.at[:, over], bsem.at[3], lrsem.at[3], at(-1, 0)),
        remote(lab.at[1, high], hlab.at[0, under], bsem.at[4], lrsem.at[4], at(1, 1)),
        remote(lab.at[1, low], hlab.at[0, over], bsem.at[5], lrsem.at[5], at(-1, 1)),
        remote(lab.at[0, low], hlab.at[1, over], bsem.at[6], lrsem.at[6], at(-1, -1)),
        remote(lab.at[0, high], hlab.at[1, under], bsem.at[7], lrsem.at[7], at(1, -1)),
    ]
    for c in lab_copies:
        c.start()

    mine = pl.ds(pl.multiple_of(me_d * TILE, TILE), TILE)

    @pl.loop(1, D)
    def _(k):
        to = other(k)
        rows = pl.ds(pl.multiple_of(to[1] * TILE, TILE), TILE)
        remote(stage.at[rows], tin.at[mine], a_send.at[0], a_recv.at[0], to).start()

    tin[mine, :] = stage[mine, :]

    def y_copies(s, j):
        rows = pl.ds(pl.multiple_of(PAD + chunk_of(j) * ZC, 8), ZC)
        return (
            remote(post.at[s, 1, pl.ds(CYP[0], 5), rows], hdn.at[s, :, rows], y_send.at[s, 0, j], y_recv.at[s, 0, j], at(0, 1)),
            remote(post.at[s, 0, pl.ds(CYM[0], 5), rows], hup.at[s, :, rows], y_send.at[s, 1, j], y_recv.at[s, 1, j], at(0, -1)),
        )

    def z_copies(s):
        czp, czm = pl.ds(CZP[0], 5), pl.ds(CZM[0], 5)
        return (
            remote(post.at[s, :, czp, high], post.at[s, :, czp, under], z_send.at[s, 0], z_recv.at[s, 0], at(1, 0)),
            remote(post.at[s, :, czm, low], post.at[s, :, czm, over], z_send.at[s, 1], z_recv.at[s, 1], at(-1, 0)),
            remote(post.at[s, 1, PLANE[15], high], hdn.at[s, PLANE[15] - CYP[0], under], z_send.at[s, 2], z_recv.at[s, 2], at(1, 1)),
            remote(post.at[s, 1, PLANE[17], low], hdn.at[s, PLANE[17] - CYP[0], over], z_send.at[s, 3], z_recv.at[s, 3], at(-1, 1)),
            remote(post.at[s, 0, PLANE[16], low], hup.at[s, PLANE[16] - CYM[0], over], z_send.at[s, 4], z_recv.at[s, 4], at(-1, -1)),
            remote(post.at[s, 0, PLANE[18], high], hup.at[s, PLANE[18] - CYM[0], under], z_send.at[s, 5], z_recv.at[s, 5], at(1, -1)),
        )

    def store_post(s, y, rows, p):
        for plane, i in enumerate(ORDER):
            post[s, y, plane, rows, :] = p[i]

    def send_chunk(s, j):
        for c in y_copies(s, j):
            c.start()

        @pl.when(j == 1)
        def _():
            for c in z_copies(s):
                c.start()

    def source(s, y, i, z):
        cx, cy, cz = DIRS[i]
        rows = pl.ds(z - cz, BF)
        if y - cy < 0:
            v = hdn[s, PLANE[i] - CYP[0], rows, :]
        elif y - cy >= R:
            v = hup[s, PLANE[i] - CYM[0], rows, :]
        else:
            plane = 16 if i == 16 else PLANE[i]
            v = post[s, y - cy, plane, rows, :]
        return lane_shift(v, cx)

    def stream(s, y, z):
        here = pl.ds(z, BF)
        f = [post[s, y, PLANE[0], here, :]]
        for i in range(1, 19):
            open_ = mask[i - 1, y, pl.ds(z - PAD, BF), :] != 0
            f.append(jnp.where(open_, source(s, y, i, z), post[s, y, PLANE[OPP[i]], here, :]))
        return f

    def wait_sources(s, j):
        @pl.when(j == 0)
        def _():
            for q in (0, 1):
                for c in y_copies(s, q):
                    c.wait_recv()
            for c in z_copies(s):
                c.wait_recv()

        @pl.when(j + 2 < N)
        def _():
            for c in y_copies(s, j + 2):
                c.wait_recv()

    @pl.loop(0, N)
    def _(j):
        f_copy(j).wait()
        z0 = chunk_of(j) * ZC
        for y in range(R):
            @pl.loop(0, ZC // BF)
            def _(b):
                z = pl.multiple_of(z0 + BF * b, 8)
                f = [fbuf[i, pl.ds(2 * z + y, BF, stride=R), :] for i in range(19)]
                store_post(0, y, pl.ds(pl.multiple_of(z + PAD, 8), BF), collide(f))
        send_chunk(0, j)

    for c in lab_copies:
        c.wait_recv()
    for y in range(R):
        @pl.loop(0, Z // BH)
        def _(b):
            z = pl.multiple_of(BH * b + PAD, 8)
            for cy in (-1, 0, 1):
                for cz in (-1, 0, 1):
                    use = [i for i in range(1, 19) if DIRS[i][1:] == (cy, cz)]
                    rows = pl.ds(z - cz, BH)
                    if y - cy < 0:
                        v = hlab[0, rows, :]
                    elif y - cy >= R:
                        v = hlab[1, rows, :]
                    else:
                        v = lab[y - cy, rows, :]
                    for i in use:
                        mask[i - 1, y, pl.ds(pl.multiple_of(BH * b, 8), BH), :] = lane_shift(v, DIRS[i][0])

    @pl.loop(1, FSTEPS)
    def _(s):
        @pl.loop(0, N)
        def _(j):
            wait_sources(s - 1, j)
            z0 = chunk_of(j) * ZC
            for y in range(R):
                @pl.loop(0, ZC // BF)
                def _(b):
                    z = pl.multiple_of(z0 + BF * b + PAD, 8)
                    store_post(s, y, pl.ds(z, BF), collide(stream(s - 1, y, z)))
            send_chunk(s, j)

    def hy_copies(t, j):
        rows = pl.ds(pl.multiple_of(PAD + j * ZH, 8), ZH)
        return (
            remote(heat.at[t, 3, 1, rows], gdn.at[t, rows], hy_send.at[t, 0, j], hy_recv.at[t, 0, j], at(0, 1)),
            remote(heat.at[t, 4, 0, rows], gup.at[t, rows], hy_send.at[t, 1, j], hy_recv.at[t, 1, j], at(0, -1)),
        )

    def hz_copies(t):
        return (
            remote(heat.at[t, 5, :, high], heat.at[t, 5, :, under], hz_send.at[t, 0], hz_recv.at[t, 0], at(1, 0)),
            remote(heat.at[t, 6, :, low], heat.at[t, 6, :, over], hz_send.at[t, 1], hz_recv.at[t, 1], at(-1, 0)),
        )

    def balance(temp, ux, uy, uz):
        a, b = 0.25 * temp, 0.125 * temp
        h = 0.5 * temp
        hx, hy, hz = h * ux, h * uy, h * uz
        return [a, b + hx, b - hx, b + hy, b - hy, b + hz, b - hz]

    def gather(t, y, z):
        here = pl.ds(z, BH)
        g = [heat[t, 0, y, here, :]]
        g.append(lane_shift(heat[t, 1, y, here, :], 1))
        g.append(lane_shift(heat[t, 2, y, here, :], -1))
        g.append(gdn[t, here, :] if y == 0 else heat[t, 3, 0, here, :])
        g.append(gup[t, here, :] if y == 1 else heat[t, 4, 1, here, :])
        g.append(heat[t, 5, y, pl.ds(z - 1, BH), :])
        g.append(heat[t, 6, y, pl.ds(z + 1, BH), :])
        return g

    def total(g):
        return ((g[0] + g[1]) + (g[2] + g[3])) + ((g[4] + g[5]) + g[6])

    def out_copy(j):
        rows = pl.ds(pl.multiple_of(chunk_of(j) * (ZC * R), ZC * R), ZC * R)
        return pltpu.make_async_copy(obuf.at[:, rows, :], out_hbm.at[:, rows, :], osem.at[j])

    whole = pl.ds(0, Z * R - TILE)
    pltpu.make_async_copy(stage.at[whole], tin.at[whole], a_recv.at[0]).wait()

    @pl.loop(0, N)
    def _(j):
        wait_sources(FSTEPS - 1, j)
        z0 = chunk_of(j) * ZC
        for y in range(R):
            @pl.loop(0, ZC // BF)
            def _(b):
                zr = pl.multiple_of(z0 + BF * b, 8)
                z = pl.multiple_of(zr + PAD, 8)
                f = stream(FSTEPS - 1, y, z)
                inter = pl.ds(2 * zr + y, BF, stride=R)
                for i in range(19):
                    obuf[i, inter, :] = f[i]
                pore = lab[y, pl.ds(z, BF), :].astype(jnp.float32)
                u = [pore * v for v in velocity(f)]
                flat = pl.ds(zr, BF)
                for k in range(3):
                    vel[k, y, flat, :] = u[k]
                vel[3, y, flat, :] = pore * RATE_PORE + (1.0 - pore) * RATE_GRAIN
                g = balance(tin[inter, :], *u)
                for k in range(7):
                    heat[0, k, y, pl.ds(z, BF), :] = g[k]
        out_copy(j).start()

    @pl.loop(0, NH)
    def _(j):
        for c in hy_copies(0, j):
            c.start()
    for c in hz_copies(0):
        c.start()

    def heat_wait(t, j):
        @pl.when(j == 0)
        def _():
            for c in hz_copies(t):
                c.wait_recv()
        for c in hy_copies(t, j):
            c.wait_recv()

    @pl.loop(1, HSTEPS)
    def _(t):
        @pl.loop(0, NH)
        def _(j):
            heat_wait(t - 1, j)
            for y in range(R):
                @pl.loop(0, ZH // BH)
                def _(b):
                    zr = pl.multiple_of(j * ZH + BH * b, 8)
                    z = pl.multiple_of(zr + PAD, 8)
                    g = gather(t - 1, y, z)
                    flat = pl.ds(zr, BH)
                    u = [vel[k, y, flat, :] for k in range(3)]
                    rate = vel[3, y, flat, :]
                    q = balance(total(g), *u)
                    for k in range(7):
                        heat[t, k, y, pl.ds(z, BH), :] = g[k] + rate * (q[k] - g[k])
            for c in hy_copies(t, j):
                c.start()
        for c in hz_copies(t):
            c.start()

    @pl.loop(0, NH)
    def _(j):
        heat_wait(HSTEPS - 1, j)
        for y in range(R):
            @pl.loop(0, ZH // BH)
            def _(b):
                zr = pl.multiple_of(j * ZH + BH * b, 8)
                z = pl.multiple_of(zr + PAD, 8)
                tout[pl.ds(2 * zr + y, BH, stride=R), :] = total(gather(HSTEPS - 1, y, z))

    @pl.loop(1, D)
    def _(k):
        to = other(k)
        rows = pl.ds(pl.multiple_of(to[1] * TILE, TILE), TILE)
        remote(tout.at[rows], tback.at[mine], a_send.at[1], a_recv.at[1], to).start()

    tback[mine, :] = tout[mine, :]

    for c in lab_copies:
        c.wait_send()

    @pl.loop(0, FSTEPS)
    def _(s):
        @pl.loop(0, N)
        def _(j):
            for c in y_copies(s, j):
                c.wait_send()
        for c in z_copies(s):
            c.wait_send()

    @pl.loop(0, HSTEPS)
    def _(t):
        @pl.loop(0, NH)
        def _(j):
            for c in hy_copies(t, j):
                c.wait_send()
        for c in hz_copies(t):
            c.wait_send()

    @pl.loop(0, N)
    def _(j):
        out_copy(j).wait()

    pltpu.make_async_copy(stage.at[whole], tin.at[whole], a_send.at[0]).wait()
    pltpu.make_async_copy(tout.at[whole], tback.at[whole], a_send.at[1]).wait()
    pltpu.make_async_copy(tout.at[whole], tback.at[whole], a_recv.at[1]).wait()
    for z in range(Z // D):
        for y in range(R):
            for m in range(D // G):
                tout_ref[z, pl.ds(R * G * m + y, G, stride=R), :] = tback[
                    pl.ds(TILE * G * m + R * z + y, G, stride=TILE), :
                ]


def local(S, D, f, labels, t0, zc=16, zh=32):
    _, Z, R, X = f.shape
    zc, zh = min(zc, Z), min(zh, Z)
    N, NH = Z // zc, Z // zh
    Zp = Z + 2 * PAD
    f32, i32 = jnp.float32, jnp.int32
    V, DMA = pltpu.VMEM, pltpu.SemaphoreType.DMA
    any_ = pl.BlockSpec(memory_space=pl.ANY)
    vmem = pl.BlockSpec(memory_space=pltpu.VMEM)
    pops, temp = pl.pallas_call(
        functools.partial(kernel, S, D, Z, zc, X, zh),
        out_shape=(
            jax.ShapeDtypeStruct((19, Z * R, X), f32),
            jax.ShapeDtypeStruct(t0.shape, f32),
        ),
        in_specs=[any_, any_, vmem],
        out_specs=(any_, vmem),
        scratch_shapes=[
            V((19, Z * R, X), f32),
            V((Z * R, X), i32),
            V((19, Z * R, X), f32),
            V((FSTEPS, R, PLANES, Zp, X), f32),
            V((FSTEPS, 5, Zp, X), f32),
            V((FSTEPS, 5, Zp, X), f32),
            V((R, Zp, X), i32),
            V((2, Zp, X), i32),
            V((18, R, Z, X), i32),
            V((4, R, Z, X), f32),
            V((HSTEPS, 7, R, Zp, X), f32),
            V((HSTEPS, Zp, X), f32),
            V((HSTEPS, Zp, X), f32),
            V((Z * R, X), f32),
            V((Z * R, X), f32),
            V((Z * R, X), f32),
            V((Z * R, X), f32),
            DMA(()),
            DMA((N,)),
            DMA((N,)),
            DMA((8,)),
            DMA((8,)),
            DMA((FSTEPS, 2, N)),
            DMA((FSTEPS, 6)),
            DMA((FSTEPS, 2, N)),
            DMA((FSTEPS, 6)),
            DMA((2,)),
            DMA((2,)),
            DMA((HSTEPS, 2, NH)),
            DMA((HSTEPS, 2)),
            DMA((HSTEPS, 2, NH)),
            DMA((HSTEPS, 2)),
        ],
        compiler_params=pltpu.CompilerParams(
            collective_id=0, has_side_effects=True, vmem_limit_bytes=56 * 1024 * 1024
        ),
    )(f.reshape(19, Z * R, X), labels.reshape(Z * R, X), t0)
    return pops.reshape(19, Z, R, X), temp


def solution(mesh):
    S, D = mesh.shape["sec"], mesh.shape["dev"]
    return jax.shard_map(
        functools.partial(local, S, D),
        mesh=mesh,
        in_specs=(
            P(None, "sec", "dev", None),
            P("sec", "dev", None),
            P(("sec", "dev"), None, None),
        ),
        out_specs=(P(None, "sec", "dev", None), P(("sec", "dev"), None, None)),
        check_vma=False,
    )
```

```python
import functools

import jax
import jax.numpy as jnp
from jax import lax
from jax.experimental import pallas as pl
from jax.experimental.pallas import tpu as pltpu
from jax.sharding import PartitionSpec as P

FSTEPS = 4
HSTEPS = 4

DIRS = [
    (0, 0, 0), (1, 0, 0), (-1, 0, 0), (0, 1, 0), (0, -1, 0), (0, 0, 1), (0, 0, -1),
    (1, 1, 0), (-1, -1, 0), (1, -1, 0), (-1, 1, 0), (1, 0, 1), (-1, 0, -1), (1, 0, -1), (-1, 0, 1),
    (0, 1, 1), (0, -1, -1), (0, 1, -1), (0, -1, 1),
]
OPP = [0, 2, 1, 4, 3, 6, 5, 8, 7, 10, 9, 12, 11, 14, 13, 16, 15, 18, 17]
OMEGA = 0.8
RATE_PORE = 1.0 / 0.7
RATE_GRAIN = 1.0 / 1.4

ORDER = [16, 4, 8, 9, 18, 5, 11, 14, 15, 3, 7, 10, 17, 6, 12, 13, 16, 0, 1, 2]
PLANE = {i: p for p, i in reversed(list(enumerate(ORDER)))}
CYM, CZP, CYP, CZM = (0, 5), (4, 9), (8, 13), (12, 17)
PLANES = len(ORDER)

MESH = pl.DeviceIdType.MESH
PAD = 8
BF = 16
BH = 32


def blocks(n):
    def over(body):
        if n == 1:
            body(0)
        else:
            pl.loop(0, n)(body)

    return over


def collide(f):
    rho = f[0]
    d = {}
    for i in range(1, 19, 2):
        rho = rho + (f[i] + f[i + 1])
        d[i] = f[i] - f[i + 1]
    mx = (d[1] + d[7]) + (d[9] + d[11]) + d[13]
    my = (d[3] + d[7]) + (d[15] - d[9]) + d[17]
    mz = (d[5] + d[11]) + (d[15] - d[13]) - d[17]
    inv = 1.0 / rho
    ux, uy, uz = mx * inv, my * inv, mz * inv
    even = rho - 1.5 * (mx * ux + my * uy + mz * uz)
    keep = 1.0 - OMEGA
    post = {0: keep * f[0] + (OMEGA / 3.0) * even}
    for i in range(1, 19, 2):
        w = OMEGA / (18.0 if i < 7 else 36.0)
        cx, cy, cz = DIRS[i]
        m = u = None
        for c, mm, uu in ((cx, mx, ux), (cy, my, uy), (cz, mz, uz)):
            if c == 0:
                continue
            if m is None:
                m, u = mm, uu
            elif c > 0:
                m, u = m + mm, u + uu
            else:
                m, u = m - mm, u - uu
        e = w * even + (4.5 * w) * (m * u)
        o = (3.0 * w) * m
        post[i] = keep * f[i] + (e + o)
        post[i + 1] = keep * f[i + 1] + (e - o)
    return post


def velocity(f):
    rho = f[0]
    d = {}
    for i in range(1, 19, 2):
        rho = rho + (f[i] + f[i + 1])
        d[i] = f[i] - f[i + 1]
    mx = (d[1] + d[7]) + (d[9] + d[11]) + d[13]
    my = (d[3] + d[7]) + (d[15] - d[9]) + d[17]
    mz = (d[5] + d[11]) + (d[15] - d[13]) - d[17]
    inv = 1.0 / rho
    return mx * inv, my * inv, mz * inv


def lane_shift(x, c):
    return pltpu.roll(x, c % x.shape[-1], 1) if c else x


def kernel(
    S, D, Z, ZC, X, ZH,
    f_hbm, lab_hbm, t0_ref, obuf, tout_ref,
    fbuf, lraw, post, hdn, hup, lab, hlab, mask, vel, heat, gdn, gup, stage, tin, tout, tback,
    lsem, fsem, bsem, lrsem, y_send, z_send, y_recv, z_recv,
    a_send, a_recv, hy_send, hz_send, hy_recv, hz_recv,
):
    N = Z // ZC
    NH = Z // ZH
    R = 2
    TILE = (Z // D) * R
    me_s, me_d = lax.axis_index("sec"), lax.axis_index("dev")

    def at(ds, dd):
        return (lax.rem(me_s + ds + S, S), lax.rem(me_d + dd + D, D))

    def other(k):
        return (me_s, lax.rem(me_d + k, D))

    def chunk_of(j):
        half = j // 2
        return jnp.where(j % 2 == 0, half, N - 1 - half)

    lab_copy = pltpu.make_async_copy(lab_hbm, lraw, lsem)
    lab_copy.start()

    def f_copy(j):
        rows = pl.ds(pl.multiple_of(chunk_of(j) * (ZC * R), ZC * R), ZC * R)
        return pltpu.make_async_copy(f_hbm.at[:, rows, :], fbuf.at[:, rows, :], fsem.at[j])

    @pl.loop(0, N)
    def _(j):
        f_copy(j).start()

    barrier = pltpu.get_barrier_semaphore()

    @pl.loop(1, D)
    def _(k):
        pl.semaphore_signal(barrier, inc=1, device_id=other(k), device_id_type=MESH)

    for ds in (-1, 1):
        for dd in (-1, 0, 1):
            pl.semaphore_signal(barrier, inc=1, device_id=at(ds, dd), device_id_type=MESH)

    G = min(8, D)
    for z in range(Z // D):
        for y in range(R):
            for m in range(D // G):
                stage[pl.ds(TILE * G * m + R * z + y, G, stride=TILE), :] = t0_ref[
                    z, pl.ds(R * G * m + y, G, stride=R), :
                ]

    lab_copy.wait()
    for y in range(R):
        for b in range(Z // 8):
            lab[y, pl.ds(PAD + 8 * b, 8), :] = lraw[pl.ds(16 * b + y, 8, stride=R), :]

    def remote(src, dst, send, recv, to):
        return pltpu.make_async_remote_copy(
            src_ref=src, dst_ref=dst, send_sem=send, recv_sem=recv, device_id=to, device_id_type=MESH
        )

    low, high = pl.ds(PAD, 8), pl.ds(Z, 8)
    under, over = pl.ds(0, 8), pl.ds(PAD + Z, 8)
    inner = pl.ds(PAD, Z)
    lab_copies = [
        remote(lab.at[1, inner], hlab.at[0, inner], bsem.at[0], lrsem.at[0], at(0, 1)),
        remote(lab.at[0, inner], hlab.at[1, inner], bsem.at[1], lrsem.at[1], at(0, -1)),
        remote(lab.at[:, high], lab.at[:, under], bsem.at[2], lrsem.at[2], at(1, 0)),
        remote(lab.at[:, low], lab.at[:, over], bsem.at[3], lrsem.at[3], at(-1, 0)),
        remote(lab.at[1, high], hlab.at[0, under], bsem.at[4], lrsem.at[4], at(1, 1)),
        remote(lab.at[1, low], hlab.at[0, over], bsem.at[5], lrsem.at[5], at(-1, 1)),
        remote(lab.at[0, low], hlab.at[1, over], bsem.at[6], lrsem.at[6], at(-1, -1)),
        remote(lab.at[0, high], hlab.at[1, under], bsem.at[7], lrsem.at[7], at(1, -1)),
    ]
    def y_copies(s, j):
        rows = pl.ds(pl.multiple_of(PAD + chunk_of(j) * ZC, 8), ZC)
        return (
            remote(post.at[s, 1, pl.ds(CYP[0], 5), rows], hdn.at[s, :, rows], y_send.at[s, 0, j], y_recv.at[s, 0, j], at(0, 1)),
            remote(post.at[s, 0, pl.ds(CYM[0], 5), rows], hup.at[s, :, rows], y_send.at[s, 1, j], y_recv.at[s, 1, j], at(0, -1)),
        )

    def z_copies(s):
        czp, czm = pl.ds(CZP[0], 5), pl.ds(CZM[0], 5)
        return (
            remote(post.at[s, :, czp, high], post.at[s, :, czp, under], z_send.at[s, 0], z_recv.at[s, 0], at(1, 0)),
            remote(post.at[s, :, czm, low], post.at[s, :, czm, over], z_send.at[s, 1], z_recv.at[s, 1], at(-1, 0)),
            remote(post.at[s, 1, PLANE[15], high], hdn.at[s, PLANE[15] - CYP[0], under], z_send.at[s, 2], z_recv.at[s, 2], at(1, 1)),
            remote(post.at[s, 1, PLANE[17], low], hdn.at[s, PLANE[17] - CYP[0], over], z_send.at[s, 3], z_recv.at[s, 3], at(-1, 1)),
            remote(post.at[s, 0, PLANE[16], low], hup.at[s, PLANE[16] - CYM[0], over], z_send.at[s, 4], z_recv.at[s, 4], at(-1, -1)),
            remote(post.at[s, 0, PLANE[18], high], hup.at[s, PLANE[18] - CYM[0], under], z_send.at[s, 5], z_recv.at[s, 5], at(1, -1)),
        )

    def store_post(s, y, rows, p):
        for plane, i in enumerate(ORDER):
            post[s, y, plane, rows, :] = p[i]

    def send_chunk(s, j):
        for c in y_copies(s, j):
            c.start()

        @pl.when(j == 1)
        def _():
            for c in z_copies(s):
                c.start()

    def source(s, y, i, z):
        cx, cy, cz = DIRS[i]
        rows = pl.ds(z - cz, BF)
        if y - cy < 0:
            v = hdn[s, PLANE[i] - CYP[0], rows, :]
        elif y - cy >= R:
            v = hup[s, PLANE[i] - CYM[0], rows, :]
        else:
            plane = 16 if i == 16 else PLANE[i]
            v = post[s, y - cy, plane, rows, :]
        return lane_shift(v, cx)

    def stream(s, y, z):
        here = pl.ds(z, BF)
        f = [post[s, y, PLANE[0], here, :]]
        for i in range(1, 19):
            open_ = mask[i - 1, y, pl.ds(z - PAD, BF), :] != 0
            f.append(jnp.where(open_, source(s, y, i, z), post[s, y, PLANE[OPP[i]], here, :]))
        return f

    def wait_sources(s, j):
        @pl.when(j == 0)
        def _():
            for q in (0, 1):
                for c in y_copies(s, q):
                    c.wait_recv()
            for c in z_copies(s):
                c.wait_recv()

        @pl.when(j + 2 < N)
        def _():
            for c in y_copies(s, j + 2):
                c.wait_recv()

    @pl.loop(0, N)
    def _(j):
        f_copy(j).wait()
        z0 = chunk_of(j) * ZC
        for y in range(R):
            @blocks(ZC // BF)
            def _(b):
                z = pl.multiple_of(z0 + BF * b, 8)
                f = [fbuf[i, pl.ds(2 * z + y, BF, stride=R), :] for i in range(19)]
                store_post(0, y, pl.ds(pl.multiple_of(z + PAD, 8), BF), collide(f))

    pl.semaphore_wait(barrier, D - 1 + 6)

    for c in lab_copies:
        c.start()

    @pl.loop(0, N)
    def _(j):
        send_chunk(0, j)

    mine = pl.ds(pl.multiple_of(me_d * TILE, TILE), TILE)

    @pl.loop(1, D)
    def _(k):
        to = other(k)
        rows = pl.ds(pl.multiple_of(to[1] * TILE, TILE), TILE)
        remote(stage.at[rows], tin.at[mine], a_send.at[0], a_recv.at[0], to).start()

    tin[mine, :] = stage[mine, :]

    for c in lab_copies:
        c.wait_recv()
    for y in range(R):
        @pl.loop(0, Z // BH)
        def _(b):
            z = pl.multiple_of(BH * b + PAD, 8)
            for cy in (-1, 0, 1):
                for cz in (-1, 0, 1):
                    use = [i for i in range(1, 19) if DIRS[i][1:] == (cy, cz)]
                    rows = pl.ds(z - cz, BH)
                    if y - cy < 0:
                        v = hlab[0, rows, :]
                    elif y - cy >= R:
                        v = hlab[1, rows, :]
                    else:
                        v = lab[y - cy, rows, :]
                    for i in use:
                        mask[i - 1, y, pl.ds(pl.multiple_of(BH * b, 8), BH), :] = lane_shift(v, DIRS[i][0])

    @pl.loop(1, FSTEPS)
    def _(s):
        @pl.loop(0, N)
        def _(j):
            wait_sources(s - 1, j)
            z0 = chunk_of(j) * ZC
            for y in range(R):
                @blocks(ZC // BF)
                def _(b):
                    z = pl.multiple_of(z0 + BF * b + PAD, 8)
                    store_post(s, y, pl.ds(z, BF), collide(stream(s - 1, y, z)))
            send_chunk(s, j)

    def hy_copies(t, j):
        rows = pl.ds(pl.multiple_of(PAD + j * ZH, 8), ZH)
        return (
            remote(heat.at[t, 3, 1, rows], gdn.at[t, rows], hy_send.at[t, 0, j], hy_recv.at[t, 0, j], at(0, 1)),
            remote(heat.at[t, 4, 0, rows], gup.at[t, rows], hy_send.at[t, 1, j], hy_recv.at[t, 1, j], at(0, -1)),
        )

    def hz_copies(t):
        return (
            remote(heat.at[t, 5, :, high], heat.at[t, 5, :, under], hz_send.at[t, 0], hz_recv.at[t, 0], at(1, 0)),
            remote(heat.at[t, 6, :, low], heat.at[t, 6, :, over], hz_send.at[t, 1], hz_recv.at[t, 1], at(-1, 0)),
        )

    def balance(temp, ux, uy, uz):
        a, b = 0.25 * temp, 0.125 * temp
        h = 0.5 * temp
        hx, hy, hz = h * ux, h * uy, h * uz
        return [a, b + hx, b - hx, b + hy, b - hy, b + hz, b - hz]

    def gather(t, y, z):
        here = pl.ds(z, BH)
        g = [heat[t, 0, y, here, :]]
        g.append(lane_shift(heat[t, 1, y, here, :], 1))
        g.append(lane_shift(heat[t, 2, y, here, :], -1))
        g.append(gdn[t, here, :] if y == 0 else heat[t, 3, 0, here, :])
        g.append(gup[t, here, :] if y == 1 else heat[t, 4, 1, here, :])
        g.append(heat[t, 5, y, pl.ds(z - 1, BH), :])
        g.append(heat[t, 6, y, pl.ds(z + 1, BH), :])
        return g

    def total(g):
        return ((g[0] + g[1]) + (g[2] + g[3])) + ((g[4] + g[5]) + g[6])

    whole = pl.ds(0, Z * R - TILE)
    pltpu.make_async_copy(stage.at[whole], tin.at[whole], a_recv.at[0]).wait()

    @pl.loop(0, N)
    def _(j):
        wait_sources(FSTEPS - 1, j)
        z0 = chunk_of(j) * ZC
        for y in range(R):
            @blocks(ZC // BF)
            def _(b):
                zr = pl.multiple_of(z0 + BF * b, 8)
                z = pl.multiple_of(zr + PAD, 8)
                f = stream(FSTEPS - 1, y, z)
                inter = pl.ds(2 * zr + y, BF, stride=R)
                for i in range(19):
                    obuf[i, inter, :] = f[i]
                pore = lab[y, pl.ds(z, BF), :].astype(jnp.float32)
                u = [pore * v for v in velocity(f)]
                flat = pl.ds(zr, BF)
                for k in range(3):
                    vel[k, y, flat, :] = u[k]
                vel[3, y, flat, :] = pore * RATE_PORE + (1.0 - pore) * RATE_GRAIN
                g = balance(tin[inter, :], *u)
                for k in range(7):
                    heat[0, k, y, pl.ds(z, BF), :] = g[k]

    @pl.loop(0, NH)
    def _(j):
        for c in hy_copies(0, j):
            c.start()
    for c in hz_copies(0):
        c.start()

    def heat_wait(t, j):
        @pl.when(j == 0)
        def _():
            for c in hz_copies(t):
                c.wait_recv()
        for c in hy_copies(t, j):
            c.wait_recv()

    @pl.loop(1, HSTEPS)
    def _(t):
        @pl.loop(0, NH)
        def _(j):
            heat_wait(t - 1, j)
            for y in range(R):
                @blocks(ZH // BH)
                def _(b):
                    zr = pl.multiple_of(j * ZH + BH * b, 8)
                    z = pl.multiple_of(zr + PAD, 8)
                    g = gather(t - 1, y, z)
                    flat = pl.ds(zr, BH)
                    u = [vel[k, y, flat, :] for k in range(3)]
                    rate = vel[3, y, flat, :]
                    q = balance(total(g), *u)
                    for k in range(7):
                        heat[t, k, y, pl.ds(z, BH), :] = g[k] + rate * (q[k] - g[k])
            for c in hy_copies(t, j):
                c.start()
        for c in hz_copies(t):
            c.start()

    @pl.loop(0, NH)
    def _(j):
        heat_wait(HSTEPS - 1, j)
        for y in range(R):
            @blocks(ZH // BH)
            def _(b):
                zr = pl.multiple_of(j * ZH + BH * b, 8)
                z = pl.multiple_of(zr + PAD, 8)
                tout[pl.ds(2 * zr + y, BH, stride=R), :] = total(gather(HSTEPS - 1, y, z))

    @pl.loop(1, D)
    def _(k):
        to = other(k)
        rows = pl.ds(pl.multiple_of(to[1] * TILE, TILE), TILE)
        remote(tout.at[rows], tback.at[mine], a_send.at[1], a_recv.at[1], to).start()

    tback[mine, :] = tout[mine, :]

    for c in lab_copies:
        c.wait_send()

    @pl.loop(0, FSTEPS)
    def _(s):
        @pl.loop(0, N)
        def _(j):
            for c in y_copies(s, j):
                c.wait_send()
        for c in z_copies(s):
            c.wait_send()

    @pl.loop(0, HSTEPS)
    def _(t):
        @pl.loop(0, NH)
        def _(j):
            for c in hy_copies(t, j):
                c.wait_send()
        for c in hz_copies(t):
            c.wait_send()

    pltpu.make_async_copy(stage.at[whole], tin.at[whole], a_send.at[0]).wait()
    pltpu.make_async_copy(tout.at[whole], tback.at[whole], a_send.at[1]).wait()
    pltpu.make_async_copy(tout.at[whole], tback.at[whole], a_recv.at[1]).wait()
    for z in range(Z // D):
        for y in range(R):
            for m in range(D // G):
                tout_ref[z, pl.ds(R * G * m + y, G, stride=R), :] = tback[
                    pl.ds(TILE * G * m + R * z + y, G, stride=TILE), :
                ]


def write_out(pops, temp, pops_out, temp_out, sem):
    copies = [
        pltpu.make_async_copy(pops, pops_out, sem.at[0]),
        pltpu.make_async_copy(temp, temp_out, sem.at[1]),
    ]
    for c in copies:
        c.start()
    for c in copies:
        c.wait()


def local(S, D, f, labels, t0, zc=16, zh=32):
    _, Z, R, X = f.shape
    zc, zh = min(zc, Z), min(zh, Z)
    N, NH = Z // zc, Z // zh
    Zp = Z + 2 * PAD
    f32, i32 = jnp.float32, jnp.int32
    V, DMA = pltpu.VMEM, pltpu.SemaphoreType.DMA
    any_ = pl.BlockSpec(memory_space=pl.ANY)
    vmem = pl.BlockSpec(memory_space=pltpu.VMEM)
    pops, temp = pl.pallas_call(
        functools.partial(kernel, S, D, Z, zc, X, zh),
        out_shape=(
            pltpu.VMEM((19, Z * R, X), f32),
            pltpu.VMEM(t0.shape, f32),
        ),
        in_specs=[any_, any_, vmem],
        out_specs=(vmem, vmem),
        scratch_shapes=[
            V((19, Z * R, X), f32),
            V((Z * R, X), i32),
            V((FSTEPS, R, PLANES, Zp, X), f32),
            V((FSTEPS, 5, Zp, X), f32),
            V((FSTEPS, 5, Zp, X), f32),
            V((R, Zp, X), i32),
            V((2, Zp, X), i32),
            V((18, R, Z, X), i32),
            V((4, R, Z, X), f32),
            V((HSTEPS, 7, R, Zp, X), f32),
            V((HSTEPS, Zp, X), f32),
            V((HSTEPS, Zp, X), f32),
            V((Z * R, X), f32),
            V((Z * R, X), f32),
            V((Z * R, X), f32),
            V((Z * R, X), f32),
            DMA(()),
            DMA((N,)),
            DMA((8,)),
            DMA((8,)),
            DMA((FSTEPS, 2, N)),
            DMA((FSTEPS, 6)),
            DMA((FSTEPS, 2, N)),
            DMA((FSTEPS, 6)),
            DMA((2,)),
            DMA((2,)),
            DMA((HSTEPS, 2, NH)),
            DMA((HSTEPS, 2)),
            DMA((HSTEPS, 2, NH)),
            DMA((HSTEPS, 2)),
        ],
        compiler_params=pltpu.CompilerParams(
            collective_id=0, has_side_effects=True, vmem_limit_bytes=56 * 1024 * 1024
        ),
    )(f.reshape(19, Z * R, X), labels.reshape(Z * R, X), t0)
    return pops.reshape(19, Z, R, X), temp


def solution(mesh):
    S, D = mesh.shape["sec"], mesh.shape["dev"]
    return jax.shard_map(
        functools.partial(local, S, D),
        mesh=mesh,
        in_specs=(
            P(None, "sec", "dev", None),
            P("sec", "dev", None),
            P(("sec", "dev"), None, None),
        ),
        out_specs=(P(None, "sec", "dev", None), P(("sec", "dev"), None, None)),
        check_vma=False,
    )
```

```python
import functools

import jax
import jax.numpy as jnp
from jax import lax
from jax.experimental import pallas as pl
from jax.experimental.pallas import tpu as pltpu
from jax.sharding import PartitionSpec as P

FSTEPS = 4

DIRS = [
    (0, 0, 0), (1, 0, 0), (-1, 0, 0), (0, 1, 0), (0, -1, 0), (0, 0, 1), (0, 0, -1),
    (1, 1, 0), (-1, -1, 0), (1, -1, 0), (-1, 1, 0), (1, 0, 1), (-1, 0, -1), (1, 0, -1), (-1, 0, 1),
    (0, 1, 1), (0, -1, -1), (0, 1, -1), (0, -1, 1),
]
OPP = [0, 2, 1, 4, 3, 6, 5, 8, 7, 10, 9, 12, 11, 14, 13, 16, 15, 18, 17]
OMEGA = 0.8
RATE_PORE = 1.0 / 0.7
RATE_GRAIN = 1.0 / 1.4

ORDER = [16, 4, 8, 9, 18, 5, 11, 14, 15, 3, 7, 10, 17, 6, 12, 13, 16, 0, 1, 2]
PLANE = {i: p for p, i in reversed(list(enumerate(ORDER)))}
CYM, CZP, CYP, CZM = (0, 5), (4, 9), (8, 13), (12, 17)
PLANES = len(ORDER)

MESH = pl.DeviceIdType.MESH
PAD = 8
BF = 16
BH = 32
HP = 16
BE = 48


def blocks(n):
    def over(body):
        if n == 1:
            body(0)
        else:
            pl.loop(0, n)(body)

    return over


def collide(f):
    rho = f[0]
    d = {}
    for i in range(1, 19, 2):
        rho = rho + (f[i] + f[i + 1])
        d[i] = f[i] - f[i + 1]
    mx = (d[1] + d[7]) + (d[9] + d[11]) + d[13]
    my = (d[3] + d[7]) + (d[15] - d[9]) + d[17]
    mz = (d[5] + d[11]) + (d[15] - d[13]) - d[17]
    inv = 1.0 / rho
    ux, uy, uz = mx * inv, my * inv, mz * inv
    even = rho - 1.5 * (mx * ux + my * uy + mz * uz)
    keep = 1.0 - OMEGA
    post = {0: keep * f[0] + (OMEGA / 3.0) * even}
    for i in range(1, 19, 2):
        w = OMEGA / (18.0 if i < 7 else 36.0)
        cx, cy, cz = DIRS[i]
        m = u = None
        for c, mm, uu in ((cx, mx, ux), (cy, my, uy), (cz, mz, uz)):
            if c == 0:
                continue
            if m is None:
                m, u = mm, uu
            elif c > 0:
                m, u = m + mm, u + uu
            else:
                m, u = m - mm, u - uu
        e = w * even + (4.5 * w) * (m * u)
        o = (3.0 * w) * m
        post[i] = keep * f[i] + (e + o)
        post[i + 1] = keep * f[i + 1] + (e - o)
    return post


def velocity(f):
    rho = f[0]
    d = {}
    for i in range(1, 19, 2):
        rho = rho + (f[i] + f[i + 1])
        d[i] = f[i] - f[i + 1]
    mx = (d[1] + d[7]) + (d[9] + d[11]) + d[13]
    my = (d[3] + d[7]) + (d[15] - d[9]) + d[17]
    mz = (d[5] + d[11]) + (d[15] - d[13]) - d[17]
    inv = 1.0 / rho
    return mx * inv, my * inv, mz * inv


def lane_shift(x, c):
    return pltpu.roll(x, c % x.shape[-1], 1) if c else x


def kernel(
    S, D, Z, ZC, X,
    f_hbm, lab_hbm, t0_ref, obuf, tout_ref,
    fbuf, lraw, post, hdn, hup, lab, hlab, mask, rate, vel, t0x, ga, gin, gb, xs, xr, stage, tin, tout, tback,
    lsem, fsem, bsem, lrsem, y_send, z_send, y_recv, z_recv,
    a_send, a_recv, t_send, t_recv, v_send, v_recv, w_send, w_recv, x_send, x_recv,
):
    N = Z // ZC
    NG, GZ = N // 2, 2 * ZC
    NX = (Z + 16) // BE
    R = 2
    TILE = (Z // D) * R
    me_s, me_d = lax.axis_index("sec"), lax.axis_index("dev")

    def at(ds, dd):
        return (lax.rem(me_s + ds + S, S), lax.rem(me_d + dd + D, D))

    def other(k):
        return (me_s, lax.rem(me_d + k, D))

    def chunk_of(j):
        half = j // 2
        return jnp.where(j % 2 == 0, half, N - 1 - half)

    lab_copy = pltpu.make_async_copy(lab_hbm, lraw, lsem)
    lab_copy.start()

    def f_copy(j):
        rows = pl.ds(pl.multiple_of(chunk_of(j) * (ZC * R), ZC * R), ZC * R)
        return pltpu.make_async_copy(f_hbm.at[:, rows, :], fbuf.at[:, rows, :], fsem.at[j])

    @pl.loop(0, N)
    def _(j):
        f_copy(j).start()

    barrier = pltpu.get_barrier_semaphore()

    @pl.loop(1, D)
    def _(k):
        pl.semaphore_signal(barrier, inc=1, device_id=other(k), device_id_type=MESH)

    for ds in (-1, 1):
        for dd in (-1, 0, 1):
            pl.semaphore_signal(barrier, inc=1, device_id=at(ds, dd), device_id_type=MESH)

    G = min(8, D)
    for z in range(Z // D):
        for y in range(R):
            for m in range(D // G):
                stage[pl.ds(TILE * G * m + R * z + y, G, stride=TILE), :] = t0_ref[
                    z, pl.ds(R * G * m + y, G, stride=R), :
                ]

    lab_copy.wait()
    for y in range(R):
        for b in range(Z // 8):
            lab[y, pl.ds(PAD + 8 * b, 8), :] = lraw[pl.ds(16 * b + y, 8, stride=R), :]

    def remote(src, dst, send, recv, to):
        return pltpu.make_async_remote_copy(
            src_ref=src, dst_ref=dst, send_sem=send, recv_sem=recv, device_id=to, device_id_type=MESH
        )

    low, high = pl.ds(PAD, 8), pl.ds(Z, 8)
    under, over = pl.ds(0, 8), pl.ds(PAD + Z, 8)
    inner = pl.ds(PAD, Z)
    lab_copies = [
        remote(lab.at[1, inner], hlab.at[0, inner], bsem.at[0], lrsem.at[0], at(0, 1)),
        remote(lab.at[0, inner], hlab.at[1, inner], bsem.at[1], lrsem.at[1], at(0, -1)),
        remote(lab.at[:, high], lab.at[:, under], bsem.at[2], lrsem.at[2], at(1, 0)),
        remote(lab.at[:, low], lab.at[:, over], bsem.at[3], lrsem.at[3], at(-1, 0)),
        remote(lab.at[1, high], hlab.at[0, under], bsem.at[4], lrsem.at[4], at(1, 1)),
        remote(lab.at[1, low], hlab.at[0, over], bsem.at[5], lrsem.at[5], at(-1, 1)),
        remote(lab.at[0, low], hlab.at[1, over], bsem.at[6], lrsem.at[6], at(-1, -1)),
        remote(lab.at[0, high], hlab.at[1, under], bsem.at[7], lrsem.at[7], at(1, -1)),
    ]
    def y_copies(s, j):
        rows = pl.ds(pl.multiple_of(PAD + chunk_of(j) * ZC, 8), ZC)
        return (
            remote(post.at[s, 1, pl.ds(CYP[0], 5), rows], hdn.at[s, :, rows], y_send.at[s, 0, j], y_recv.at[s, 0, j], at(0, 1)),
            remote(post.at[s, 0, pl.ds(CYM[0], 5), rows], hup.at[s, :, rows], y_send.at[s, 1, j], y_recv.at[s, 1, j], at(0, -1)),
        )

    def z_copies(s):
        czp, czm = pl.ds(CZP[0], 5), pl.ds(CZM[0], 5)
        return (
            remote(post.at[s, :, czp, high], post.at[s, :, czp, under], z_send.at[s, 0], z_recv.at[s, 0], at(1, 0)),
            remote(post.at[s, :, czm, low], post.at[s, :, czm, over], z_send.at[s, 1], z_recv.at[s, 1], at(-1, 0)),
            remote(post.at[s, 1, PLANE[15], high], hdn.at[s, PLANE[15] - CYP[0], under], z_send.at[s, 2], z_recv.at[s, 2], at(1, 1)),
            remote(post.at[s, 1, PLANE[17], low], hdn.at[s, PLANE[17] - CYP[0], over], z_send.at[s, 3], z_recv.at[s, 3], at(-1, 1)),
            remote(post.at[s, 0, PLANE[16], low], hup.at[s, PLANE[16] - CYM[0], over], z_send.at[s, 4], z_recv.at[s, 4], at(-1, -1)),
            remote(post.at[s, 0, PLANE[18], high], hup.at[s, PLANE[18] - CYM[0], under], z_send.at[s, 5], z_recv.at[s, 5], at(1, -1)),
        )

    def store_post(s, y, rows, p):
        for plane, i in enumerate(ORDER):
            post[s, y, plane, rows, :] = p[i]

    def send_chunk(s, j):
        for c in y_copies(s, j):
            c.start()

        @pl.when(j == 1)
        def _():
            for c in z_copies(s):
                c.start()

    def source(s, y, i, z):
        cx, cy, cz = DIRS[i]
        rows = pl.ds(z - cz, BF)
        if y - cy < 0:
            v = hdn[s, PLANE[i] - CYP[0], rows, :]
        elif y - cy >= R:
            v = hup[s, PLANE[i] - CYM[0], rows, :]
        else:
            plane = 16 if i == 16 else PLANE[i]
            v = post[s, y - cy, plane, rows, :]
        return lane_shift(v, cx)

    def stream(s, y, z):
        here = pl.ds(z, BF)
        f = [post[s, y, PLANE[0], here, :]]
        for i in range(1, 19):
            open_ = mask[i - 1, y, pl.ds(z - PAD, BF), :] != 0
            f.append(jnp.where(open_, source(s, y, i, z), post[s, y, PLANE[OPP[i]], here, :]))
        return f

    def wait_sources(s, j):
        @pl.when(j == 0)
        def _():
            for q in (0, 1):
                for c in y_copies(s, q):
                    c.wait_recv()
            for c in z_copies(s):
                c.wait_recv()

        @pl.when(j + 2 < N)
        def _():
            for c in y_copies(s, j + 2):
                c.wait_recv()

    @pl.loop(0, N)
    def _(j):
        f_copy(j).wait()
        z0 = chunk_of(j) * ZC
        for y in range(R):
            @blocks(ZC // BF)
            def _(b):
                z = pl.multiple_of(z0 + BF * b, 8)
                f = [fbuf[i, pl.ds(2 * z + y, BF, stride=R), :] for i in range(19)]
                store_post(0, y, pl.ds(pl.multiple_of(z + PAD, 8), BF), collide(f))

    pl.semaphore_wait(barrier, D - 1 + 6)

    for c in lab_copies:
        c.start()

    @pl.loop(0, N)
    def _(j):
        send_chunk(0, j)

    mine = pl.ds(pl.multiple_of(me_d * TILE, TILE), TILE)

    @pl.loop(1, D)
    def _(k):
        to = other(k)
        rows = pl.ds(pl.multiple_of(to[1] * TILE, TILE), TILE)
        remote(stage.at[rows], tin.at[mine], a_send.at[0], a_recv.at[0], to).start()

    tin[mine, :] = stage[mine, :]

    for c in lab_copies:
        c.wait_recv()
    for y in range(R):
        @pl.loop(0, Z // BH)
        def _(b):
            z = pl.multiple_of(BH * b + PAD, 8)
            for cy in (-1, 0, 1):
                for cz in (-1, 0, 1):
                    use = [i for i in range(1, 19) if DIRS[i][1:] == (cy, cz)]
                    rows = pl.ds(z - cz, BH)
                    if y - cy < 0:
                        v = hlab[0, rows, :]
                    elif y - cy >= R:
                        v = hlab[1, rows, :]
                    else:
                        v = lab[y - cy, rows, :]
                    for i in use:
                        mask[i - 1, y, pl.ds(pl.multiple_of(BH * b, 8), BH), :] = lane_shift(v, DIRS[i][0])

    for e, labels in enumerate((hlab.at[0], lab.at[0], lab.at[1], hlab.at[1])):
        @pl.loop(0, NX)
        def _(b):
            pore = labels[pl.ds(pl.multiple_of(BE * b, 8), BE), :].astype(jnp.float32)
            rate[e, pl.ds(pl.multiple_of(BE * b + 8, 8), BE), :] = pore * RATE_PORE + (1.0 - pore) * RATE_GRAIN

    hin, hlow, hhigh = pl.ds(HP, Z), pl.ds(HP, 8), pl.ds(HP + Z - 8, 8)
    hunder, hover = pl.ds(HP - 8, 8), pl.ds(HP + Z, 8)
    own, before, after = pl.ds(2, 2), pl.ds(0, 2), pl.ds(4, 2)
    t_copies = [
        remote(t0x.at[own, src], t0x.at[to, dst], t_send.at[q], t_recv.at[q], at(ds, dd))
        for q, (src, to, dst, ds, dd) in enumerate(
            (
                (hin, before, hin, 0, 1),
                (hin, after, hin, 0, -1),
                (hhigh, own, hunder, 1, 0),
                (hlow, own, hover, -1, 0),
                (hhigh, before, hunder, 1, 1),
                (hlow, before, hover, -1, 1),
                (hhigh, after, hunder, 1, -1),
                (hlow, after, hover, -1, -1),
            )
        )
    ]
    whole = pl.ds(0, Z * R - TILE)

    def spread_temperature():
        pltpu.make_async_copy(stage.at[whole], tin.at[whole], a_recv.at[0]).wait()
        for y in range(R):
            @pl.loop(0, Z // BH)
            def _(b):
                t0x[2 + y, pl.ds(pl.multiple_of(HP + BH * b, 8), BH), :] = tin[pl.ds(2 * BH * b + y, BH, stride=R), :]
        for c in t_copies:
            c.start()

    @pl.loop(1, FSTEPS)
    def _(s):
        @pl.loop(0, N)
        def _(j):
            wait_sources(s - 1, j)
            z0 = chunk_of(j) * ZC
            for y in range(R):
                @blocks(ZC // BF)
                def _(b):
                    z = pl.multiple_of(z0 + BF * b + PAD, 8)
                    store_post(s, y, pl.ds(z, BF), collide(stream(s - 1, y, z)))
            send_chunk(s, j)

        @pl.when(s == 1)
        def _():
            spread_temperature()

    def v_copies(g):
        rows = pl.ds(pl.multiple_of(HP + g * GZ, 8), GZ)
        return (
            remote(vel.at[3, :, rows], vel.at[1, :, rows], v_send.at[g, 0], v_recv.at[g, 0], at(0, 1)),
            remote(vel.at[2, 2, rows], vel.at[0, 2, rows], v_send.at[g, 1], v_recv.at[g, 1], at(0, 1)),
            remote(vel.at[2, :, rows], vel.at[4, :, rows], v_send.at[g, 2], v_recv.at[g, 2], at(0, -1)),
            remote(vel.at[3, 2, rows], vel.at[5, 2, rows], v_send.at[g, 3], v_recv.at[g, 3], at(0, -1)),
        )

    w_copies = []
    for ds, src, dst in ((1, hhigh, hunder), (-1, hlow, hover)):
        for dd, fro, to in (
            (0, vel.at[own, :, src], vel.at[own, :, dst]),
            (1, vel.at[3, :, src], vel.at[1, :, dst]),
            (1, vel.at[2, 2, src], vel.at[0, 2, dst]),
            (-1, vel.at[2, :, src], vel.at[4, :, dst]),
            (-1, vel.at[3, 2, src], vel.at[5, 2, dst]),
        ):
            q = len(w_copies)
            w_copies.append(remote(fro, to, w_send.at[q], w_recv.at[q], at(ds, dd)))

    def x_copies(b):
        rows = pl.ds(pl.multiple_of(8 + BE * b, 8), BE)
        return (
            remote(xs.at[0, :, rows], xr.at[0, :, rows], x_send.at[0, b], x_recv.at[0, b], at(0, 1)),
            remote(xs.at[1, :, rows], xr.at[1, :, rows], x_send.at[1, b], x_recv.at[1, b], at(0, -1)),
        )

    def balance(temp, ux, uy, uz):
        a, b = 0.25 * temp, 0.125 * temp
        h = 0.5 * temp
        hx, hy, hz = h * ux, h * uy, h * uz
        return [a, b + hx, b - hx, b + hy, b - hy, b + hz, b - hz]

    def total(g):
        return ((g[0] + g[1]) + (g[2] + g[3])) + ((g[4] + g[5]) + g[6])

    def relax(g, q, r):
        return g + r * (q - g)

    def speed(e, here):
        return vel[e, 0, here, :], vel[e, 2, here, :], vel[e, 1, here, :]

    def gather(y, z, n):
        here = pl.ds(z, n)
        return [
            ga[0, y, here, :],
            lane_shift(ga[1, y, here, :], 1),
            lane_shift(ga[2, y, here, :], -1),
            gin[0, here, :] if y == 0 else ga[3, 0, here, :],
            gin[1, here, :] if y == 1 else ga[4, 1, here, :],
            ga[5, y, pl.ds(z - 1, n), :],
            ga[6, y, pl.ds(z + 1, n), :],
        ]

    def block_rows(b):
        return pl.multiple_of(8 + BE * b, 8)

    @pl.loop(0, N)
    def _(j):
        wait_sources(FSTEPS - 1, j)
        z0 = chunk_of(j) * ZC
        for y in range(R):
            @blocks(ZC // BF)
            def _(b):
                zr = pl.multiple_of(z0 + BF * b, 8)
                z = pl.multiple_of(zr + PAD, 8)
                f = stream(FSTEPS - 1, y, z)
                inter = pl.ds(2 * zr + y, BF, stride=R)
                for i in range(19):
                    obuf[i, inter, :] = f[i]
                pore = lab[y, pl.ds(z, BF), :].astype(jnp.float32)
                ux, uy, uz = velocity(f)
                there = pl.ds(pl.multiple_of(zr + HP, 8), BF)
                vel[2 + y, 0, there, :] = pore * ux
                vel[2 + y, 1, there, :] = pore * uz
                vel[2 + y, 2, there, :] = pore * uy

        @pl.when(j == 1)
        def _():
            for c in w_copies:
                c.start()

        @pl.when((j // 2) % 2 == 1)
        def _():
            for c in v_copies(chunk_of(j) // 2):
                c.start()

    for c in t_copies:
        c.wait_recv()
    for c in w_copies:
        c.wait_recv()

    @pl.loop(0, NG)
    def _(g):
        for c in v_copies(g):
            c.wait_recv()

    @pl.loop(0, NX)
    def _(b):
        z = block_rows(b)
        here, dn, up = pl.ds(z, BE), pl.ds(z - 1, BE), pl.ds(z + 1, BE)
        for e in (1, 2, 3, 4):
            t = t0x[e, here, :]
            q = balance(t, *speed(e, here))
            prev, nxt = t0x[e - 1, here, :], t0x[e + 1, here, :]
            tdn, tup = t0x[e, dn, :], t0x[e, up, :]
            g = [
                q[0],
                lane_shift(q[1], 1),
                lane_shift(q[2], -1),
                0.125 * prev + 0.5 * prev * vel[e - 1, 2, here, :],
                0.125 * nxt - 0.5 * nxt * vel[e + 1, 2, here, :],
                0.125 * tdn + 0.5 * tdn * vel[e, 1, dn, :],
                0.125 * tup - 0.5 * tup * vel[e, 1, up, :],
            ]
            q = balance(total(g), *speed(e, here))
            r = rate[e - 1, here, :]
            if e == 1:
                gin[0, here, :] = relax(g[3], q[3], r)
            elif e == 4:
                gin[1, here, :] = relax(g[4], q[4], r)
            else:
                for k in range(7):
                    ga[k, e - 2, here, :] = relax(g[k], q[k], r)

    @pl.loop(0, NX)
    def _(b):
        z = block_rows(b)
        here = pl.ds(z, BE)
        for y in range(R):
            g = gather(y, z, BE)
            q = balance(total(g), *speed(2 + y, here))
            r = rate[1 + y, here, :]
            p = [relax(g[k], q[k], r) for k in range(7)]
            for n, k in enumerate((0, 1, 2, 5, 6)):
                gb[n, y, here, :] = p[k]
            xs[0, y, here, :] = p[3]
            xs[1, 1 - y, here, :] = p[4]

    def others(y, z):
        here = pl.ds(z, BE)
        return [
            gb[0, y, here, :],
            lane_shift(gb[1, y, here, :], 1),
            lane_shift(gb[2, y, here, :], -1),
            gb[3, y, pl.ds(z - 1, BE), :],
            gb[4, y, pl.ds(z + 1, BE), :],
        ]

    @pl.loop(0, NX)
    def _(b):
        z = block_rows(b)
        for y in range(R):
            a = others(y, z)
            xs[1 - y, 2, pl.ds(z, BE), :] = (a[0] + (a[1] + a[2])) + (a[3] + a[4])
        for c in x_copies(b):
            c.start()

    @pl.loop(0, NX)
    def _(b):
        z = block_rows(b)
        here = pl.ds(z, BE)
        for c in x_copies(b):
            c.wait_recv()
        for y in range(R):
            a = others(y, z)
            yp = xr[0, 1, here, :] if y == 0 else xs[0, 0, here, :]
            ym = xr[1, 1, here, :] if y == 1 else xs[1, 0, here, :]
            g = a[:3] + [yp, ym] + a[3:]
            q = balance(total(g), *speed(2 + y, here))
            r = rate[1 + y, here, :]
            for k in range(7):
                ga[k, y, here, :] = relax(g[k], q[k], r)
        for side, e, sign in ((0, 1, 0.5), (1, 4, -0.5)):
            g = xr[side, 0, here, :]
            t = (xr[side, 2, here, :] + g) + xs[1 - side, 1, here, :]
            q = 0.125 * t + sign * t * vel[e, 2, here, :]
            gin[side, here, :] = relax(g, q, rate[e - 1, here, :])

    for y in range(R):
        @pl.loop(0, Z // BH)
        def _(b):
            zr = pl.multiple_of(BH * b, 8)
            tout[pl.ds(2 * zr + y, BH, stride=R), :] = total(gather(y, pl.multiple_of(zr + HP, 8), BH))

    @pl.loop(1, D)
    def _(k):
        to = other(k)
        rows = pl.ds(pl.multiple_of(to[1] * TILE, TILE), TILE)
        remote(tout.at[rows], tback.at[mine], a_send.at[1], a_recv.at[1], to).start()

    tback[mine, :] = tout[mine, :]

    for c in lab_copies:
        c.wait_send()

    @pl.loop(0, FSTEPS)
    def _(s):
        @pl.loop(0, N)
        def _(j):
            for c in y_copies(s, j):
                c.wait_send()
        for c in z_copies(s):
            c.wait_send()

    for c in t_copies + w_copies:
        c.wait_send()

    @pl.loop(0, NG)
    def _(g):
        for c in v_copies(g):
            c.wait_send()

    @pl.loop(0, NX)
    def _(b):
        for c in x_copies(b):
            c.wait_send()

    pltpu.make_async_copy(stage.at[whole], tin.at[whole], a_send.at[0]).wait()
    pltpu.make_async_copy(tout.at[whole], tback.at[whole], a_send.at[1]).wait()
    pltpu.make_async_copy(tout.at[whole], tback.at[whole], a_recv.at[1]).wait()
    for z in range(Z // D):
        for y in range(R):
            for m in range(D // G):
                tout_ref[z, pl.ds(R * G * m + y, G, stride=R), :] = tback[
                    pl.ds(TILE * G * m + R * z + y, G, stride=TILE), :
                ]


def write_out(pops, temp, pops_out, temp_out, sem):
    copies = [
        pltpu.make_async_copy(pops, pops_out, sem.at[0]),
        pltpu.make_async_copy(temp, temp_out, sem.at[1]),
    ]
    for c in copies:
        c.start()
    for c in copies:
        c.wait()


def local(S, D, f, labels, t0, zc=16):
    _, Z, R, X = f.shape
    N = Z // zc
    Zp, Zh = Z + 2 * PAD, Z + 2 * HP
    NG, NX = N // 2, (Z + 16) // BE
    f32, i32 = jnp.float32, jnp.int32
    V, DMA = pltpu.VMEM, pltpu.SemaphoreType.DMA
    any_ = pl.BlockSpec(memory_space=pl.ANY)
    vmem = pl.BlockSpec(memory_space=pltpu.VMEM)
    pops, temp = pl.pallas_call(
        functools.partial(kernel, S, D, Z, zc, X),
        out_shape=(
            pltpu.VMEM((19, Z * R, X), f32),
            pltpu.VMEM(t0.shape, f32),
        ),
        in_specs=[any_, any_, vmem],
        out_specs=(vmem, vmem),
        scratch_shapes=[
            V((19, Z * R, X), f32),
            V((Z * R, X), i32),
            V((FSTEPS, R, PLANES, Zp, X), f32),
            V((FSTEPS, 5, Zp, X), f32),
            V((FSTEPS, 5, Zp, X), f32),
            V((R, Zp, X), i32),
            V((2, Zp, X), i32),
            V((18, R, Z, X), i32),
            V((4, Zh, X), f32),
            V((6, 3, Zh, X), f32),
            V((6, Zh, X), f32),
            V((7, R, Zh, X), f32),
            V((2, Zh, X), f32),
            V((5, R, Zh, X), f32),
            V((2, 3, Zh, X), f32),
            V((2, 3, Zh, X), f32),
            V((Z * R, X), f32),
            V((Z * R, X), f32),
            V((Z * R, X), f32),
            V((Z * R, X), f32),
            DMA(()),
            DMA((N,)),
            DMA((8,)),
            DMA((8,)),
            DMA((FSTEPS, 2, N)),
            DMA((FSTEPS, 6)),
            DMA((FSTEPS, 2, N)),
            DMA((FSTEPS, 6)),
            DMA((2,)),
            DMA((2,)),
            DMA((8,)),
            DMA((8,)),
            DMA((NG, 4)),
            DMA((NG, 4)),
            DMA((10,)),
            DMA((10,)),
            DMA((2, NX)),
            DMA((2, NX)),
        ],
        compiler_params=pltpu.CompilerParams(
            collective_id=0, has_side_effects=True, vmem_limit_bytes=56 * 1024 * 1024
        ),
    )(f.reshape(19, Z * R, X), labels.reshape(Z * R, X), t0)
    return pops.reshape(19, Z, R, X), temp


def solution(mesh):
    S, D = mesh.shape["sec"], mesh.shape["dev"]
    return jax.shard_map(
        functools.partial(local, S, D),
        mesh=mesh,
        in_specs=(
            P(None, "sec", "dev", None),
            P("sec", "dev", None),
            P(("sec", "dev"), None, None),
        ),
        out_specs=(P(None, "sec", "dev", None), P(("sec", "dev"), None, None)),
        check_vma=False,
    )
```

```python
import functools

import jax
import jax.numpy as jnp
from jax import lax
from jax.experimental import pallas as pl
from jax.experimental.pallas import tpu as pltpu
from jax.sharding import PartitionSpec as P

FSTEPS = 4

DIRS = [
    (0, 0, 0), (1, 0, 0), (-1, 0, 0), (0, 1, 0), (0, -1, 0), (0, 0, 1), (0, 0, -1),
    (1, 1, 0), (-1, -1, 0), (1, -1, 0), (-1, 1, 0), (1, 0, 1), (-1, 0, -1), (1, 0, -1), (-1, 0, 1),
    (0, 1, 1), (0, -1, -1), (0, 1, -1), (0, -1, 1),
]
OPP = [0, 2, 1, 4, 3, 6, 5, 8, 7, 10, 9, 12, 11, 14, 13, 16, 15, 18, 17]
OMEGA = 0.8
RATE_PORE = 1.0 / 0.7
RATE_GRAIN = 1.0 / 1.4

ORDER = [16, 4, 8, 9, 18, 5, 11, 14, 15, 3, 7, 10, 17, 6, 12, 13, 16, 0, 1, 2]
PLANE = {i: p for p, i in reversed(list(enumerate(ORDER)))}
CYM, CZP, CYP, CZM = (0, 5), (4, 9), (8, 13), (12, 17)
PLANES = len(ORDER)

MESH = pl.DeviceIdType.MESH
PAD = 8
BF = 16
BH = 32
HP = 16
BE = 72


def plane_of(e, part):
    return 3 * e + ("xzy" if e % 2 == 0 else "yxz").index(part)


def blocks(n):
    def over(body):
        if n == 1:
            body(0)
        else:
            pl.loop(0, n)(body)

    return over


def collide(f):
    rho = f[0]
    d = {}
    for i in range(1, 19, 2):
        rho = rho + (f[i] + f[i + 1])
        d[i] = f[i] - f[i + 1]
    mx = (d[1] + d[7]) + (d[9] + d[11]) + d[13]
    my = (d[3] + d[7]) + (d[15] - d[9]) + d[17]
    mz = (d[5] + d[11]) + (d[15] - d[13]) - d[17]
    inv = 1.0 / rho
    ux, uy, uz = mx * inv, my * inv, mz * inv
    even = rho - 1.5 * (mx * ux + my * uy + mz * uz)
    keep = 1.0 - OMEGA
    post = {0: keep * f[0] + (OMEGA / 3.0) * even}
    for i in range(1, 19, 2):
        w = OMEGA / (18.0 if i < 7 else 36.0)
        cx, cy, cz = DIRS[i]
        m = u = None
        for c, mm, uu in ((cx, mx, ux), (cy, my, uy), (cz, mz, uz)):
            if c == 0:
                continue
            if m is None:
                m, u = mm, uu
            elif c > 0:
                m, u = m + mm, u + uu
            else:
                m, u = m - mm, u - uu
        e = w * even + (4.5 * w) * (m * u)
        o = (3.0 * w) * m
        post[i] = keep * f[i] + (e + o)
        post[i + 1] = keep * f[i + 1] + (e - o)
    return post


def velocity(f):
    rho = f[0]
    d = {}
    for i in range(1, 19, 2):
        rho = rho + (f[i] + f[i + 1])
        d[i] = f[i] - f[i + 1]
    mx = (d[1] + d[7]) + (d[9] + d[11]) + d[13]
    my = (d[3] + d[7]) + (d[15] - d[9]) + d[17]
    mz = (d[5] + d[11]) + (d[15] - d[13]) - d[17]
    inv = 1.0 / rho
    return mx * inv, my * inv, mz * inv


def lane_shift(x, c):
    return pltpu.roll(x, c % x.shape[-1], 1) if c else x


def kernel(
    S, D, Z, ZC, X,
    f_hbm, lab_hbm, t0_ref, obuf, tout_ref,
    fbuf, lraw, post, hdn, hup, lab, near, hlab, mask, rate, vel, t0x, ga, gin, gb, xs, xr, stage, tin, tout, tback,
    lsem, fsem, bsem, lrsem, y_send, z_send, y_recv, z_recv,
    a_send, a_recv, t_send, t_recv, v_send, v_recv, w_send, w_recv, x_send, x_recv,
):
    N = Z // ZC
    NX = (Z + 16) // BE
    R = 2
    TILE = (Z // D) * R
    me_s, me_d = lax.axis_index("sec"), lax.axis_index("dev")

    def at(ds, dd):
        return (lax.rem(me_s + ds + S, S), lax.rem(me_d + dd + D, D))

    def other(k):
        return (me_s, lax.rem(me_d + k, D))

    def chunk_of(j):
        half = j // 2
        return jnp.where(j % 2 == 0, half, N - 1 - half)

    lab_copy = pltpu.make_async_copy(lab_hbm, lraw, lsem)
    lab_copy.start()

    def f_copy(j):
        rows = pl.ds(pl.multiple_of(chunk_of(j) * (ZC * R), ZC * R), ZC * R)
        return pltpu.make_async_copy(f_hbm.at[:, rows, :], fbuf.at[:, rows, :], fsem.at[j])

    @pl.loop(0, N)
    def _(j):
        f_copy(j).start()

    barrier = pltpu.get_barrier_semaphore()

    @pl.loop(1, D)
    def _(k):
        pl.semaphore_signal(barrier, inc=1, device_id=other(k), device_id_type=MESH)

    for ds in (-1, 1):
        for dd in (-1, 0, 1):
            pl.semaphore_signal(barrier, inc=1, device_id=at(ds, dd), device_id_type=MESH)

    G = min(8, D)
    for z in range(Z // D):
        for y in range(R):
            for m in range(D // G):
                stage[pl.ds(TILE * G * m + R * z + y, G, stride=TILE), :] = t0_ref[
                    z, pl.ds(R * G * m + y, G, stride=R), :
                ]

    lab_copy.wait()
    for y in range(R):
        for b in range(Z // 8):
            lab[y, pl.ds(PAD + 8 * b, 8), :] = lraw[pl.ds(16 * b + y, 8, stride=R), :]
            near[y, pl.ds(PAD + 8 * b, 8), :] = lraw[pl.ds(16 * b + y, 8, stride=R), :]

    def remote(src, dst, send, recv, to):
        return pltpu.make_async_remote_copy(
            src_ref=src, dst_ref=dst, send_sem=send, recv_sem=recv, device_id=to, device_id_type=MESH
        )

    low, high = pl.ds(PAD, 8), pl.ds(Z, 8)
    under, over = pl.ds(0, 8), pl.ds(PAD + Z, 8)
    inner = pl.ds(PAD, Z)
    lab_copies = [
        remote(lab.at[1, inner], hlab.at[0, inner], bsem.at[0], lrsem.at[0], at(0, 1)),
        remote(lab.at[0, inner], hlab.at[1, inner], bsem.at[1], lrsem.at[1], at(0, -1)),
        remote(lab.at[:, high], lab.at[:, under], bsem.at[2], lrsem.at[2], at(1, 0)),
        remote(lab.at[:, low], lab.at[:, over], bsem.at[3], lrsem.at[3], at(-1, 0)),
        remote(lab.at[1, high], hlab.at[0, under], bsem.at[4], lrsem.at[4], at(1, 1)),
        remote(lab.at[1, low], hlab.at[0, over], bsem.at[5], lrsem.at[5], at(-1, 1)),
        remote(lab.at[0, low], hlab.at[1, over], bsem.at[6], lrsem.at[6], at(-1, -1)),
        remote(lab.at[0, high], hlab.at[1, under], bsem.at[7], lrsem.at[7], at(1, -1)),
    ]
    def y_copies(s, j):
        rows = pl.ds(pl.multiple_of(PAD + chunk_of(j) * ZC, 8), ZC)
        return (
            remote(post.at[s, 1, pl.ds(CYP[0], 5), rows], hdn.at[s, :, rows], y_send.at[s, 0, j], y_recv.at[s, 0, j], at(0, 1)),
            remote(post.at[s, 0, pl.ds(CYM[0], 5), rows], hup.at[s, :, rows], y_send.at[s, 1, j], y_recv.at[s, 1, j], at(0, -1)),
        )

    def z_copies(s):
        czp, czm = pl.ds(CZP[0], 5), pl.ds(CZM[0], 5)
        return (
            remote(post.at[s, :, czp, high], post.at[s, :, czp, under], z_send.at[s, 0], z_recv.at[s, 0], at(1, 0)),
            remote(post.at[s, :, czm, low], post.at[s, :, czm, over], z_send.at[s, 1], z_recv.at[s, 1], at(-1, 0)),
            remote(post.at[s, 1, PLANE[15], high], hdn.at[s, PLANE[15] - CYP[0], under], z_send.at[s, 2], z_recv.at[s, 2], at(1, 1)),
            remote(post.at[s, 1, PLANE[17], low], hdn.at[s, PLANE[17] - CYP[0], over], z_send.at[s, 3], z_recv.at[s, 3], at(-1, 1)),
            remote(post.at[s, 0, PLANE[16], low], hup.at[s, PLANE[16] - CYM[0], over], z_send.at[s, 4], z_recv.at[s, 4], at(-1, -1)),
            remote(post.at[s, 0, PLANE[18], high], hup.at[s, PLANE[18] - CYM[0], under], z_send.at[s, 5], z_recv.at[s, 5], at(1, -1)),
        )

    def store_post(s, y, rows, p):
        for plane, i in enumerate(ORDER):
            post[s, y, plane, rows, :] = p[i]

    def send_chunk(s, j):
        edges = z_copies(s)

        @pl.when(j == 0)
        def _():
            for q in (3, 4, 1):
                edges[q].start()

        @pl.when(j == 1)
        def _():
            for q in (2, 5, 0):
                edges[q].start()

        for c in y_copies(s, j):
            c.start()

    def source(s, y, i, z):
        cx, cy, cz = DIRS[i]
        rows = pl.ds(z - cz, BF)
        if y - cy < 0:
            v = hdn[s, PLANE[i] - CYP[0], rows, :]
        elif y - cy >= R:
            v = hup[s, PLANE[i] - CYM[0], rows, :]
        else:
            plane = 16 if i == 16 else PLANE[i]
            v = post[s, y - cy, plane, rows, :]
        return lane_shift(v, cx)

    def stream(s, y, z):
        here = pl.ds(z, BF)
        f = [post[s, y, PLANE[0], here, :]]
        for i in range(1, 19):
            open_ = mask[i - 1, y, pl.ds(z - PAD, BF), :] != 0
            f.append(jnp.where(open_, source(s, y, i, z), post[s, y, PLANE[OPP[i]], here, :]))
        return f

    def wait_sources(s, j):
        @pl.when(j == 0)
        def _():
            for q in (0, 1):
                for c in y_copies(s, q):
                    c.wait_recv()
            for c in z_copies(s):
                c.wait_recv()

        @pl.when(j + 2 < N)
        def _():
            for c in y_copies(s, j + 2):
                c.wait_recv()

    @pl.loop(0, N)
    def _(j):
        f_copy(j).wait()
        z0 = chunk_of(j) * ZC
        for y in range(R):
            @blocks(ZC // BF)
            def _(b):
                z = pl.multiple_of(z0 + BF * b, 8)
                f = [fbuf[i, pl.ds(2 * z + y, BF, stride=R), :] for i in range(19)]
                store_post(0, y, pl.ds(pl.multiple_of(z + PAD, 8), BF), collide(f))

    moving = range(1, 19)

    def set_masks(y, which, z, n, rows_of=lab):
        for cy, cz in sorted({DIRS[i][1:] for i in which}):
            rows = pl.ds(z + PAD - cz, n)
            if y - cy < 0:
                v = hlab[0, rows, :]
            elif y - cy >= R:
                v = hlab[1, rows, :]
            else:
                v = rows_of[y - cy, rows, :]
            for i in which:
                if DIRS[i][1:] == (cy, cz):
                    mask[i - 1, y, pl.ds(pl.multiple_of(z, 8), n), :] = lane_shift(v, DIRS[i][0])

    for y in range(R):
        @pl.loop(0, Z // BH)
        def _(b):
            set_masks(y, [i for i in moving if 0 <= y - DIRS[i][1] < R], BH * b, BH, near)

    pl.semaphore_wait(barrier, D - 1 + 6)

    for c in lab_copies:
        c.start()

    @pl.loop(0, N)
    def _(j):
        send_chunk(0, j)

    mine = pl.ds(pl.multiple_of(me_d * TILE, TILE), TILE)

    @pl.loop(1, D)
    def _(k):
        to = other(k)
        rows = pl.ds(pl.multiple_of(to[1] * TILE, TILE), TILE)
        remote(stage.at[rows], tin.at[mine], a_send.at[0], a_recv.at[0], to).start()

    tin[mine, :] = stage[mine, :]

    for c in lab_copies:
        c.wait_recv()
    for y in range(R):
        @pl.loop(0, Z // BH)
        def _(b):
            set_masks(y, [i for i in moving if not 0 <= y - DIRS[i][1] < R], BH * b, BH)
        for cz, z in ((1, 0), (-1, Z - 8)):
            set_masks(y, [i for i in moving if 0 <= y - DIRS[i][1] < R and DIRS[i][2] == cz], z, 8)

    hin, hlow, hhigh = pl.ds(HP, Z), pl.ds(HP, 8), pl.ds(HP + Z - 8, 8)
    hunder, hover = pl.ds(HP - 8, 8), pl.ds(HP + Z, 8)
    own, before, after = pl.ds(2, 2), pl.ds(0, 2), pl.ds(4, 2)
    t_copies = [
        remote(t0x.at[own, src], t0x.at[to, dst], t_send.at[q], t_recv.at[q], at(ds, dd))
        for q, (src, to, dst, ds, dd) in enumerate(
            (
                (hin, before, hin, 0, 1),
                (hin, after, hin, 0, -1),
                (hhigh, own, hunder, 1, 0),
                (hlow, own, hover, -1, 0),
                (hhigh, before, hunder, 1, 1),
                (hlow, before, hover, -1, 1),
                (hhigh, after, hunder, 1, -1),
                (hlow, after, hover, -1, -1),
            )
        )
    ]
    whole = pl.ds(0, Z * R - TILE)

    def spread_temperature():
        pltpu.make_async_copy(stage.at[whole], tin.at[whole], a_recv.at[0]).wait()
        for y in range(R):
            @pl.loop(0, Z // BH)
            def _(b):
                t0x[2 + y, pl.ds(pl.multiple_of(HP + BH * b, 8), BH), :] = tin[pl.ds(2 * BH * b + y, BH, stride=R), :]
        for c in t_copies:
            c.start()
        for e, labels in enumerate((hlab.at[0], lab.at[0], lab.at[1], hlab.at[1])):
            @pl.loop(0, NX)
            def _(b):
                pore = labels[pl.ds(pl.multiple_of(BE * b, 8), BE), :].astype(jnp.float32)
                rate[e, pl.ds(pl.multiple_of(BE * b + 8, 8), BE), :] = pore * RATE_PORE + (1.0 - pore) * RATE_GRAIN

    @pl.loop(1, FSTEPS)
    def _(s):
        @pl.loop(0, N)
        def _(j):
            wait_sources(s - 1, j)
            z0 = chunk_of(j) * ZC
            for y in range(R):
                @blocks(ZC // BF)
                def _(b):
                    z = pl.multiple_of(z0 + BF * b + PAD, 8)
                    store_post(s, y, pl.ds(z, BF), collide(stream(s - 1, y, z)))
            send_chunk(s, j)

        @pl.when(s == 1)
        def _():
            spread_temperature()

    upward, from_down = pl.ds(plane_of(2, "y"), 4), pl.ds(plane_of(0, "y"), 4)
    downward, from_up = pl.ds(plane_of(2, "x"), 4), pl.ds(plane_of(4, "x"), 4)
    both = pl.ds(plane_of(2, "x"), 6)

    def v_copies(j):
        rows = pl.ds(pl.multiple_of(HP + chunk_of(j) * ZC, 8), ZC)
        return (
            remote(vel.at[upward, rows], vel.at[from_down, rows], v_send.at[j, 0], v_recv.at[j, 0], at(0, 1)),
            remote(vel.at[downward, rows], vel.at[from_up, rows], v_send.at[j, 1], v_recv.at[j, 1], at(0, -1)),
        )

    w_copies = []
    for ds, src, dst in ((1, hhigh, hunder), (-1, hlow, hover)):
        for dd, fro, to in ((0, both, both), (1, upward, from_down), (-1, downward, from_up)):
            q = len(w_copies)
            w_copies.append(remote(vel.at[fro, src], vel.at[to, dst], w_send.at[q], w_recv.at[q], at(ds, dd)))

    def x_copies(b, part):
        rows = pl.ds(pl.multiple_of(8 + BE * b, 8), BE)
        planes = (pl.ds(0, 2), pl.ds(2, 1))[part]
        return [
            remote(
                xs.at[side, planes, rows], xr.at[side, planes, rows], x_send.at[side, b, part], x_recv.at[side, b, part], at(0, dd)
            )
            for side, dd in ((0, 1), (1, -1))
        ]

    def balance(temp, ux, uy, uz):
        a, b = 0.25 * temp, 0.125 * temp
        h = 0.5 * temp
        hx, hy, hz = h * ux, h * uy, h * uz
        return [a, b + hx, b - hx, b + hy, b - hy, b + hz, b - hz]

    def total(g):
        return ((g[0] + g[1]) + (g[2] + g[3])) + ((g[4] + g[5]) + g[6])

    def relax(g, q, r):
        return g + r * (q - g)

    def speed(e, here):
        return [vel[plane_of(e, part), here, :] for part in "xyz"]

    def gather(y, z, n):
        here = pl.ds(z, n)
        return [
            ga[0, y, here, :],
            lane_shift(ga[1, y, here, :], 1),
            lane_shift(ga[2, y, here, :], -1),
            gin[0, here, :] if y == 0 else ga[3, 0, here, :],
            gin[1, here, :] if y == 1 else ga[4, 1, here, :],
            ga[5, y, pl.ds(z - 1, n), :],
            ga[6, y, pl.ds(z + 1, n), :],
        ]

    def block_rows(b):
        return pl.multiple_of(8 + BE * b, 8)

    @pl.loop(0, N)
    def _(j):
        wait_sources(FSTEPS - 1, j)
        z0 = chunk_of(j) * ZC
        for y in range(R):
            @blocks(ZC // BF)
            def _(b):
                zr = pl.multiple_of(z0 + BF * b, 8)
                z = pl.multiple_of(zr + PAD, 8)
                f = stream(FSTEPS - 1, y, z)
                inter = pl.ds(2 * zr + y, BF, stride=R)
                for i in range(19):
                    obuf[i, inter, :] = f[i]
                pore = lab[y, pl.ds(z, BF), :].astype(jnp.float32)
                ux, uy, uz = velocity(f)
                there = pl.ds(pl.multiple_of(zr + HP, 8), BF)
                for part, u in (("x", ux), ("y", uy), ("z", uz)):
                    vel[plane_of(2 + y, part), there, :] = pore * u

        @pl.when(j == 1)
        def _():
            for c in w_copies:
                c.start()

        for c in v_copies(j):
            c.start()

    for c in t_copies:
        c.wait_recv()
    for c in w_copies:
        c.wait_recv()

    @pl.loop(0, N)
    def _(j):
        for c in v_copies(j):
            c.wait_recv()

    @pl.loop(0, NX)
    def _(b):
        z = block_rows(b)
        here, dn, up = pl.ds(z, BE), pl.ds(z - 1, BE), pl.ds(z + 1, BE)
        for e in (1, 2, 3, 4):
            t = t0x[e, here, :]
            q = balance(t, *speed(e, here))
            prev, nxt = t0x[e - 1, here, :], t0x[e + 1, here, :]
            tdn, tup = t0x[e, dn, :], t0x[e, up, :]
            g = [
                q[0],
                lane_shift(q[1], 1),
                lane_shift(q[2], -1),
                0.125 * prev + 0.5 * prev * vel[plane_of(e - 1, "y"), here, :],
                0.125 * nxt - 0.5 * nxt * vel[plane_of(e + 1, "y"), here, :],
                0.125 * tdn + 0.5 * tdn * vel[plane_of(e, "z"), dn, :],
                0.125 * tup - 0.5 * tup * vel[plane_of(e, "z"), up, :],
            ]
            q = balance(total(g), *speed(e, here))
            r = rate[e - 1, here, :]
            if e == 1:
                gin[0, here, :] = relax(g[3], q[3], r)
            elif e == 4:
                gin[1, here, :] = relax(g[4], q[4], r)
            else:
                for k in range(7):
                    ga[k, e - 2, here, :] = relax(g[k], q[k], r)

    @pl.loop(0, NX)
    def _(b):
        z = block_rows(b)
        here = pl.ds(z, BE)
        for y in range(R):
            g = gather(y, z, BE)
            q = balance(total(g), *speed(2 + y, here))
            r = rate[1 + y, here, :]
            p = [relax(g[k], q[k], r) for k in range(7)]
            for n, k in enumerate((0, 1, 2, 5, 6)):
                gb[n, y, here, :] = p[k]
            xs[0, y, here, :] = p[3]
            xs[1, 1 - y, here, :] = p[4]
        for c in x_copies(b, 0):
            c.start()

    def others(y, z):
        here = pl.ds(z, BE)
        return [
            gb[0, y, here, :],
            lane_shift(gb[1, y, here, :], 1),
            lane_shift(gb[2, y, here, :], -1),
            gb[3, y, pl.ds(z - 1, BE), :],
            gb[4, y, pl.ds(z + 1, BE), :],
        ]

    @pl.loop(0, NX)
    def _(b):
        z = block_rows(b)
        for y in range(R):
            a = others(y, z)
            xs[1 - y, 2, pl.ds(z, BE), :] = (a[0] + (a[1] + a[2])) + (a[3] + a[4])
        for c in x_copies(b, 1):
            c.start()

    @pl.loop(0, NX)
    def _(b):
        z = block_rows(b)
        here = pl.ds(z, BE)
        for c in x_copies(b, 0) + x_copies(b, 1):
            c.wait_recv()
        for y in range(R):
            a = others(y, z)
            yp = xr[0, 1, here, :] if y == 0 else xs[0, 0, here, :]
            ym = xr[1, 1, here, :] if y == 1 else xs[1, 0, here, :]
            g = a[:3] + [yp, ym] + a[3:]
            q = balance(total(g), *speed(2 + y, here))
            r = rate[1 + y, here, :]
            for k in range(7):
                ga[k, y, here, :] = relax(g[k], q[k], r)
        for side, e, sign in ((0, 1, 0.5), (1, 4, -0.5)):
            g = xr[side, 0, here, :]
            t = (xr[side, 2, here, :] + g) + xs[1 - side, 1, here, :]
            q = 0.125 * t + sign * t * vel[plane_of(e, "y"), here, :]
            gin[side, here, :] = relax(g, q, rate[e - 1, here, :])

    for y in range(R):
        @pl.loop(0, Z // BH)
        def _(b):
            zr = pl.multiple_of(BH * b, 8)
            tout[pl.ds(2 * zr + y, BH, stride=R), :] = total(gather(y, pl.multiple_of(zr + HP, 8), BH))

    @pl.loop(1, D)
    def _(k):
        to = other(k)
        rows = pl.ds(pl.multiple_of(to[1] * TILE, TILE), TILE)
        remote(tout.at[rows], tback.at[mine], a_send.at[1], a_recv.at[1], to).start()

    tback[mine, :] = tout[mine, :]

    for c in lab_copies:
        c.wait_send()

    @pl.loop(0, FSTEPS)
    def _(s):
        @pl.loop(0, N)
        def _(j):
            for c in y_copies(s, j):
                c.wait_send()
        for c in z_copies(s):
            c.wait_send()

    for c in t_copies + w_copies:
        c.wait_send()

    @pl.loop(0, N)
    def _(j):
        for c in v_copies(j):
            c.wait_send()

    @pl.loop(0, NX)
    def _(b):
        for c in x_copies(b, 0) + x_copies(b, 1):
            c.wait_send()

    pltpu.make_async_copy(stage.at[whole], tin.at[whole], a_send.at[0]).wait()
    pltpu.make_async_copy(tout.at[whole], tback.at[whole], a_send.at[1]).wait()
    pltpu.make_async_copy(tout.at[whole], tback.at[whole], a_recv.at[1]).wait()
    for z in range(Z // D):
        for y in range(R):
            for m in range(D // G):
                tout_ref[z, pl.ds(R * G * m + y, G, stride=R), :] = tback[
                    pl.ds(TILE * G * m + R * z + y, G, stride=TILE), :
                ]


def write_out(pops, temp, pops_out, temp_out, sem):
    copies = [
        pltpu.make_async_copy(pops, pops_out, sem.at[0]),
        pltpu.make_async_copy(temp, temp_out, sem.at[1]),
    ]
    for c in copies:
        c.start()
    for c in copies:
        c.wait()


def local(S, D, f, labels, t0, zc=16):
    _, Z, R, X = f.shape
    N = Z // zc
    Zp, Zh = Z + 2 * PAD, Z + 2 * HP
    NX = (Z + 16) // BE
    f32, i32 = jnp.float32, jnp.int32
    V, DMA = pltpu.VMEM, pltpu.SemaphoreType.DMA
    any_ = pl.BlockSpec(memory_space=pl.ANY)
    vmem = pl.BlockSpec(memory_space=pltpu.VMEM)
    pops, temp = pl.pallas_call(
        functools.partial(kernel, S, D, Z, zc, X),
        out_shape=(
            pltpu.VMEM((19, Z * R, X), f32),
            pltpu.VMEM(t0.shape, f32),
        ),
        in_specs=[any_, any_, vmem],
        out_specs=(vmem, vmem),
        scratch_shapes=[
            V((19, Z * R, X), f32),
            V((Z * R, X), i32),
            V((FSTEPS, R, PLANES, Zp, X), f32),
            V((FSTEPS, 5, Zp, X), f32),
            V((FSTEPS, 5, Zp, X), f32),
            V((R, Zp, X), i32),
            V((R, Zp, X), i32),
            V((2, Zp, X), i32),
            V((18, R, Z, X), i32),
            V((4, Zh, X), f32),
            V((18, Zh, X), f32),
            V((6, Zh, X), f32),
            V((7, R, Zh, X), f32),
            V((2, Zh, X), f32),
            V((5, R, Zh, X), f32),
            V((2, 3, Zh, X), f32),
            V((2, 3, Zh, X), f32),
            V((Z * R, X), f32),
            V((Z * R, X), f32),
            V((Z * R, X), f32),
            V((Z * R, X), f32),
            DMA(()),
            DMA((N,)),
            DMA((8,)),
            DMA((8,)),
            DMA((FSTEPS, 2, N)),
            DMA((FSTEPS, 6)),
            DMA((FSTEPS, 2, N)),
            DMA((FSTEPS, 6)),
            DMA((2,)),
            DMA((2,)),
            DMA((8,)),
            DMA((8,)),
            DMA((N, 2)),
            DMA((N, 2)),
            DMA((6,)),
            DMA((6,)),
            DMA((2, NX, 2)),
            DMA((2, NX, 2)),
        ],
        compiler_params=pltpu.CompilerParams(
            collective_id=0, has_side_effects=True, vmem_limit_bytes=56 * 1024 * 1024
        ),
    )(f.reshape(19, Z * R, X), labels.reshape(Z * R, X), t0)
    return pops.reshape(19, Z, R, X), temp


def solution(mesh):
    S, D = mesh.shape["sec"], mesh.shape["dev"]
    return jax.shard_map(
        functools.partial(local, S, D),
        mesh=mesh,
        in_specs=(
            P(None, "sec", "dev", None),
            P("sec", "dev", None),
            P(("sec", "dev"), None, None),
        ),
        out_specs=(P(None, "sec", "dev", None), P(("sec", "dev"), None, None)),
        check_vma=False,
    )
```

```python
import functools

import jax
import jax.numpy as jnp
from jax import lax
from jax.experimental import pallas as pl
from jax.experimental.pallas import tpu as pltpu
from jax.sharding import PartitionSpec as P

FSTEPS = 4

DIRS = [
    (0, 0, 0), (1, 0, 0), (-1, 0, 0), (0, 1, 0), (0, -1, 0), (0, 0, 1), (0, 0, -1),
    (1, 1, 0), (-1, -1, 0), (1, -1, 0), (-1, 1, 0), (1, 0, 1), (-1, 0, -1), (1, 0, -1), (-1, 0, 1),
    (0, 1, 1), (0, -1, -1), (0, 1, -1), (0, -1, 1),
]
OPP = [0, 2, 1, 4, 3, 6, 5, 8, 7, 10, 9, 12, 11, 14, 13, 16, 15, 18, 17]
OMEGA = 0.8
RATE_PORE = 1.0 / 0.7
RATE_GRAIN = 1.0 / 1.4

ORDER = [16, 4, 8, 9, 18, 5, 11, 14, 15, 3, 7, 10, 17, 6, 12, 13, 16, 0, 1, 2]
PLANE = {i: p for p, i in reversed(list(enumerate(ORDER)))}
CYM, CZP, CYP, CZM = (0, 5), (4, 9), (8, 13), (12, 17)
PLANES = len(ORDER)

MESH = pl.DeviceIdType.MESH
PAD = 8
BF = 16
BH = 32
HP = 16
BE = 24
BX = 72


def plane_of(e, part):
    return 3 * e + ("xzy" if e % 2 == 0 else "yxz").index(part)


def blocks(n):
    def over(body):
        if n == 1:
            body(0)
        else:
            pl.loop(0, n)(body)

    return over


def collide(f):
    rho = f[0]
    d = {}
    for i in range(1, 19, 2):
        rho = rho + (f[i] + f[i + 1])
        d[i] = f[i] - f[i + 1]
    mx = (d[1] + d[7]) + (d[9] + d[11]) + d[13]
    my = (d[3] + d[7]) + (d[15] - d[9]) + d[17]
    mz = (d[5] + d[11]) + (d[15] - d[13]) - d[17]
    inv = 1.0 / rho
    ux, uy, uz = mx * inv, my * inv, mz * inv
    even = rho - 1.5 * (mx * ux + my * uy + mz * uz)
    keep = 1.0 - OMEGA
    post = {0: keep * f[0] + (OMEGA / 3.0) * even}
    for i in range(1, 19, 2):
        w = OMEGA / (18.0 if i < 7 else 36.0)
        cx, cy, cz = DIRS[i]
        m = u = None
        for c, mm, uu in ((cx, mx, ux), (cy, my, uy), (cz, mz, uz)):
            if c == 0:
                continue
            if m is None:
                m, u = mm, uu
            elif c > 0:
                m, u = m + mm, u + uu
            else:
                m, u = m - mm, u - uu
        e = w * even + (4.5 * w) * (m * u)
        o = (3.0 * w) * m
        post[i] = keep * f[i] + (e + o)
        post[i + 1] = keep * f[i + 1] + (e - o)
    return post


def velocity(f):
    rho = f[0]
    d = {}
    for i in range(1, 19, 2):
        rho = rho + (f[i] + f[i + 1])
        d[i] = f[i] - f[i + 1]
    mx = (d[1] + d[7]) + (d[9] + d[11]) + d[13]
    my = (d[3] + d[7]) + (d[15] - d[9]) + d[17]
    mz = (d[5] + d[11]) + (d[15] - d[13]) - d[17]
    inv = 1.0 / rho
    return mx * inv, my * inv, mz * inv


def lane_shift(x, c):
    return pltpu.roll(x, c % x.shape[-1], 1) if c else x


def kernel(
    S, D, Z, ZC, X,
    f_hbm, lab_hbm, t0_hbm, obuf, tout_ref,
    fbuf, lraw, t0_ref, post, hdn, hup, lab, near, hlab, mask, rate, vel, t0x, ga, gin, gb, xs, xr, stage, tin, tout, tback,
    lsem, t0sem, fsem, bsem, lrsem, y_send, z_send, y_recv, z_recv,
    a_send, a_recv, t_send, t_recv, v_send, v_recv, w_send, w_recv, x_send, x_recv,
):
    N = Z // ZC
    NX = (Z + 16) // BX
    R = 2
    TILE = (Z // D) * R
    me_s, me_d = lax.axis_index("sec"), lax.axis_index("dev")

    def at(ds, dd):
        return (lax.rem(me_s + ds + S, S), lax.rem(me_d + dd + D, D))

    def other(k):
        return (me_s, lax.rem(me_d + k, D))

    def chunk_of(j):
        half = j // 2
        return jnp.where(j % 2 == 0, half, N - 1 - half)

    lab_copy = pltpu.make_async_copy(lab_hbm, lraw, lsem)
    lab_copy.start()
    t0_copy = pltpu.make_async_copy(t0_hbm, t0_ref, t0sem)
    t0_copy.start()

    def f_copy(j):
        rows = pl.ds(pl.multiple_of(chunk_of(j) * (ZC * R), ZC * R), ZC * R)
        return pltpu.make_async_copy(f_hbm.at[:, rows, :], fbuf.at[:, rows, :], fsem.at[j])

    @pl.loop(0, N)
    def _(j):
        f_copy(j).start()

    barrier = pltpu.get_barrier_semaphore()

    @pl.loop(1, D)
    def _(k):
        pl.semaphore_signal(barrier, inc=1, device_id=other(k), device_id_type=MESH)

    for ds in (-1, 1):
        for dd in (-1, 0, 1):
            pl.semaphore_signal(barrier, inc=1, device_id=at(ds, dd), device_id_type=MESH)

    t0_copy.wait()
    G = min(8, D)
    for z in range(Z // D):
        for y in range(R):
            for m in range(D // G):
                stage[pl.ds(TILE * G * m + R * z + y, G, stride=TILE), :] = t0_ref[
                    z, pl.ds(R * G * m + y, G, stride=R), :
                ]

    lab_copy.wait()
    for y in range(R):
        for b in range(Z // 8):
            lab[y, pl.ds(PAD + 8 * b, 8), :] = lraw[pl.ds(16 * b + y, 8, stride=R), :]
            near[y, pl.ds(PAD + 8 * b, 8), :] = lraw[pl.ds(16 * b + y, 8, stride=R), :]

    def remote(src, dst, send, recv, to):
        return pltpu.make_async_remote_copy(
            src_ref=src, dst_ref=dst, send_sem=send, recv_sem=recv, device_id=to, device_id_type=MESH
        )

    low, high = pl.ds(PAD, 8), pl.ds(Z, 8)
    under, over = pl.ds(0, 8), pl.ds(PAD + Z, 8)
    inner = pl.ds(PAD, Z)
    lab_copies = [
        remote(lab.at[1, inner], hlab.at[0, inner], bsem.at[0], lrsem.at[0], at(0, 1)),
        remote(lab.at[0, inner], hlab.at[1, inner], bsem.at[1], lrsem.at[1], at(0, -1)),
        remote(lab.at[:, high], lab.at[:, under], bsem.at[2], lrsem.at[2], at(1, 0)),
        remote(lab.at[:, low], lab.at[:, over], bsem.at[3], lrsem.at[3], at(-1, 0)),
        remote(lab.at[1, high], hlab.at[0, under], bsem.at[4], lrsem.at[4], at(1, 1)),
        remote(lab.at[1, low], hlab.at[0, over], bsem.at[5], lrsem.at[5], at(-1, 1)),
        remote(lab.at[0, low], hlab.at[1, over], bsem.at[6], lrsem.at[6], at(-1, -1)),
        remote(lab.at[0, high], hlab.at[1, under], bsem.at[7], lrsem.at[7], at(1, -1)),
    ]
    def y_copies(s, j):
        rows = pl.ds(pl.multiple_of(PAD + chunk_of(j) * ZC, 8), ZC)
        return (
            remote(post.at[s, 1, pl.ds(CYP[0], 5), rows], hdn.at[s, :, rows], y_send.at[s, 0, j], y_recv.at[s, 0, j], at(0, 1)),
            remote(post.at[s, 0, pl.ds(CYM[0], 5), rows], hup.at[s, :, rows], y_send.at[s, 1, j], y_recv.at[s, 1, j], at(0, -1)),
        )

    def z_copies(s):
        czp, czm = pl.ds(CZP[0], 5), pl.ds(CZM[0], 5)
        return (
            remote(post.at[s, :, czp, high], post.at[s, :, czp, under], z_send.at[s, 0], z_recv.at[s, 0], at(1, 0)),
            remote(post.at[s, :, czm, low], post.at[s, :, czm, over], z_send.at[s, 1], z_recv.at[s, 1], at(-1, 0)),
            remote(post.at[s, 1, PLANE[15], high], hdn.at[s, PLANE[15] - CYP[0], under], z_send.at[s, 2], z_recv.at[s, 2], at(1, 1)),
            remote(post.at[s, 1, PLANE[17], low], hdn.at[s, PLANE[17] - CYP[0], over], z_send.at[s, 3], z_recv.at[s, 3], at(-1, 1)),
            remote(post.at[s, 0, PLANE[16], low], hup.at[s, PLANE[16] - CYM[0], over], z_send.at[s, 4], z_recv.at[s, 4], at(-1, -1)),
            remote(post.at[s, 0, PLANE[18], high], hup.at[s, PLANE[18] - CYM[0], under], z_send.at[s, 5], z_recv.at[s, 5], at(1, -1)),
        )

    def store_post(s, y, rows, p):
        for plane, i in enumerate(ORDER):
            post[s, y, plane, rows, :] = p[i]

    def send_chunk(s, j):
        edges = z_copies(s)

        @pl.when(j == 0)
        def _():
            for q in (3, 4, 1):
                edges[q].start()

        @pl.when(j == 1)
        def _():
            for q in (2, 5, 0):
                edges[q].start()

        for c in y_copies(s, j):
            c.start()

    def source(s, y, i, z):
        cx, cy, cz = DIRS[i]
        rows = pl.ds(z - cz, BF)
        if y - cy < 0:
            v = hdn[s, PLANE[i] - CYP[0], rows, :]
        elif y - cy >= R:
            v = hup[s, PLANE[i] - CYM[0], rows, :]
        else:
            plane = 16 if i == 16 else PLANE[i]
            v = post[s, y - cy, plane, rows, :]
        return lane_shift(v, cx)

    def stream(s, y, z):
        here = pl.ds(z, BF)
        f = [post[s, y, PLANE[0], here, :]]
        for i in range(1, 19):
            open_ = mask[i - 1, y, pl.ds(z - PAD, BF), :] != 0
            f.append(jnp.where(open_, source(s, y, i, z), post[s, y, PLANE[OPP[i]], here, :]))
        return f

    def wait_sources(s, j):
        @pl.when(j == 0)
        def _():
            for q in (0, 1):
                for c in y_copies(s, q):
                    c.wait_recv()
            for c in z_copies(s):
                c.wait_recv()

        @pl.when(j + 2 < N)
        def _():
            for c in y_copies(s, j + 2):
                c.wait_recv()

    @pl.loop(0, N)
    def _(j):
        f_copy(j).wait()
        z0 = chunk_of(j) * ZC
        for y in range(R):
            @blocks(ZC // BF)
            def _(b):
                z = pl.multiple_of(z0 + BF * b, 8)
                f = [fbuf[i, pl.ds(2 * z + y, BF, stride=R), :] for i in range(19)]
                store_post(0, y, pl.ds(pl.multiple_of(z + PAD, 8), BF), collide(f))

    moving = range(1, 19)

    def set_masks(y, which, z, n, rows_of=lab):
        for cy, cz in sorted({DIRS[i][1:] for i in which}):
            rows = pl.ds(z + PAD - cz, n)
            if y - cy < 0:
                v = hlab[0, rows, :]
            elif y - cy >= R:
                v = hlab[1, rows, :]
            else:
                v = rows_of[y - cy, rows, :]
            for i in which:
                if DIRS[i][1:] == (cy, cz):
                    mask[i - 1, y, pl.ds(pl.multiple_of(z, 8), n), :] = lane_shift(v, DIRS[i][0])

    for y in range(R):
        @pl.loop(0, Z // BH)
        def _(b):
            set_masks(y, [i for i in moving if 0 <= y - DIRS[i][1] < R], BH * b, BH, near)

    pl.semaphore_wait(barrier, D - 1 + 6)

    for c in lab_copies:
        c.start()

    @pl.loop(0, N)
    def _(j):
        send_chunk(0, j)

    mine = pl.ds(pl.multiple_of(me_d * TILE, TILE), TILE)

    @pl.loop(1, D)
    def _(k):
        to = other(k)
        rows = pl.ds(pl.multiple_of(to[1] * TILE, TILE), TILE)
        remote(stage.at[rows], tin.at[mine], a_send.at[0], a_recv.at[0], to).start()

    tin[mine, :] = stage[mine, :]

    for c in lab_copies:
        c.wait_recv()
    for y in range(R):
        @pl.loop(0, Z // BH)
        def _(b):
            set_masks(y, [i for i in moving if not 0 <= y - DIRS[i][1] < R], BH * b, BH)
        for cz, z in ((1, 0), (-1, Z - 8)):
            set_masks(y, [i for i in moving if 0 <= y - DIRS[i][1] < R and DIRS[i][2] == cz], z, 8)

    hin, hlow, hhigh = pl.ds(HP, Z), pl.ds(HP, 8), pl.ds(HP + Z - 8, 8)
    hunder, hover = pl.ds(HP - 8, 8), pl.ds(HP + Z, 8)
    own, before, after = pl.ds(2, 2), pl.ds(0, 2), pl.ds(4, 2)
    t_copies = [
        remote(t0x.at[own, src], t0x.at[to, dst], t_send.at[q], t_recv.at[q], at(ds, dd))
        for q, (src, to, dst, ds, dd) in enumerate(
            (
                (hin, before, hin, 0, 1),
                (hin, after, hin, 0, -1),
                (hhigh, own, hunder, 1, 0),
                (hlow, own, hover, -1, 0),
                (hhigh, before, hunder, 1, 1),
                (hlow, before, hover, -1, 1),
                (hhigh, after, hunder, 1, -1),
                (hlow, after, hover, -1, -1),
            )
        )
    ]
    whole = pl.ds(0, Z * R - TILE)

    def spread_temperature():
        pltpu.make_async_copy(stage.at[whole], tin.at[whole], a_recv.at[0]).wait()
        for y in range(R):
            @pl.loop(0, Z // BH)
            def _(b):
                t0x[2 + y, pl.ds(pl.multiple_of(HP + BH * b, 8), BH), :] = tin[pl.ds(2 * BH * b + y, BH, stride=R), :]
        for c in t_copies:
            c.start()
        for e, labels in enumerate((hlab.at[0], lab.at[0], lab.at[1], hlab.at[1])):
            @pl.loop(0, NX)
            def _(b):
                pore = labels[pl.ds(pl.multiple_of(BX * b, 8), BX), :].astype(jnp.float32)
                rate[e, pl.ds(pl.multiple_of(BX * b + 8, 8), BX), :] = pore * RATE_PORE + (1.0 - pore) * RATE_GRAIN

    @pl.loop(1, FSTEPS)
    def _(s):
        @pl.loop(0, N)
        def _(j):
            wait_sources(s - 1, j)
            z0 = chunk_of(j) * ZC
            for y in range(R):
                @blocks(ZC // BF)
                def _(b):
                    z = pl.multiple_of(z0 + BF * b + PAD, 8)
                    store_post(s, y, pl.ds(z, BF), collide(stream(s - 1, y, z)))
            send_chunk(s, j)

        @pl.when(s == 1)
        def _():
            spread_temperature()

    upward, from_down = pl.ds(plane_of(2, "y"), 4), pl.ds(plane_of(0, "y"), 4)
    downward, from_up = pl.ds(plane_of(2, "x"), 4), pl.ds(plane_of(4, "x"), 4)
    both = pl.ds(plane_of(2, "x"), 6)

    def v_copies(j):
        rows = pl.ds(pl.multiple_of(HP + chunk_of(j) * ZC, 8), ZC)
        return (
            remote(vel.at[upward, rows], vel.at[from_down, rows], v_send.at[j, 0], v_recv.at[j, 0], at(0, 1)),
            remote(vel.at[downward, rows], vel.at[from_up, rows], v_send.at[j, 1], v_recv.at[j, 1], at(0, -1)),
        )

    w_copies = []
    for ds, src, dst in ((1, hhigh, hunder), (-1, hlow, hover)):
        for dd, fro, to in ((0, both, both), (1, upward, from_down), (-1, downward, from_up)):
            q = len(w_copies)
            w_copies.append(remote(vel.at[fro, src], vel.at[to, dst], w_send.at[q], w_recv.at[q], at(ds, dd)))

    def x_copies(b, part):
        rows = pl.ds(pl.multiple_of(8 + BX * b, 8), BX)
        planes = (pl.ds(0, 2), pl.ds(2, 1))[part]
        return [
            remote(
                xs.at[side, planes, rows], xr.at[side, planes, rows], x_send.at[side, b, part], x_recv.at[side, b, part], at(0, dd)
            )
            for side, dd in ((0, 1), (1, -1))
        ]

    def balance(temp, ux, uy, uz):
        a, b = 0.25 * temp, 0.125 * temp
        h = 0.5 * temp
        hx, hy, hz = h * ux, h * uy, h * uz
        return [a, b + hx, b - hx, b + hy, b - hy, b + hz, b - hz]

    def total(g):
        return ((g[0] + g[1]) + (g[2] + g[3])) + ((g[4] + g[5]) + g[6])

    def relax(g, q, r):
        return g + r * (q - g)

    def speed(e, here):
        return [vel[plane_of(e, part), here, :] for part in "xyz"]

    def gather(y, z, n):
        here = pl.ds(z, n)
        return [
            ga[0, y, here, :],
            lane_shift(ga[1, y, here, :], 1),
            lane_shift(ga[2, y, here, :], -1),
            gin[0, here, :] if y == 0 else ga[3, 0, here, :],
            gin[1, here, :] if y == 1 else ga[4, 1, here, :],
            ga[5, y, pl.ds(z - 1, n), :],
            ga[6, y, pl.ds(z + 1, n), :],
        ]

    def over_block(b):
        def run(body):
            @blocks(BX // BE)
            def _(k):
                body(pl.multiple_of(8 + BX * b + BE * k, 8))

        return run

    @pl.loop(0, N)
    def _(j):
        wait_sources(FSTEPS - 1, j)
        z0 = chunk_of(j) * ZC
        for y in range(R):
            @blocks(ZC // BF)
            def _(b):
                zr = pl.multiple_of(z0 + BF * b, 8)
                z = pl.multiple_of(zr + PAD, 8)
                f = stream(FSTEPS - 1, y, z)
                inter = pl.ds(2 * zr + y, BF, stride=R)
                for i in range(19):
                    obuf[i, inter, :] = f[i]
                pore = lab[y, pl.ds(z, BF), :].astype(jnp.float32)
                ux, uy, uz = velocity(f)
                there = pl.ds(pl.multiple_of(zr + HP, 8), BF)
                for part, u in (("x", ux), ("y", uy), ("z", uz)):
                    vel[plane_of(2 + y, part), there, :] = pore * u

        @pl.when(j == 1)
        def _():
            for c in w_copies:
                c.start()

        for c in v_copies(j):
            c.start()

    for c in t_copies:
        c.wait_recv()
    for c in w_copies:
        c.wait_recv()

    @pl.loop(0, N)
    def _(j):
        for c in v_copies(j):
            c.wait_recv()

    @pl.loop(0, NX)
    def _(b):
        @over_block(b)
        def _(z):
            here, dn, up = pl.ds(z, BE), pl.ds(z - 1, BE), pl.ds(z + 1, BE)
            for e in (1, 2, 3, 4):
                t = t0x[e, here, :]
                q = balance(t, *speed(e, here))
                prev, nxt = t0x[e - 1, here, :], t0x[e + 1, here, :]
                tdn, tup = t0x[e, dn, :], t0x[e, up, :]
                g = [
                    q[0],
                    lane_shift(q[1], 1),
                    lane_shift(q[2], -1),
                    0.125 * prev + 0.5 * prev * vel[plane_of(e - 1, "y"), here, :],
                    0.125 * nxt - 0.5 * nxt * vel[plane_of(e + 1, "y"), here, :],
                    0.125 * tdn + 0.5 * tdn * vel[plane_of(e, "z"), dn, :],
                    0.125 * tup - 0.5 * tup * vel[plane_of(e, "z"), up, :],
                ]
                q = balance(total(g), *speed(e, here))
                r = rate[e - 1, here, :]
                if e == 1:
                    gin[0, here, :] = relax(g[3], q[3], r)
                elif e == 4:
                    gin[1, here, :] = relax(g[4], q[4], r)
                else:
                    for k in range(7):
                        ga[k, e - 2, here, :] = relax(g[k], q[k], r)

    @pl.loop(0, NX)
    def _(b):
        @over_block(b)
        def _(z):
            here = pl.ds(z, BE)
            for y in range(R):
                g = gather(y, z, BE)
                q = balance(total(g), *speed(2 + y, here))
                r = rate[1 + y, here, :]
                p = [relax(g[k], q[k], r) for k in range(7)]
                for n, k in enumerate((0, 1, 2, 5, 6)):
                    gb[n, y, here, :] = p[k]
                xs[0, y, here, :] = p[3]
                xs[1, 1 - y, here, :] = p[4]

        for c in x_copies(b, 0):
            c.start()

    def others(y, z):
        here = pl.ds(z, BE)
        return [
            gb[0, y, here, :],
            lane_shift(gb[1, y, here, :], 1),
            lane_shift(gb[2, y, here, :], -1),
            gb[3, y, pl.ds(z - 1, BE), :],
            gb[4, y, pl.ds(z + 1, BE), :],
        ]

    @pl.loop(0, NX)
    def _(b):
        @over_block(b)
        def _(z):
            for y in range(R):
                a = others(y, z)
                xs[1 - y, 2, pl.ds(z, BE), :] = (a[0] + (a[1] + a[2])) + (a[3] + a[4])

        for c in x_copies(b, 1):
            c.start()

    @pl.loop(0, NX)
    def _(b):
        for c in x_copies(b, 0) + x_copies(b, 1):
            c.wait_recv()
        @over_block(b)
        def _(z):
            here = pl.ds(z, BE)
            for y in range(R):
                a = others(y, z)
                yp = xr[0, 1, here, :] if y == 0 else xs[0, 0, here, :]
                ym = xr[1, 1, here, :] if y == 1 else xs[1, 0, here, :]
                g = a[:3] + [yp, ym] + a[3:]
                q = balance(total(g), *speed(2 + y, here))
                r = rate[1 + y, here, :]
                for k in range(7):
                    ga[k, y, here, :] = relax(g[k], q[k], r)
            for side, e, sign in ((0, 1, 0.5), (1, 4, -0.5)):
                g = xr[side, 0, here, :]
                t = (xr[side, 2, here, :] + g) + xs[1 - side, 1, here, :]
                q = 0.125 * t + sign * t * vel[plane_of(e, "y"), here, :]
                gin[side, here, :] = relax(g, q, rate[e - 1, here, :])

    for y in range(R):
        @pl.loop(0, Z // BH)
        def _(b):
            zr = pl.multiple_of(BH * b, 8)
            tout[pl.ds(2 * zr + y, BH, stride=R), :] = total(gather(y, pl.multiple_of(zr + HP, 8), BH))

    @pl.loop(1, D)
    def _(k):
        to = other(k)
        rows = pl.ds(pl.multiple_of(to[1] * TILE, TILE), TILE)
        remote(tout.at[rows], tback.at[mine], a_send.at[1], a_recv.at[1], to).start()

    tback[mine, :] = tout[mine, :]

    for c in lab_copies:
        c.wait_send()

    @pl.loop(0, FSTEPS)
    def _(s):
        @pl.loop(0, N)
        def _(j):
            for c in y_copies(s, j):
                c.wait_send()
        for c in z_copies(s):
            c.wait_send()

    for c in t_copies + w_copies:
        c.wait_send()

    @pl.loop(0, N)
    def _(j):
        for c in v_copies(j):
            c.wait_send()

    @pl.loop(0, NX)
    def _(b):
        for c in x_copies(b, 0) + x_copies(b, 1):
            c.wait_send()

    pltpu.make_async_copy(stage.at[whole], tin.at[whole], a_send.at[0]).wait()
    pltpu.make_async_copy(tout.at[whole], tback.at[whole], a_send.at[1]).wait()
    pltpu.make_async_copy(tout.at[whole], tback.at[whole], a_recv.at[1]).wait()
    for z in range(Z // D):
        for y in range(R):
            for m in range(D // G):
                tout_ref[z, pl.ds(R * G * m + y, G, stride=R), :] = tback[
                    pl.ds(TILE * G * m + R * z + y, G, stride=TILE), :
                ]


def write_out(pops, temp, pops_out, temp_out, sem):
    copies = [
        pltpu.make_async_copy(pops, pops_out, sem.at[0]),
        pltpu.make_async_copy(temp, temp_out, sem.at[1]),
    ]
    for c in copies:
        c.start()
    for c in copies:
        c.wait()


def local(S, D, f, labels, t0, zc=16):
    _, Z, R, X = f.shape
    N = Z // zc
    Zp, Zh = Z + 2 * PAD, Z + 2 * HP
    NX = (Z + 16) // BX
    f32, i32 = jnp.float32, jnp.int32
    V, DMA = pltpu.VMEM, pltpu.SemaphoreType.DMA
    any_ = pl.BlockSpec(memory_space=pl.ANY)
    vmem = pl.BlockSpec(memory_space=pltpu.VMEM)
    pops, temp = pl.pallas_call(
        functools.partial(kernel, S, D, Z, zc, X),
        out_shape=(
            pltpu.VMEM((19, Z * R, X), f32),
            pltpu.VMEM(t0.shape, f32),
        ),
        in_specs=[any_, any_, any_],
        out_specs=(vmem, vmem),
        scratch_shapes=[
            V((19, Z * R, X), f32),
            V((Z * R, X), i32),
            V(t0.shape, f32),
            V((FSTEPS, R, PLANES, Zp, X), f32),
            V((FSTEPS, 5, Zp, X), f32),
            V((FSTEPS, 5, Zp, X), f32),
            V((R, Zp, X), i32),
            V((R, Zp, X), i32),
            V((2, Zp, X), i32),
            V((18, R, Z, X), i32),
            V((4, Zh, X), f32),
            V((18, Zh, X), f32),
            V((6, Zh, X), f32),
            V((7, R, Zh, X), f32),
            V((2, Zh, X), f32),
            V((5, R, Zh, X), f32),
            V((2, 3, Zh, X), f32),
            V((2, 3, Zh, X), f32),
            V((Z * R, X), f32),
            V((Z * R, X), f32),
            V((Z * R, X), f32),
            V((Z * R, X), f32),
            DMA(()),
            DMA(()),
            DMA((N,)),
            DMA((8,)),
            DMA((8,)),
            DMA((FSTEPS, 2, N)),
            DMA((FSTEPS, 6)),
            DMA((FSTEPS, 2, N)),
            DMA((FSTEPS, 6)),
            DMA((2,)),
            DMA((2,)),
            DMA((8,)),
            DMA((8,)),
            DMA((N, 2)),
            DMA((N, 2)),
            DMA((6,)),
            DMA((6,)),
            DMA((2, NX, 2)),
            DMA((2, NX, 2)),
        ],
        compiler_params=pltpu.CompilerParams(
            collective_id=0, has_side_effects=True, vmem_limit_bytes=56 * 1024 * 1024
        ),
    )(f.reshape(19, Z * R, X), labels.reshape(Z * R, X), t0)
    return pops.reshape(19, Z, R, X), temp


def solution(mesh):
    S, D = mesh.shape["sec"], mesh.shape["dev"]
    return jax.shard_map(
        functools.partial(local, S, D),
        mesh=mesh,
        in_specs=(
            P(None, "sec", "dev", None),
            P("sec", "dev", None),
            P(("sec", "dev"), None, None),
        ),
        out_specs=(P(None, "sec", "dev", None), P(("sec", "dev"), None, None)),
        check_vma=False,
    )
```

```python
import functools

import jax
import jax.numpy as jnp
from jax import lax
from jax.experimental import pallas as pl
from jax.experimental.pallas import tpu as pltpu
from jax.sharding import PartitionSpec as P

FSTEPS = 4

DIRS = [
    (0, 0, 0), (1, 0, 0), (-1, 0, 0), (0, 1, 0), (0, -1, 0), (0, 0, 1), (0, 0, -1),
    (1, 1, 0), (-1, -1, 0), (1, -1, 0), (-1, 1, 0), (1, 0, 1), (-1, 0, -1), (1, 0, -1), (-1, 0, 1),
    (0, 1, 1), (0, -1, -1), (0, 1, -1), (0, -1, 1),
]
OPP = [0, 2, 1, 4, 3, 6, 5, 8, 7, 10, 9, 12, 11, 14, 13, 16, 15, 18, 17]
OMEGA = 0.8
RATE_PORE = 1.0 / 0.7
RATE_GRAIN = 1.0 / 1.4

ORDER = [16, 4, 8, 9, 18, 5, 11, 14, 15, 3, 7, 10, 17, 6, 12, 13, 16, 0, 1, 2]
PLANE = {i: p for p, i in reversed(list(enumerate(ORDER)))}
CYM, CZP, CYP, CZM = (0, 5), (4, 9), (8, 13), (12, 17)
PLANES = len(ORDER)

MESH = pl.DeviceIdType.MESH
PAD = 8
BF = 16
BH = 64
HP = 16
BE = 24
BX = 72


def plane_of(e, part):
    return 3 * e + ("xzy" if e % 2 == 0 else "yxz").index(part)


def blocks(n):
    def over(body):
        if n == 1:
            body(0)
        else:
            pl.loop(0, n)(body)

    return over


def collide(f):
    rho = f[0]
    d = {}
    for i in range(1, 19, 2):
        rho = rho + (f[i] + f[i + 1])
        d[i] = f[i] - f[i + 1]
    mx = (d[1] + d[7]) + (d[9] + d[11]) + d[13]
    my = (d[3] + d[7]) + (d[15] - d[9]) + d[17]
    mz = (d[5] + d[11]) + (d[15] - d[13]) - d[17]
    inv = 1.0 / rho
    ux, uy, uz = mx * inv, my * inv, mz * inv
    even = rho - 1.5 * (mx * ux + my * uy + mz * uz)
    keep = 1.0 - OMEGA
    post = {0: keep * f[0] + (OMEGA / 3.0) * even}
    for i in range(1, 19, 2):
        w = OMEGA / (18.0 if i < 7 else 36.0)
        cx, cy, cz = DIRS[i]
        m = u = None
        for c, mm, uu in ((cx, mx, ux), (cy, my, uy), (cz, mz, uz)):
            if c == 0:
                continue
            if m is None:
                m, u = mm, uu
            elif c > 0:
                m, u = m + mm, u + uu
            else:
                m, u = m - mm, u - uu
        e = w * even + (4.5 * w) * (m * u)
        o = (3.0 * w) * m
        post[i] = keep * f[i] + (e + o)
        post[i + 1] = keep * f[i + 1] + (e - o)
    return post


def velocity(f):
    rho = f[0]
    d = {}
    for i in range(1, 19, 2):
        rho = rho + (f[i] + f[i + 1])
        d[i] = f[i] - f[i + 1]
    mx = (d[1] + d[7]) + (d[9] + d[11]) + d[13]
    my = (d[3] + d[7]) + (d[15] - d[9]) + d[17]
    mz = (d[5] + d[11]) + (d[15] - d[13]) - d[17]
    inv = 1.0 / rho
    return mx * inv, my * inv, mz * inv


def lane_shift(x, c):
    return pltpu.roll(x, c % x.shape[-1], 1) if c else x


def kernel(
    S, D, Z, ZC, X,
    f_hbm, lab_hbm, t0_hbm, obuf, tout_ref,
    fbuf, lraw, t0_ref, post, hdn, hup, lab, near, hlab, mask, rate, vel, t0x, ga, gin, gb, xs, xr, stage, tin, tout, tback,
    lsem, t0sem, fsem, bsem, lrsem, y_send, z_send, y_recv, z_recv,
    a_send, a_recv, t_send, t_recv, v_send, v_recv, w_send, w_recv, x_send, x_recv,
):
    N = Z // ZC
    NX = (Z + 16) // BX
    R = 2
    TILE = (Z // D) * R
    me_s, me_d = lax.axis_index("sec"), lax.axis_index("dev")

    def at(ds, dd):
        return (lax.rem(me_s + ds + S, S), lax.rem(me_d + dd + D, D))

    def other(k):
        return (me_s, lax.rem(me_d + k, D))

    def chunk_of(j):
        half = j // 2
        return jnp.where(j % 2 == 0, half, N - 1 - half)

    lab_copy = pltpu.make_async_copy(lab_hbm, lraw, lsem)
    lab_copy.start()
    t0_copy = pltpu.make_async_copy(t0_hbm, t0_ref, t0sem)
    t0_copy.start()

    def f_copy(j):
        rows = pl.ds(pl.multiple_of(chunk_of(j) * (ZC * R), ZC * R), ZC * R)
        return pltpu.make_async_copy(f_hbm.at[:, rows, :], fbuf.at[:, rows, :], fsem.at[j])

    @pl.loop(0, N)
    def _(j):
        f_copy(j).start()

    barrier = pltpu.get_barrier_semaphore()

    @pl.loop(1, D)
    def _(k):
        pl.semaphore_signal(barrier, inc=1, device_id=other(k), device_id_type=MESH)

    for ds in (-1, 1):
        for dd in (-1, 0, 1):
            pl.semaphore_signal(barrier, inc=1, device_id=at(ds, dd), device_id_type=MESH)

    t0_copy.wait()
    G = min(8, D)
    for z in range(Z // D):
        for y in range(R):
            for m in range(D // G):
                stage[pl.ds(TILE * G * m + R * z + y, G, stride=TILE), :] = t0_ref[
                    z, pl.ds(R * G * m + y, G, stride=R), :
                ]

    lab_copy.wait()
    for y in range(R):
        for b in range(Z // 8):
            lab[y, pl.ds(PAD + 8 * b, 8), :] = lraw[pl.ds(16 * b + y, 8, stride=R), :]
            near[y, pl.ds(PAD + 8 * b, 8), :] = lraw[pl.ds(16 * b + y, 8, stride=R), :]

    def remote(src, dst, send, recv, to):
        return pltpu.make_async_remote_copy(
            src_ref=src, dst_ref=dst, send_sem=send, recv_sem=recv, device_id=to, device_id_type=MESH
        )

    low, high = pl.ds(PAD, 8), pl.ds(Z, 8)
    under, over = pl.ds(0, 8), pl.ds(PAD + Z, 8)
    inner = pl.ds(PAD, Z)
    lab_copies = [
        remote(lab.at[1, inner], hlab.at[0, inner], bsem.at[0], lrsem.at[0], at(0, 1)),
        remote(lab.at[0, inner], hlab.at[1, inner], bsem.at[1], lrsem.at[1], at(0, -1)),
        remote(lab.at[:, high], lab.at[:, under], bsem.at[2], lrsem.at[2], at(1, 0)),
        remote(lab.at[:, low], lab.at[:, over], bsem.at[3], lrsem.at[3], at(-1, 0)),
        remote(lab.at[1, high], hlab.at[0, under], bsem.at[4], lrsem.at[4], at(1, 1)),
        remote(lab.at[1, low], hlab.at[0, over], bsem.at[5], lrsem.at[5], at(-1, 1)),
        remote(lab.at[0, low], hlab.at[1, over], bsem.at[6], lrsem.at[6], at(-1, -1)),
        remote(lab.at[0, high], hlab.at[1, under], bsem.at[7], lrsem.at[7], at(1, -1)),
    ]
    def y_copies(s, j):
        rows = pl.ds(pl.multiple_of(PAD + chunk_of(j) * ZC, 8), ZC)
        return (
            remote(post.at[s, 1, pl.ds(CYP[0], 5), rows], hdn.at[s, :, rows], y_send.at[s, 0, j], y_recv.at[s, 0, j], at(0, 1)),
            remote(post.at[s, 0, pl.ds(CYM[0], 5), rows], hup.at[s, :, rows], y_send.at[s, 1, j], y_recv.at[s, 1, j], at(0, -1)),
        )

    def z_copies(s):
        czp, czm = pl.ds(CZP[0], 5), pl.ds(CZM[0], 5)
        return (
            remote(post.at[s, :, czp, high], post.at[s, :, czp, under], z_send.at[s, 0], z_recv.at[s, 0], at(1, 0)),
            remote(post.at[s, :, czm, low], post.at[s, :, czm, over], z_send.at[s, 1], z_recv.at[s, 1], at(-1, 0)),
            remote(post.at[s, 1, PLANE[15], high], hdn.at[s, PLANE[15] - CYP[0], under], z_send.at[s, 2], z_recv.at[s, 2], at(1, 1)),
            remote(post.at[s, 1, PLANE[17], low], hdn.at[s, PLANE[17] - CYP[0], over], z_send.at[s, 3], z_recv.at[s, 3], at(-1, 1)),
            remote(post.at[s, 0, PLANE[16], low], hup.at[s, PLANE[16] - CYM[0], over], z_send.at[s, 4], z_recv.at[s, 4], at(-1, -1)),
            remote(post.at[s, 0, PLANE[18], high], hup.at[s, PLANE[18] - CYM[0], under], z_send.at[s, 5], z_recv.at[s, 5], at(1, -1)),
        )

    def store_post(s, y, rows, p):
        for plane, i in enumerate(ORDER):
            post[s, y, plane, rows, :] = p[i]

    def send_chunk(s, j):
        edges = z_copies(s)

        @pl.when(j == 0)
        def _():
            for q in (3, 4, 1):
                edges[q].start()

        @pl.when(j == 1)
        def _():
            for q in (2, 5, 0):
                edges[q].start()

        for c in y_copies(s, j):
            c.start()

    def source(s, y, i, z):
        cx, cy, cz = DIRS[i]
        rows = pl.ds(z - cz, BF)
        if y - cy < 0:
            v = hdn[s, PLANE[i] - CYP[0], rows, :]
        elif y - cy >= R:
            v = hup[s, PLANE[i] - CYM[0], rows, :]
        else:
            plane = 16 if i == 16 else PLANE[i]
            v = post[s, y - cy, plane, rows, :]
        return lane_shift(v, cx)

    def stream(s, y, z):
        here = pl.ds(z, BF)
        f = [post[s, y, PLANE[0], here, :]]
        for i in range(1, 19):
            open_ = mask[i - 1, y, pl.ds(z - PAD, BF), :] != 0
            f.append(jnp.where(open_, source(s, y, i, z), post[s, y, PLANE[OPP[i]], here, :]))
        return f

    def wait_sources(s, j):
        @pl.when(j == 0)
        def _():
            for q in (0, 1):
                for c in y_copies(s, q):
                    c.wait_recv()
            for c in z_copies(s):
                c.wait_recv()

        @pl.when(j + 2 < N)
        def _():
            for c in y_copies(s, j + 2):
                c.wait_recv()

    @pl.loop(0, N)
    def _(j):
        f_copy(j).wait()
        z0 = chunk_of(j) * ZC
        for y in range(R):
            @blocks(ZC // BF)
            def _(b):
                z = pl.multiple_of(z0 + BF * b, 8)
                f = [fbuf[i, pl.ds(2 * z + y, BF, stride=R), :] for i in range(19)]
                store_post(0, y, pl.ds(pl.multiple_of(z + PAD, 8), BF), collide(f))

    moving = range(1, 19)

    def set_masks(y, which, z, n, rows_of=lab):
        for cy, cz in sorted({DIRS[i][1:] for i in which}):
            rows = pl.ds(z + PAD - cz, n)
            if y - cy < 0:
                v = hlab[0, rows, :]
            elif y - cy >= R:
                v = hlab[1, rows, :]
            else:
                v = rows_of[y - cy, rows, :]
            for i in which:
                if DIRS[i][1:] == (cy, cz):
                    mask[i - 1, y, pl.ds(pl.multiple_of(z, 8), n), :] = lane_shift(v, DIRS[i][0])

    for y in range(R):
        @pl.loop(0, Z // BH)
        def _(b):
            set_masks(y, [i for i in moving if 0 <= y - DIRS[i][1] < R], BH * b, BH, near)

    pl.semaphore_wait(barrier, D - 1 + 6)

    for c in lab_copies:
        c.start()

    @pl.loop(0, N)
    def _(j):
        send_chunk(0, j)

    mine = pl.ds(pl.multiple_of(me_d * TILE, TILE), TILE)

    @pl.loop(1, D)
    def _(k):
        to = other(k)
        rows = pl.ds(pl.multiple_of(to[1] * TILE, TILE), TILE)
        remote(stage.at[rows], tin.at[mine], a_send.at[0], a_recv.at[0], to).start()

    tin[mine, :] = stage[mine, :]

    for c in lab_copies:
        c.wait_recv()
    for y in range(R):
        @pl.loop(0, Z // BH)
        def _(b):
            set_masks(y, [i for i in moving if not 0 <= y - DIRS[i][1] < R], BH * b, BH)
        for cz, z in ((1, 0), (-1, Z - 8)):
            set_masks(y, [i for i in moving if 0 <= y - DIRS[i][1] < R and DIRS[i][2] == cz], z, 8)

    hin, hlow, hhigh = pl.ds(HP, Z), pl.ds(HP, 8), pl.ds(HP + Z - 8, 8)
    hunder, hover = pl.ds(HP - 8, 8), pl.ds(HP + Z, 8)
    own, before, after = pl.ds(2, 2), pl.ds(0, 2), pl.ds(4, 2)
    t_copies = [
        remote(t0x.at[own, src], t0x.at[to, dst], t_send.at[q], t_recv.at[q], at(ds, dd))
        for q, (src, to, dst, ds, dd) in enumerate(
            (
                (hin, before, hin, 0, 1),
                (hin, after, hin, 0, -1),
                (hhigh, own, hunder, 1, 0),
                (hlow, own, hover, -1, 0),
                (hhigh, before, hunder, 1, 1),
                (hlow, before, hover, -1, 1),
                (hhigh, after, hunder, 1, -1),
                (hlow, after, hover, -1, -1),
            )
        )
    ]
    whole = pl.ds(0, Z * R - TILE)

    def spread_temperature():
        pltpu.make_async_copy(stage.at[whole], tin.at[whole], a_recv.at[0]).wait()
        for y in range(R):
            @pl.loop(0, Z // BH)
            def _(b):
                t0x[2 + y, pl.ds(pl.multiple_of(HP + BH * b, 8), BH), :] = tin[pl.ds(2 * BH * b + y, BH, stride=R), :]
        for c in t_copies:
            c.start()
        for e, labels in enumerate((hlab.at[0], lab.at[0], lab.at[1], hlab.at[1])):
            @pl.loop(0, NX)
            def _(b):
                pore = labels[pl.ds(pl.multiple_of(BX * b, 8), BX), :].astype(jnp.float32)
                rate[e, pl.ds(pl.multiple_of(BX * b + 8, 8), BX), :] = pore * RATE_PORE + (1.0 - pore) * RATE_GRAIN

    @pl.loop(1, FSTEPS)
    def _(s):
        @pl.loop(0, N)
        def _(j):
            wait_sources(s - 1, j)
            z0 = chunk_of(j) * ZC
            for y in range(R):
                @blocks(ZC // BF)
                def _(b):
                    z = pl.multiple_of(z0 + BF * b + PAD, 8)
                    store_post(s, y, pl.ds(z, BF), collide(stream(s - 1, y, z)))
            send_chunk(s, j)

        @pl.when(s == 1)
        def _():
            spread_temperature()

    upward, from_down = pl.ds(plane_of(2, "y"), 4), pl.ds(plane_of(0, "y"), 4)
    downward, from_up = pl.ds(plane_of(2, "x"), 4), pl.ds(plane_of(4, "x"), 4)
    both = pl.ds(plane_of(2, "x"), 6)

    def v_copies(j):
        rows = pl.ds(pl.multiple_of(HP + chunk_of(j) * ZC, 8), ZC)
        return (
            remote(vel.at[upward, rows], vel.at[from_down, rows], v_send.at[j, 0], v_recv.at[j, 0], at(0, 1)),
            remote(vel.at[downward, rows], vel.at[from_up, rows], v_send.at[j, 1], v_recv.at[j, 1], at(0, -1)),
        )

    w_copies = []
    for ds, src, dst in ((1, hhigh, hunder), (-1, hlow, hover)):
        for dd, fro, to in ((0, both, both), (1, upward, from_down), (-1, downward, from_up)):
            q = len(w_copies)
            w_copies.append(remote(vel.at[fro, src], vel.at[to, dst], w_send.at[q], w_recv.at[q], at(ds, dd)))

    def x_copies(b, part):
        rows = pl.ds(pl.multiple_of(8 + BX * b, 8), BX)
        planes = (pl.ds(0, 2), pl.ds(2, 1))[part]
        return [
            remote(
                xs.at[side, planes, rows], xr.at[side, planes, rows], x_send.at[side, b, part], x_recv.at[side, b, part], at(0, dd)
            )
            for side, dd in ((0, 1), (1, -1))
        ]

    def balance(temp, ux, uy, uz):
        a, b = 0.25 * temp, 0.125 * temp
        h = 0.5 * temp
        hx, hy, hz = h * ux, h * uy, h * uz
        return [a, b + hx, b - hx, b + hy, b - hy, b + hz, b - hz]

    def total(g):
        return ((g[0] + g[1]) + (g[2] + g[3])) + ((g[4] + g[5]) + g[6])

    def relax(g, q, r):
        return g + r * (q - g)

    def speed(e, here):
        return [vel[plane_of(e, part), here, :] for part in "xyz"]

    def gather(y, z, n):
        here = pl.ds(z, n)
        return [
            ga[0, y, here, :],
            lane_shift(ga[1, y, here, :], 1),
            lane_shift(ga[2, y, here, :], -1),
            gin[0, here, :] if y == 0 else ga[3, 0, here, :],
            gin[1, here, :] if y == 1 else ga[4, 1, here, :],
            ga[5, y, pl.ds(z - 1, n), :],
            ga[6, y, pl.ds(z + 1, n), :],
        ]

    def over_block(b):
        def run(body):
            @blocks(BX // BE)
            def _(k):
                body(pl.multiple_of(8 + BX * b + BE * k, 8))

        return run

    @pl.loop(0, N)
    def _(j):
        wait_sources(FSTEPS - 1, j)
        z0 = chunk_of(j) * ZC
        for y in range(R):
            @blocks(ZC // BF)
            def _(b):
                zr = pl.multiple_of(z0 + BF * b, 8)
                z = pl.multiple_of(zr + PAD, 8)
                f = stream(FSTEPS - 1, y, z)
                inter = pl.ds(2 * zr + y, BF, stride=R)
                for i in range(19):
                    obuf[i, inter, :] = f[i]
                pore = lab[y, pl.ds(z, BF), :].astype(jnp.float32)
                ux, uy, uz = velocity(f)
                there = pl.ds(pl.multiple_of(zr + HP, 8), BF)
                for part, u in (("x", ux), ("y", uy), ("z", uz)):
                    vel[plane_of(2 + y, part), there, :] = pore * u

        @pl.when(j == 1)
        def _():
            for c in w_copies:
                c.start()

        for c in v_copies(j):
            c.start()

    for c in t_copies:
        c.wait_recv()
    for c in w_copies:
        c.wait_recv()

    @pl.loop(0, N)
    def _(j):
        for c in v_copies(j):
            c.wait_recv()

    @pl.loop(0, NX)
    def _(b):
        @over_block(b)
        def _(z):
            here, dn, up = pl.ds(z, BE), pl.ds(z - 1, BE), pl.ds(z + 1, BE)
            for e in (1, 2, 3, 4):
                t = t0x[e, here, :]
                q = balance(t, *speed(e, here))
                prev, nxt = t0x[e - 1, here, :], t0x[e + 1, here, :]
                tdn, tup = t0x[e, dn, :], t0x[e, up, :]
                g = [
                    q[0],
                    lane_shift(q[1], 1),
                    lane_shift(q[2], -1),
                    0.125 * prev + 0.5 * prev * vel[plane_of(e - 1, "y"), here, :],
                    0.125 * nxt - 0.5 * nxt * vel[plane_of(e + 1, "y"), here, :],
                    0.125 * tdn + 0.5 * tdn * vel[plane_of(e, "z"), dn, :],
                    0.125 * tup - 0.5 * tup * vel[plane_of(e, "z"), up, :],
                ]
                q = balance(total(g), *speed(e, here))
                r = rate[e - 1, here, :]
                if e == 1:
                    gin[0, here, :] = relax(g[3], q[3], r)
                elif e == 4:
                    gin[1, here, :] = relax(g[4], q[4], r)
                else:
                    for k in range(7):
                        ga[k, e - 2, here, :] = relax(g[k], q[k], r)

    @pl.loop(0, NX)
    def _(b):
        @over_block(b)
        def _(z):
            here = pl.ds(z, BE)
            for y in range(R):
                g = gather(y, z, BE)
                q = balance(total(g), *speed(2 + y, here))
                r = rate[1 + y, here, :]
                p = [relax(g[k], q[k], r) for k in range(7)]
                for n, k in enumerate((0, 1, 2, 5, 6)):
                    gb[n, y, here, :] = p[k]
                xs[0, y, here, :] = p[3]
                xs[1, 1 - y, here, :] = p[4]

        for c in x_copies(b, 0):
            c.start()

    def others(y, z):
        here = pl.ds(z, BE)
        return [
            gb[0, y, here, :],
            lane_shift(gb[1, y, here, :], 1),
            lane_shift(gb[2, y, here, :], -1),
            gb[3, y, pl.ds(z - 1, BE), :],
            gb[4, y, pl.ds(z + 1, BE), :],
        ]

    @pl.loop(0, NX)
    def _(b):
        @over_block(b)
        def _(z):
            for y in range(R):
                a = others(y, z)
                xs[1 - y, 2, pl.ds(z, BE), :] = (a[0] + (a[1] + a[2])) + (a[3] + a[4])

        for c in x_copies(b, 1):
            c.start()

    @pl.loop(0, NX)
    def _(b):
        for c in x_copies(b, 0) + x_copies(b, 1):
            c.wait_recv()
        @over_block(b)
        def _(z):
            here = pl.ds(z, BE)
            for y in range(R):
                a = others(y, z)
                yp = xr[0, 1, here, :] if y == 0 else xs[0, 0, here, :]
                ym = xr[1, 1, here, :] if y == 1 else xs[1, 0, here, :]
                g = a[:3] + [yp, ym] + a[3:]
                q = balance(total(g), *speed(2 + y, here))
                r = rate[1 + y, here, :]
                for k in range(7):
                    ga[k, y, here, :] = relax(g[k], q[k], r)
            for side, e, sign in ((0, 1, 0.5), (1, 4, -0.5)):
                g = xr[side, 0, here, :]
                t = (xr[side, 2, here, :] + g) + xs[1 - side, 1, here, :]
                q = 0.125 * t + sign * t * vel[plane_of(e, "y"), here, :]
                gin[side, here, :] = relax(g, q, rate[e - 1, here, :])

    for y in range(R):
        @pl.loop(0, Z // BH)
        def _(b):
            zr = pl.multiple_of(BH * b, 8)
            tout[pl.ds(2 * zr + y, BH, stride=R), :] = total(gather(y, pl.multiple_of(zr + HP, 8), BH))

    @pl.loop(1, D)
    def _(k):
        to = other(k)
        rows = pl.ds(pl.multiple_of(to[1] * TILE, TILE), TILE)
        remote(tout.at[rows], tback.at[mine], a_send.at[1], a_recv.at[1], to).start()

    tback[mine, :] = tout[mine, :]

    for c in lab_copies:
        c.wait_send()

    @pl.loop(0, FSTEPS)
    def _(s):
        @pl.loop(0, N)
        def _(j):
            for c in y_copies(s, j):
                c.wait_send()
        for c in z_copies(s):
            c.wait_send()

    for c in t_copies + w_copies:
        c.wait_send()

    @pl.loop(0, N)
    def _(j):
        for c in v_copies(j):
            c.wait_send()

    @pl.loop(0, NX)
    def _(b):
        for c in x_copies(b, 0) + x_copies(b, 1):
            c.wait_send()

    pltpu.make_async_copy(stage.at[whole], tin.at[whole], a_send.at[0]).wait()
    pltpu.make_async_copy(tout.at[whole], tback.at[whole], a_send.at[1]).wait()
    pltpu.make_async_copy(tout.at[whole], tback.at[whole], a_recv.at[1]).wait()
    for z in range(Z // D):
        for y in range(R):
            for m in range(D // G):
                tout_ref[z, pl.ds(R * G * m + y, G, stride=R), :] = tback[
                    pl.ds(TILE * G * m + R * z + y, G, stride=TILE), :
                ]


def write_out(pops, temp, pops_out, temp_out, sem):
    copies = [
        pltpu.make_async_copy(pops, pops_out, sem.at[0]),
        pltpu.make_async_copy(temp, temp_out, sem.at[1]),
    ]
    for c in copies:
        c.start()
    for c in copies:
        c.wait()


def local(S, D, f, labels, t0, zc=16):
    _, Z, R, X = f.shape
    N = Z // zc
    Zp, Zh = Z + 2 * PAD, Z + 2 * HP
    NX = (Z + 16) // BX
    f32, i32 = jnp.float32, jnp.int32
    V, DMA = pltpu.VMEM, pltpu.SemaphoreType.DMA
    any_ = pl.BlockSpec(memory_space=pl.ANY)
    vmem = pl.BlockSpec(memory_space=pltpu.VMEM)
    pops, temp = pl.pallas_call(
        functools.partial(kernel, S, D, Z, zc, X),
        out_shape=(
            pltpu.VMEM((19, Z * R, X), f32),
            pltpu.VMEM(t0.shape, f32),
        ),
        in_specs=[any_, any_, any_],
        out_specs=(vmem, vmem),
        scratch_shapes=[
            V((19, Z * R, X), f32),
            V((Z * R, X), i32),
            V(t0.shape, f32),
            V((FSTEPS, R, PLANES, Zp, X), f32),
            V((FSTEPS, 5, Zp, X), f32),
            V((FSTEPS, 5, Zp, X), f32),
            V((R, Zp, X), i32),
            V((R, Zp, X), i32),
            V((2, Zp, X), i32),
            V((18, R, Z, X), i32),
            V((4, Zh, X), f32),
            V((18, Zh, X), f32),
            V((6, Zh, X), f32),
            V((7, R, Zh, X), f32),
            V((2, Zh, X), f32),
            V((5, R, Zh, X), f32),
            V((2, 3, Zh, X), f32),
            V((2, 3, Zh, X), f32),
            V((Z * R, X), f32),
            V((Z * R, X), f32),
            V((Z * R, X), f32),
            V((Z * R, X), f32),
            DMA(()),
            DMA(()),
            DMA((N,)),
            DMA((8,)),
            DMA((8,)),
            DMA((FSTEPS, 2, N)),
            DMA((FSTEPS, 6)),
            DMA((FSTEPS, 2, N)),
            DMA((FSTEPS, 6)),
            DMA((2,)),
            DMA((2,)),
            DMA((8,)),
            DMA((8,)),
            DMA((N, 2)),
            DMA((N, 2)),
            DMA((6,)),
            DMA((6,)),
            DMA((2, NX, 2)),
            DMA((2, NX, 2)),
        ],
        compiler_params=pltpu.CompilerParams(
            collective_id=0, has_side_effects=True, vmem_limit_bytes=56 * 1024 * 1024
        ),
    )(f.reshape(19, Z * R, X), labels.reshape(Z * R, X), t0)
    return pops.reshape(19, Z, R, X), temp


def solution(mesh):
    S, D = mesh.shape["sec"], mesh.shape["dev"]
    return jax.shard_map(
        functools.partial(local, S, D),
        mesh=mesh,
        in_specs=(
            P(None, "sec", "dev", None),
            P("sec", "dev", None),
            P(("sec", "dev"), None, None),
        ),
        out_specs=(P(None, "sec", "dev", None), P(("sec", "dev"), None, None)),
        check_vma=False,
    )
```

```python
import functools

import jax
import jax.numpy as jnp
from jax import lax
from jax.experimental import pallas as pl
from jax.experimental.pallas import tpu as pltpu
from jax.sharding import PartitionSpec as P

FSTEPS = 4

DIRS = [
    (0, 0, 0), (1, 0, 0), (-1, 0, 0), (0, 1, 0), (0, -1, 0), (0, 0, 1), (0, 0, -1),
    (1, 1, 0), (-1, -1, 0), (1, -1, 0), (-1, 1, 0), (1, 0, 1), (-1, 0, -1), (1, 0, -1), (-1, 0, 1),
    (0, 1, 1), (0, -1, -1), (0, 1, -1), (0, -1, 1),
]
OPP = [0, 2, 1, 4, 3, 6, 5, 8, 7, 10, 9, 12, 11, 14, 13, 16, 15, 18, 17]
OMEGA = 0.8
RATE_PORE = 1.0 / 0.7
RATE_GRAIN = 1.0 / 1.4

ORDER = [16, 4, 8, 9, 18, 5, 11, 14, 15, 3, 7, 10, 17, 6, 12, 13, 16, 0, 1, 2]
PLANE = {i: p for p, i in reversed(list(enumerate(ORDER)))}
CYM, CZP, CYP, CZM = (0, 5), (4, 9), (8, 13), (12, 17)
PLANES = len(ORDER)

MESH = pl.DeviceIdType.MESH
PAD = 8
BF = 16
BH = 64
HP = 16
BE = 24
BX = 48


def plane_of(e, part):
    return 3 * e + ("xzy" if e % 2 == 0 else "yxz").index(part)


def blocks(n):
    def over(body):
        if n == 1:
            body(0)
        else:
            pl.loop(0, n)(body)

    return over


def collide(f):
    rho = f[0]
    d = {}
    for i in range(1, 19, 2):
        rho = rho + (f[i] + f[i + 1])
        d[i] = f[i] - f[i + 1]
    mx = (d[1] + d[7]) + (d[9] + d[11]) + d[13]
    my = (d[3] + d[7]) + (d[15] - d[9]) + d[17]
    mz = (d[5] + d[11]) + (d[15] - d[13]) - d[17]
    inv = 1.0 / rho
    ux, uy, uz = mx * inv, my * inv, mz * inv
    even = rho - 1.5 * (mx * ux + my * uy + mz * uz)
    keep = 1.0 - OMEGA
    post = {0: keep * f[0] + (OMEGA / 3.0) * even}
    for i in range(1, 19, 2):
        w = OMEGA / (18.0 if i < 7 else 36.0)
        cx, cy, cz = DIRS[i]
        m = u = None
        for c, mm, uu in ((cx, mx, ux), (cy, my, uy), (cz, mz, uz)):
            if c == 0:
                continue
            if m is None:
                m, u = mm, uu
            elif c > 0:
                m, u = m + mm, u + uu
            else:
                m, u = m - mm, u - uu
        e = w * even + (4.5 * w) * (m * u)
        o = (3.0 * w) * m
        post[i] = keep * f[i] + (e + o)
        post[i + 1] = keep * f[i + 1] + (e - o)
    return post


def velocity(f):
    rho = f[0]
    d = {}
    for i in range(1, 19, 2):
        rho = rho + (f[i] + f[i + 1])
        d[i] = f[i] - f[i + 1]
    mx = (d[1] + d[7]) + (d[9] + d[11]) + d[13]
    my = (d[3] + d[7]) + (d[15] - d[9]) + d[17]
    mz = (d[5] + d[11]) + (d[15] - d[13]) - d[17]
    inv = 1.0 / rho
    return mx * inv, my * inv, mz * inv


def lane_shift(x, c):
    return pltpu.roll(x, c % x.shape[-1], 1) if c else x


def kernel(
    S, D, Z, ZC, X,
    f_hbm, lab_hbm, t0_hbm, obuf, tout_ref,
    fbuf, lraw, t0_ref, post, hdn, hup, lab, near, hlab, mask, rate, vel, t0x, ga, gin, gb, xs, xr, stage, tin, tout, tback,
    lsem, t0sem, fsem, bsem, lrsem, y_send, z_send, y_recv, z_recv,
    a_send, a_recv, t_send, t_recv, v_send, v_recv, w_send, w_recv, x_send, x_recv,
):
    N = Z // ZC
    NX = (Z + 16) // BX
    R = 2
    TILE = (Z // D) * R
    me_s, me_d = lax.axis_index("sec"), lax.axis_index("dev")

    def at(ds, dd):
        return (lax.rem(me_s + ds + S, S), lax.rem(me_d + dd + D, D))

    def other(k):
        return (me_s, lax.rem(me_d + k, D))

    def chunk_of(j):
        half = j // 2
        return jnp.where(j % 2 == 0, half, N - 1 - half)

    lab_copy = pltpu.make_async_copy(lab_hbm, lraw, lsem)
    lab_copy.start()
    t0_copy = pltpu.make_async_copy(t0_hbm, t0_ref, t0sem)
    t0_copy.start()

    def f_copy(j):
        rows = pl.ds(pl.multiple_of(chunk_of(j) * (ZC * R), ZC * R), ZC * R)
        return pltpu.make_async_copy(f_hbm.at[:, rows, :], fbuf.at[:, rows, :], fsem.at[j])

    @pl.loop(0, N)
    def _(j):
        f_copy(j).start()

    barrier = pltpu.get_barrier_semaphore()

    @pl.loop(1, D)
    def _(k):
        pl.semaphore_signal(barrier, inc=1, device_id=other(k), device_id_type=MESH)

    for ds in (-1, 1):
        for dd in (-1, 0, 1):
            pl.semaphore_signal(barrier, inc=1, device_id=at(ds, dd), device_id_type=MESH)

    t0_copy.wait()
    G = min(8, D)
    for z in range(Z // D):
        for y in range(R):
            for m in range(D // G):
                stage[pl.ds(TILE * G * m + R * z + y, G, stride=TILE), :] = t0_ref[
                    z, pl.ds(R * G * m + y, G, stride=R), :
                ]

    lab_copy.wait()
    for y in range(R):
        for b in range(Z // 8):
            lab[y, pl.ds(PAD + 8 * b, 8), :] = lraw[pl.ds(16 * b + y, 8, stride=R), :]
            near[y, pl.ds(PAD + 8 * b, 8), :] = lraw[pl.ds(16 * b + y, 8, stride=R), :]

    def remote(src, dst, send, recv, to):
        return pltpu.make_async_remote_copy(
            src_ref=src, dst_ref=dst, send_sem=send, recv_sem=recv, device_id=to, device_id_type=MESH
        )

    low, high = pl.ds(PAD, 8), pl.ds(Z, 8)
    under, over = pl.ds(0, 8), pl.ds(PAD + Z, 8)
    inner = pl.ds(PAD, Z)
    lab_copies = [
        remote(lab.at[1, inner], hlab.at[0, inner], bsem.at[0], lrsem.at[0], at(0, 1)),
        remote(lab.at[0, inner], hlab.at[1, inner], bsem.at[1], lrsem.at[1], at(0, -1)),
        remote(lab.at[:, high], lab.at[:, under], bsem.at[2], lrsem.at[2], at(1, 0)),
        remote(lab.at[:, low], lab.at[:, over], bsem.at[3], lrsem.at[3], at(-1, 0)),
        remote(lab.at[1, high], hlab.at[0, under], bsem.at[4], lrsem.at[4], at(1, 1)),
        remote(lab.at[1, low], hlab.at[0, over], bsem.at[5], lrsem.at[5], at(-1, 1)),
        remote(lab.at[0, low], hlab.at[1, over], bsem.at[6], lrsem.at[6], at(-1, -1)),
        remote(lab.at[0, high], hlab.at[1, under], bsem.at[7], lrsem.at[7], at(1, -1)),
    ]
    def y_copies(s, j):
        rows = pl.ds(pl.multiple_of(PAD + chunk_of(j) * ZC, 8), ZC)
        return (
            remote(post.at[s, 1, pl.ds(CYP[0], 5), rows], hdn.at[s, :, rows], y_send.at[s, 0, j], y_recv.at[s, 0, j], at(0, 1)),
            remote(post.at[s, 0, pl.ds(CYM[0], 5), rows], hup.at[s, :, rows], y_send.at[s, 1, j], y_recv.at[s, 1, j], at(0, -1)),
        )

    def z_copies(s):
        czp, czm = pl.ds(CZP[0], 5), pl.ds(CZM[0], 5)
        return (
            remote(post.at[s, :, czp, high], post.at[s, :, czp, under], z_send.at[s, 0], z_recv.at[s, 0], at(1, 0)),
            remote(post.at[s, :, czm, low], post.at[s, :, czm, over], z_send.at[s, 1], z_recv.at[s, 1], at(-1, 0)),
            remote(post.at[s, 1, PLANE[15], high], hdn.at[s, PLANE[15] - CYP[0], under], z_send.at[s, 2], z_recv.at[s, 2], at(1, 1)),
            remote(post.at[s, 1, PLANE[17], low], hdn.at[s, PLANE[17] - CYP[0], over], z_send.at[s, 3], z_recv.at[s, 3], at(-1, 1)),
            remote(post.at[s, 0, PLANE[16], low], hup.at[s, PLANE[16] - CYM[0], over], z_send.at[s, 4], z_recv.at[s, 4], at(-1, -1)),
            remote(post.at[s, 0, PLANE[18], high], hup.at[s, PLANE[18] - CYM[0], under], z_send.at[s, 5], z_recv.at[s, 5], at(1, -1)),
        )

    def store_post(s, y, rows, p):
        for plane, i in enumerate(ORDER):
            post[s, y, plane, rows, :] = p[i]

    def send_chunk(s, j):
        edges = z_copies(s)

        @pl.when(j == 0)
        def _():
            for q in (3, 4, 1):
                edges[q].start()

        @pl.when(j == 1)
        def _():
            for q in (2, 5, 0):
                edges[q].start()

        for c in y_copies(s, j):
            c.start()

    def source(s, y, i, z):
        cx, cy, cz = DIRS[i]
        rows = pl.ds(z - cz, BF)
        if y - cy < 0:
            v = hdn[s, PLANE[i] - CYP[0], rows, :]
        elif y - cy >= R:
            v = hup[s, PLANE[i] - CYM[0], rows, :]
        else:
            plane = 16 if i == 16 else PLANE[i]
            v = post[s, y - cy, plane, rows, :]
        return lane_shift(v, cx)

    def stream(s, y, z):
        here = pl.ds(z, BF)
        f = [post[s, y, PLANE[0], here, :]]
        for i in range(1, 19):
            open_ = mask[i - 1, y, pl.ds(z - PAD, BF), :] != 0
            f.append(jnp.where(open_, source(s, y, i, z), post[s, y, PLANE[OPP[i]], here, :]))
        return f

    def wait_sources(s, j):
        @pl.when(j == 0)
        def _():
            for q in (0, 1):
                for c in y_copies(s, q):
                    c.wait_recv()
            for c in z_copies(s):
                c.wait_recv()

        @pl.when(j + 2 < N)
        def _():
            for c in y_copies(s, j + 2):
                c.wait_recv()

    @pl.loop(0, N)
    def _(j):
        f_copy(j).wait()
        z0 = chunk_of(j) * ZC
        for y in range(R):
            @blocks(ZC // BF)
            def _(b):
                z = pl.multiple_of(z0 + BF * b, 8)
                f = [fbuf[i, pl.ds(2 * z + y, BF, stride=R), :] for i in range(19)]
                store_post(0, y, pl.ds(pl.multiple_of(z + PAD, 8), BF), collide(f))

    moving = range(1, 19)

    def set_masks(y, which, z, n, rows_of=lab):
        for cy, cz in sorted({DIRS[i][1:] for i in which}):
            rows = pl.ds(z + PAD - cz, n)
            if y - cy < 0:
                v = hlab[0, rows, :]
            elif y - cy >= R:
                v = hlab[1, rows, :]
            else:
                v = rows_of[y - cy, rows, :]
            for i in which:
                if DIRS[i][1:] == (cy, cz):
                    mask[i - 1, y, pl.ds(pl.multiple_of(z, 8), n), :] = lane_shift(v, DIRS[i][0])

    for y in range(R):
        @pl.loop(0, Z // BH)
        def _(b):
            set_masks(y, [i for i in moving if 0 <= y - DIRS[i][1] < R], BH * b, BH, near)

    pl.semaphore_wait(barrier, D - 1 + 6)

    for c in lab_copies:
        c.start()

    @pl.loop(0, N)
    def _(j):
        send_chunk(0, j)

    mine = pl.ds(pl.multiple_of(me_d * TILE, TILE), TILE)

    @pl.loop(1, D)
    def _(k):
        to = other(k)
        rows = pl.ds(pl.multiple_of(to[1] * TILE, TILE), TILE)
        remote(stage.at[rows], tin.at[mine], a_send.at[0], a_recv.at[0], to).start()

    tin[mine, :] = stage[mine, :]

    for c in lab_copies:
        c.wait_recv()
    for y in range(R):
        @pl.loop(0, Z // BH)
        def _(b):
            set_masks(y, [i for i in moving if not 0 <= y - DIRS[i][1] < R], BH * b, BH)
        for cz, z in ((1, 0), (-1, Z - 8)):
            set_masks(y, [i for i in moving if 0 <= y - DIRS[i][1] < R and DIRS[i][2] == cz], z, 8)

    hin, hlow, hhigh = pl.ds(HP, Z), pl.ds(HP, 8), pl.ds(HP + Z - 8, 8)
    hunder, hover = pl.ds(HP - 8, 8), pl.ds(HP + Z, 8)
    own, before, after = pl.ds(2, 2), pl.ds(0, 2), pl.ds(4, 2)
    t_copies = [
        remote(t0x.at[own, src], t0x.at[to, dst], t_send.at[q], t_recv.at[q], at(ds, dd))
        for q, (src, to, dst, ds, dd) in enumerate(
            (
                (hin, before, hin, 0, 1),
                (hin, after, hin, 0, -1),
                (hhigh, own, hunder, 1, 0),
                (hlow, own, hover, -1, 0),
                (hhigh, before, hunder, 1, 1),
                (hlow, before, hover, -1, 1),
                (hhigh, after, hunder, 1, -1),
                (hlow, after, hover, -1, -1),
            )
        )
    ]
    whole = pl.ds(0, Z * R - TILE)

    def spread_temperature():
        pltpu.make_async_copy(stage.at[whole], tin.at[whole], a_recv.at[0]).wait()
        for y in range(R):
            @pl.loop(0, Z // BH)
            def _(b):
                t0x[2 + y, pl.ds(pl.multiple_of(HP + BH * b, 8), BH), :] = tin[pl.ds(2 * BH * b + y, BH, stride=R), :]
        for c in t_copies:
            c.start()
        for e, labels in enumerate((hlab.at[0], lab.at[0], lab.at[1], hlab.at[1])):
            @pl.loop(0, NX)
            def _(b):
                pore = labels[pl.ds(pl.multiple_of(BX * b, 8), BX), :].astype(jnp.float32)
                rate[e, pl.ds(pl.multiple_of(BX * b + 8, 8), BX), :] = pore * RATE_PORE + (1.0 - pore) * RATE_GRAIN

    @pl.loop(1, FSTEPS)
    def _(s):
        @pl.loop(0, N)
        def _(j):
            wait_sources(s - 1, j)
            z0 = chunk_of(j) * ZC
            for y in range(R):
                @blocks(ZC // BF)
                def _(b):
                    z = pl.multiple_of(z0 + BF * b + PAD, 8)
                    store_post(s, y, pl.ds(z, BF), collide(stream(s - 1, y, z)))
            send_chunk(s, j)

        @pl.when(s == 1)
        def _():
            spread_temperature()

    upward, from_down = pl.ds(plane_of(2, "y"), 4), pl.ds(plane_of(0, "y"), 4)
    downward, from_up = pl.ds(plane_of(2, "x"), 4), pl.ds(plane_of(4, "x"), 4)
    both = pl.ds(plane_of(2, "x"), 6)

    def v_copies(j):
        rows = pl.ds(pl.multiple_of(HP + chunk_of(j) * ZC, 8), ZC)
        return (
            remote(vel.at[upward, rows], vel.at[from_down, rows], v_send.at[j, 0], v_recv.at[j, 0], at(0, 1)),
            remote(vel.at[downward, rows], vel.at[from_up, rows], v_send.at[j, 1], v_recv.at[j, 1], at(0, -1)),
        )

    w_copies = []
    for ds, src, dst in ((1, hhigh, hunder), (-1, hlow, hover)):
        for dd, fro, to in ((0, both, both), (1, upward, from_down), (-1, downward, from_up)):
            q = len(w_copies)
            w_copies.append(remote(vel.at[fro, src], vel.at[to, dst], w_send.at[q], w_recv.at[q], at(ds, dd)))

    def x_copies(b, part):
        rows = pl.ds(pl.multiple_of(8 + BX * b, 8), BX)
        planes = (pl.ds(0, 2), pl.ds(2, 1))[part]
        return [
            remote(
                xs.at[side, planes, rows], xr.at[side, planes, rows], x_send.at[side, b, part], x_recv.at[side, b, part], at(0, dd)
            )
            for side, dd in ((0, 1), (1, -1))
        ]

    def balance(temp, ux, uy, uz):
        a, b = 0.25 * temp, 0.125 * temp
        h = 0.5 * temp
        hx, hy, hz = h * ux, h * uy, h * uz
        return [a, b + hx, b - hx, b + hy, b - hy, b + hz, b - hz]

    def total(g):
        return ((g[0] + g[1]) + (g[2] + g[3])) + ((g[4] + g[5]) + g[6])

    def relax(g, q, r):
        return g + r * (q - g)

    def speed(e, here):
        return [vel[plane_of(e, part), here, :] for part in "xyz"]

    def gather(y, z, n):
        here = pl.ds(z, n)
        return [
            ga[0, y, here, :],
            lane_shift(ga[1, y, here, :], 1),
            lane_shift(ga[2, y, here, :], -1),
            gin[0, here, :] if y == 0 else ga[3, 0, here, :],
            gin[1, here, :] if y == 1 else ga[4, 1, here, :],
            ga[5, y, pl.ds(z - 1, n), :],
            ga[6, y, pl.ds(z + 1, n), :],
        ]

    def over_block(b):
        def run(body):
            @blocks(BX // BE)
            def _(k):
                body(pl.multiple_of(8 + BX * b + BE * k, 8))

        return run

    @pl.loop(0, N)
    def _(j):
        wait_sources(FSTEPS - 1, j)
        z0 = chunk_of(j) * ZC
        for y in range(R):
            @blocks(ZC // BF)
            def _(b):
                zr = pl.multiple_of(z0 + BF * b, 8)
                z = pl.multiple_of(zr + PAD, 8)
                f = stream(FSTEPS - 1, y, z)
                inter = pl.ds(2 * zr + y, BF, stride=R)
                for i in range(19):
                    obuf[i, inter, :] = f[i]
                pore = lab[y, pl.ds(z, BF), :].astype(jnp.float32)
                ux, uy, uz = velocity(f)
                there = pl.ds(pl.multiple_of(zr + HP, 8), BF)
                for part, u in (("x", ux), ("y", uy), ("z", uz)):
                    vel[plane_of(2 + y, part), there, :] = pore * u

        @pl.when(j == 1)
        def _():
            for c in w_copies:
                c.start()

        for c in v_copies(j):
            c.start()

    for c in t_copies:
        c.wait_recv()
    for c in w_copies:
        c.wait_recv()

    @pl.loop(0, N)
    def _(j):
        for c in v_copies(j):
            c.wait_recv()

    @pl.loop(0, NX)
    def _(b):
        @over_block(b)
        def _(z):
            here, dn, up = pl.ds(z, BE), pl.ds(z - 1, BE), pl.ds(z + 1, BE)
            for e in (1, 2, 3, 4):
                t = t0x[e, here, :]
                q = balance(t, *speed(e, here))
                prev, nxt = t0x[e - 1, here, :], t0x[e + 1, here, :]
                tdn, tup = t0x[e, dn, :], t0x[e, up, :]
                g = [
                    q[0],
                    lane_shift(q[1], 1),
                    lane_shift(q[2], -1),
                    0.125 * prev + 0.5 * prev * vel[plane_of(e - 1, "y"), here, :],
                    0.125 * nxt - 0.5 * nxt * vel[plane_of(e + 1, "y"), here, :],
                    0.125 * tdn + 0.5 * tdn * vel[plane_of(e, "z"), dn, :],
                    0.125 * tup - 0.5 * tup * vel[plane_of(e, "z"), up, :],
                ]
                q = balance(total(g), *speed(e, here))
                r = rate[e - 1, here, :]
                if e == 1:
                    gin[0, here, :] = relax(g[3], q[3], r)
                elif e == 4:
                    gin[1, here, :] = relax(g[4], q[4], r)
                else:
                    for k in range(7):
                        ga[k, e - 2, here, :] = relax(g[k], q[k], r)

    @pl.loop(0, NX)
    def _(b):
        @over_block(b)
        def _(z):
            here = pl.ds(z, BE)
            for y in range(R):
                g = gather(y, z, BE)
                q = balance(total(g), *speed(2 + y, here))
                r = rate[1 + y, here, :]
                p = [relax(g[k], q[k], r) for k in range(7)]
                for n, k in enumerate((0, 1, 2, 5, 6)):
                    gb[n, y, here, :] = p[k]
                xs[0, y, here, :] = p[3]
                xs[1, 1 - y, here, :] = p[4]

        for c in x_copies(b, 0):
            c.start()

    def others(y, z):
        here = pl.ds(z, BE)
        return [
            gb[0, y, here, :],
            lane_shift(gb[1, y, here, :], 1),
            lane_shift(gb[2, y, here, :], -1),
            gb[3, y, pl.ds(z - 1, BE), :],
            gb[4, y, pl.ds(z + 1, BE), :],
        ]

    @pl.loop(0, NX)
    def _(b):
        @over_block(b)
        def _(z):
            for y in range(R):
                a = others(y, z)
                xs[1 - y, 2, pl.ds(z, BE), :] = (a[0] + (a[1] + a[2])) + (a[3] + a[4])

        for c in x_copies(b, 1):
            c.start()

    @pl.loop(0, NX)
    def _(b):
        for c in x_copies(b, 0) + x_copies(b, 1):
            c.wait_recv()
        @over_block(b)
        def _(z):
            here = pl.ds(z, BE)
            for y in range(R):
                a = others(y, z)
                yp = xr[0, 1, here, :] if y == 0 else xs[0, 0, here, :]
                ym = xr[1, 1, here, :] if y == 1 else xs[1, 0, here, :]
                g = a[:3] + [yp, ym] + a[3:]
                q = balance(total(g), *speed(2 + y, here))
                r = rate[1 + y, here, :]
                for k in range(7):
                    ga[k, y, here, :] = relax(g[k], q[k], r)
            for side, e, sign in ((0, 1, 0.5), (1, 4, -0.5)):
                g = xr[side, 0, here, :]
                t = (xr[side, 2, here, :] + g) + xs[1 - side, 1, here, :]
                q = 0.125 * t + sign * t * vel[plane_of(e, "y"), here, :]
                gin[side, here, :] = relax(g, q, rate[e - 1, here, :])

    for y in range(R):
        @pl.loop(0, Z // BH)
        def _(b):
            zr = pl.multiple_of(BH * b, 8)
            tout[pl.ds(2 * zr + y, BH, stride=R), :] = total(gather(y, pl.multiple_of(zr + HP, 8), BH))

    @pl.loop(1, D)
    def _(k):
        to = other(k)
        rows = pl.ds(pl.multiple_of(to[1] * TILE, TILE), TILE)
        remote(tout.at[rows], tback.at[mine], a_send.at[1], a_recv.at[1], to).start()

    tback[mine, :] = tout[mine, :]

    for c in lab_copies:
        c.wait_send()

    @pl.loop(0, FSTEPS)
    def _(s):
        @pl.loop(0, N)
        def _(j):
            for c in y_copies(s, j):
                c.wait_send()
        for c in z_copies(s):
            c.wait_send()

    for c in t_copies + w_copies:
        c.wait_send()

    @pl.loop(0, N)
    def _(j):
        for c in v_copies(j):
            c.wait_send()

    @pl.loop(0, NX)
    def _(b):
        for c in x_copies(b, 0) + x_copies(b, 1):
            c.wait_send()

    pltpu.make_async_copy(stage.at[whole], tin.at[whole], a_send.at[0]).wait()
    pltpu.make_async_copy(tout.at[whole], tback.at[whole], a_send.at[1]).wait()
    pltpu.make_async_copy(tout.at[whole], tback.at[whole], a_recv.at[1]).wait()
    for z in range(Z // D):
        for y in range(R):
            for m in range(D // G):
                tout_ref[z, pl.ds(R * G * m + y, G, stride=R), :] = tback[
                    pl.ds(TILE * G * m + R * z + y, G, stride=TILE), :
                ]


def write_out(pops, temp, pops_out, temp_out, sem):
    copies = [
        pltpu.make_async_copy(pops, pops_out, sem.at[0]),
        pltpu.make_async_copy(temp, temp_out, sem.at[1]),
    ]
    for c in copies:
        c.start()
    for c in copies:
        c.wait()


def local(S, D, f, labels, t0, zc=16):
    _, Z, R, X = f.shape
    N = Z // zc
    Zp, Zh = Z + 2 * PAD, Z + 2 * HP
    NX = (Z + 16) // BX
    f32, i32 = jnp.float32, jnp.int32
    V, DMA = pltpu.VMEM, pltpu.SemaphoreType.DMA
    any_ = pl.BlockSpec(memory_space=pl.ANY)
    vmem = pl.BlockSpec(memory_space=pltpu.VMEM)
    pops, temp = pl.pallas_call(
        functools.partial(kernel, S, D, Z, zc, X),
        out_shape=(
            pltpu.VMEM((19, Z * R, X), f32),
            pltpu.VMEM(t0.shape, f32),
        ),
        in_specs=[any_, any_, any_],
        out_specs=(vmem, vmem),
        scratch_shapes=[
            V((19, Z * R, X), f32),
            V((Z * R, X), i32),
            V(t0.shape, f32),
            V((FSTEPS, R, PLANES, Zp, X), f32),
            V((FSTEPS, 5, Zp, X), f32),
            V((FSTEPS, 5, Zp, X), f32),
            V((R, Zp, X), i32),
            V((R, Zp, X), i32),
            V((2, Zp, X), i32),
            V((18, R, Z, X), i32),
            V((4, Zh, X), f32),
            V((18, Zh, X), f32),
            V((6, Zh, X), f32),
            V((7, R, Zh, X), f32),
            V((2, Zh, X), f32),
            V((5, R, Zh, X), f32),
            V((2, 3, Zh, X), f32),
            V((2, 3, Zh, X), f32),
            V((Z * R, X), f32),
            V((Z * R, X), f32),
            V((Z * R, X), f32),
            V((Z * R, X), f32),
            DMA(()),
            DMA(()),
            DMA((N,)),
            DMA((8,)),
            DMA((8,)),
            DMA((FSTEPS, 2, N)),
            DMA((FSTEPS, 6)),
            DMA((FSTEPS, 2, N)),
            DMA((FSTEPS, 6)),
            DMA((2,)),
            DMA((2,)),
            DMA((8,)),
            DMA((8,)),
            DMA((N, 2)),
            DMA((N, 2)),
            DMA((6,)),
            DMA((6,)),
            DMA((2, NX, 2)),
            DMA((2, NX, 2)),
        ],
        compiler_params=pltpu.CompilerParams(
            collective_id=0, has_side_effects=True, vmem_limit_bytes=56 * 1024 * 1024
        ),
    )(f.reshape(19, Z * R, X), labels.reshape(Z * R, X), t0)
    return pops.reshape(19, Z, R, X), temp


def solution(mesh):
    S, D = mesh.shape["sec"], mesh.shape["dev"]
    return jax.shard_map(
        functools.partial(local, S, D),
        mesh=mesh,
        in_specs=(
            P(None, "sec", "dev", None),
            P("sec", "dev", None),
            P(("sec", "dev"), None, None),
        ),
        out_specs=(P(None, "sec", "dev", None), P(("sec", "dev"), None, None)),
        check_vma=False,
    )
```
